32 devices in a mesh: section: 4 (over y, x), expert: 8 (over z, core).
Axes of the slice: x: 2, y: 2, z: 4, core: 2. Of those that a mesh axis runs over, the one named last changes fastest.
Arguments:
- tokens: bfloat16 [4, 128, 4096], P('section', 'expert'), may hold values from -6 to 6
- norm_gain: float32 [4, 4096], P('section'), may hold values from 0.1 to 1.9
- first_routes: int32 [4, 128, 1], P('section', 'expert'), may hold values from 0 to 3; in each aligned block of 16 rows (0 to 15, 16 to 31, ..., all dimensions but the last counted through in order) at most 5 rows name the same one
- first_gates: float32 [4, 128, 1], P('section', 'expert'), may hold values from 0.25 to 2
- second_routes: int32 [4, 128, 1], P('section', 'expert'), may hold values from 0 to 3; in each aligned block of 16 rows (0 to 15, 16 to 31, ..., all dimensions but the last counted through in order) at most 5 rows name the same one
- second_gates: float32 [4, 128, 1], P('section', 'expert'), may hold values from 0.25 to 2
- gate_proj: bfloat16 [4, 8, 4096, 512], P('section', 'expert'), may hold values from -0.09375 to 0.09375
- up_proj: bfloat16 [4, 8, 4096, 512], P('section', 'expert'), may hold values from -0.09375 to 0.09375
- down_proj: bfloat16 [4, 8, 512, 4096], P('section', 'expert'), may hold values from -0.1875 to 0.1875
Outputs:
- mixed: bfloat16 [4, 128, 4096], P('section', 'expert')
The draws below stay inside these ranges and needn't reach their ends.
Inputs may be any that keep to these rules, and one draw needn't show every extreme that they name: `first_routes`: within the 16 rows of one device, no expert id appears more than 5 times, and in some devices one id appears exactly 5 times. `second_routes`: within the 16 rows of one device, no expert id appears more than 5 times, and in some devices one id appears exactly 5 times.
All inputs are finite; a program needn't handle non-finite values.
Results may differ from the reference program's by a relative error of at most 0.0078.
Values may be sent and summed in bfloat16 or wider, within the bound.
No kernel may reach another device: no remote copies, remote signals or barrier semaphores. Data moves between devices by JAX's collectives and lax.ppermute only.
A program may use at most 64 MiB of HBM per device.

```python
import math
import jax
import jax.numpy as jnp
import numpy as np
from jax import lax

D = 4096
FF = 1024
EXPERTS = 4
TOP = 1
MB_DEV = 16
CAP = 5
HID_DEV = 512
TOKENS_MB = 128
N_SECTION = 4
N_EXPERT = 8


def level_of(stream_key, extent, shards, smallest, top_value):
    loudness, own = 1.0, jax.random.fold_in(stream_key, 6)
    for axis_at, blocks in shards:
        draws = jnp.exp(jax.random.uniform(jax.random.fold_in(own, axis_at), (blocks,), jnp.float32, smallest / len(shards), top_value / len(shards)))
        loudness = loudness * jnp.repeat(draws, extent[axis_at] // blocks).reshape([-1 if axis == axis_at else 1 for axis in range(len(extent))])
    return loudness


def shared_out(own_key, own, number, rows, amount, top, most, lean):
    sequence = jax.random.permutation(own_key, amount)
    crowded, common = shares(amount, rows * top, most, lean, True), shares(amount, rows * top, most, lean, False)
    places = jnp.arange(amount)

    def named(sizes, rotation):
        used = int((sizes > 0).sum())
        fixed = max(1, used // 4)
        passed = fixed + (places - fixed + rotation * (used - fixed)) % max(1, amount - fixed)
        return jnp.zeros((amount,), jnp.int32).at[sequence[jnp.where(places < fixed, places, passed)]].set(jnp.asarray(sizes, jnp.int32))

    sizes = jnp.where(number % 4 == 0, named(crowded, number // 4), named(common, number - number // 4 - 1))
    mixed = jax.random.permutation(jax.random.fold_in(own, 3), amount)
    source_of, sink = mixed[0:amount // 2 * 2:2], mixed[1:amount // 2 * 2:2]
    slack = jnp.minimum(sizes[source_of] - 1, most - sizes[sink]) // 2
    slack = jnp.where((source_of == sequence[0]) | (sink == sequence[0]) | (sizes[sink] == 0), 0, jnp.maximum(slack, 0))
    passed = jax.random.randint(jax.random.fold_in(own, 4), (amount // 2,), 0, 1 << 20) % (slack + 1)
    sizes = sizes.at[source_of].add(-passed).at[sink].add(passed)
    members = jnp.searchsorted(jnp.cumsum(sizes), jnp.arange(rows * top), side="right").astype(jnp.int32)
    table = members.reshape(top, rows).T
    table = table[jax.random.permutation(jax.random.fold_in(own, 1), rows)]
    rotation = jax.random.randint(jax.random.fold_in(own, 2), (rows, 1), 0, top)
    return jnp.take_along_axis(table, (jnp.arange(top)[None, :] + rotation) % top, axis=1)


def shares(count, total, limit, lean, full):
    portions = [(1 << 20) // math.isqrt(rank ** lean) + 1 for rank in range(1, count + 1)]
    largest = limit if full else min(limit, max(-(-total // count), total * portions[0] // sum(portions)))
    least = 1 if total - largest >= count - 1 else 0
    given, surplus = [largest] + [least] * (count - 1), total - largest - least * (count - 1)
    while surplus > 0:
        free = [i for i in range(1, count) if given[i] < largest] or [i for i in range(1, count) if given[i] < limit]
        pool, remaining = sum([portions[i] for i in free]), surplus
        for i in free:
            extra = min(limit - given[i], max(1, remaining * portions[i] // pool), surplus)
            given[i] = given[i] + extra
            surplus = surplus - extra
    return np.array(given)


def bell_draw(own_key, shape, scale, reach, split=(), held_as=jnp.bfloat16):
    loudness = level_of(own_key, shape, split, -0.22, 0.18) if split else 1.0
    array = jax.random.normal(own_key, shape, jnp.float32) * scale * loudness
    return jnp.minimum(jnp.maximum(array, -reach), reach).astype(held_as)


def setup_inputs(seed: int = 0) -> dict:
    splits = jax.random.split(jax.random.key(seed), 10)
    tokens = bell_draw(splits[0], (N_SECTION, TOKENS_MB, D), 1.0, 6.0, ((0, 4), (1, 8)))
    norm_gain = jnp.clip(1.0 + 0.18 * jax.random.normal(splits[1], (N_SECTION, D), jnp.float32), 0.1, 1.9)
    first_routes_keys = jax.random.split(jax.random.fold_in(splits[2], 1), N_SECTION * TOKENS_MB // MB_DEV)
    first_routes_turns = jax.random.permutation(jax.random.fold_in(splits[2], 3), N_SECTION * TOKENS_MB // MB_DEV)
    first_routes = jax.vmap(lambda own, number: shared_out(jax.random.fold_in(splits[2], 2), own, number, MB_DEV, EXPERTS, TOP, CAP, 2))(first_routes_keys, first_routes_turns).reshape((N_SECTION, TOKENS_MB, TOP))
    first_gates = jnp.clip(jnp.exp(math.log(2.0) - 2.0794415 * jax.random.uniform(splits[3], (N_SECTION, TOKENS_MB, TOP), jnp.float32) ** level_of(splits[3], (N_SECTION, TOKENS_MB, TOP), ((0, 4), (1, 8)), -0.2, 0.2)), 0.25, 2.0)
    second_routes_keys = jax.random.split(jax.random.fold_in(splits[4], 1), N_SECTION * TOKENS_MB // MB_DEV)
    second_routes_turns = jax.random.permutation(jax.random.fold_in(splits[4], 3), N_SECTION * TOKENS_MB // MB_DEV)
    second_routes = jax.vmap(lambda own, number: shared_out(jax.random.fold_in(splits[4], 2), own, number, MB_DEV, EXPERTS, TOP, CAP, 2))(second_routes_keys, second_routes_turns).reshape((N_SECTION, TOKENS_MB, TOP))
    second_gates = jnp.clip(jnp.exp(math.log(2.0) - 2.0794415 * jax.random.uniform(splits[5], (N_SECTION, TOKENS_MB, TOP), jnp.float32) ** level_of(splits[5], (N_SECTION, TOKENS_MB, TOP), ((0, 4), (1, 8)), -0.2, 0.2)), 0.25, 2.0)
    gate_proj = bell_draw(splits[6], (N_SECTION, N_EXPERT, D, HID_DEV), D ** -0.5, 0.09375, ((0, 4), (1, 8)))
    up_proj = bell_draw(splits[7], (N_SECTION, N_EXPERT, D, HID_DEV), D ** -0.5, 0.09375, ((0, 4), (1, 8)))
    down_proj = bell_draw(splits[8], (N_SECTION, N_EXPERT, HID_DEV, D), FF ** -0.5, 0.1875, ((0, 4), (1, 8)))
    return {"tokens": tokens, "norm_gain": norm_gain, "first_routes": first_routes, "first_gates": first_gates, "second_routes": second_routes, "second_gates": second_gates, "gate_proj": gate_proj, "up_proj": up_proj, "down_proj": down_proj}


EPS = 1e-06

def normalize(activations, norm_scale):
    values = activations.astype(jnp.float32)
    inv_scale = lax.rsqrt(lax.optimization_barrier(jnp.mean(values * values, axis=-1, keepdims=True)) + EPS)
    return (values * inv_scale * norm_scale.astype(jnp.float32)[None, :]).astype(jnp.bfloat16)

def section_layer(section_args):
    activations, norm_scale, routes, gate_weight, w_gate, w_up, w_down = section_args
    group_size = N_EXPERT // EXPERTS
    row_count = activations.shape[0]
    slot_total = N_EXPERT * CAP
    normed = normalize(activations, norm_scale)
    padded = jnp.concatenate([normed, jnp.zeros((1, D), jnp.bfloat16)], axis=0)
    chosen = routes[:, 0]
    row_order = jnp.arange(row_count, dtype=jnp.int32)
    combined = jnp.zeros((row_count, D), jnp.float32)
    for expert in range(EXPERTS):
        chosen_mask = (chosen == expert).astype(jnp.int32)
        slot_place = jnp.cumsum(chosen_mask) - 1
        target = jnp.where(chosen_mask > 0, slot_place, slot_total).astype(jnp.int32)
        slot_rows = jnp.full((slot_total,), row_count, jnp.int32).at[target].set(row_order, mode='drop')
        picked = padded[slot_rows]
        summed = jnp.zeros((slot_total, D), jnp.float32)
        for slice_index in range(group_size):
            weight_row = expert * group_size + slice_index
            gate_val = jnp.dot(picked, w_gate[weight_row], preferred_element_type=jnp.float32)
            up_val = jnp.dot(picked, w_up[weight_row], preferred_element_type=jnp.float32)
            hidden = (jax.nn.silu(gate_val) * up_val).astype(jnp.bfloat16)
            partial_value = jnp.dot(hidden, w_down[weight_row], preferred_element_type=jnp.float32).astype(jnp.bfloat16)
            summed = summed + lax.optimization_barrier(partial_value).astype(jnp.float32)
        combined = combined.at[slot_rows].add(summed, mode='drop')
    update = (gate_weight[:, 0:1] * combined).astype(jnp.bfloat16)
    update = lax.optimization_barrier(update)
    return (activations.astype(jnp.float32) + update.astype(jnp.float32)).astype(jnp.bfloat16)

def reference(tokens, norm_gain, first_routes, first_gates, second_routes, second_gates, gate_proj, up_proj, down_proj):
    first_pass = lax.map(section_layer, (tokens, norm_gain, first_routes, first_gates, gate_proj, up_proj, down_proj))
    carried = jnp.roll(first_pass, 1, axis=0)
    return lax.map(section_layer, (carried, norm_gain, second_routes, second_gates, gate_proj, up_proj, down_proj))
```

```python
import jax
import jax.numpy as jnp
from jax import lax
from jax.sharding import PartitionSpec as P

EXPERTS = 4
EPS = 1e-06


def normalize(activations, norm_scale):
    values = activations.astype(jnp.float32)
    inv_scale = lax.rsqrt(jnp.mean(values * values, axis=-1, keepdims=True) + EPS)
    return (values * inv_scale * norm_scale[None, :]).astype(jnp.bfloat16)


def layer(rows, norm_scale, routes, gates, w_gate, w_up, w_down):
    width = rows.shape[1]
    group = lax.axis_size("expert") // EXPERTS
    mine = lax.axis_index("expert") // group
    normed = normalize(rows, norm_scale)
    ids = jnp.broadcast_to(routes.astype(jnp.bfloat16), (rows.shape[0], 128))
    everyone = lax.all_gather(
        jnp.concatenate([normed, ids], axis=1), "expert", axis=0, tiled=True
    )
    here = everyone[:, width : width + 1] == mine.astype(jnp.bfloat16)
    values = everyone[:, :width]
    gate_val = jnp.dot(values, w_gate, preferred_element_type=jnp.float32)
    up_val = jnp.dot(values, w_up, preferred_element_type=jnp.float32)
    hidden = jnp.where(here, jax.nn.silu(gate_val) * up_val, 0.0).astype(jnp.bfloat16)
    partial_value = jnp.dot(hidden, w_down, preferred_element_type=jnp.float32)
    summed = lax.psum_scatter(
        partial_value.astype(jnp.bfloat16), "expert", scatter_dimension=0, tiled=True
    )
    update = (gates * summed.astype(jnp.float32)).astype(jnp.bfloat16)
    return (rows.astype(jnp.float32) + update.astype(jnp.float32)).astype(jnp.bfloat16)


def on_device(tokens, gain, routes_1, gates_1, routes_2, gates_2, gate_proj, up_proj, down_proj):
    sections = lax.axis_size("section")
    weights = (gate_proj[0, 0], up_proj[0, 0], down_proj[0, 0])
    first = layer(tokens[0], gain[0], routes_1[0], gates_1[0], *weights)
    carried = lax.ppermute(first, "section", [(i, (i + 1) % sections) for i in range(sections)])
    return layer(carried, gain[0], routes_2[0], gates_2[0], *weights)[None]


def solution(mesh):
    rows = P("section", "expert", None)
    slabs = P("section", "expert", None, None)
    return jax.shard_map(
        on_device,
        mesh=mesh,
        in_specs=(rows, P("section", None), rows, rows, rows, rows, slabs, slabs, slabs),
        out_specs=rows,
        check_vma=False,
    )
```

```python
import functools

import jax
import jax.numpy as jnp
from jax import lax
from jax.experimental import pallas as pl
from jax.experimental.pallas import tpu as pltpu
from jax.sharding import PartitionSpec as P

EXPERTS = 4
CAP = 5
ROWS = 16
CHUNKS = 3
EPS = 1e-06
F32 = jnp.float32
BF16 = jnp.bfloat16
VMEM = pl.BlockSpec(memory_space=pltpu.VMEM)


def fifth(value):
    return (value * 205) >> 10


def chunk_width(width):
    return -(-width // (CHUNKS * 128)) * 128


def chunk_span(width, chunk):
    start = chunk * chunk_width(width)
    return start, min(width, start + chunk_width(width)) - start


def upright(row):
    rows = row.shape[1]
    same = lax.broadcasted_iota(jnp.int32, (rows, rows), 0) == lax.broadcasted_iota(
        jnp.int32, (rows, rows), 1
    )
    return jnp.sum(jnp.where(same, row, 0.0), axis=1, keepdims=True)


def slots_of(routes):
    rows = routes.shape[0]
    lanes = lax.broadcasted_iota(jnp.int32, (rows, 128), 1).astype(F32)
    one_hot = (routes == lanes).astype(F32)
    earlier = lax.broadcasted_iota(jnp.int32, (rows, rows), 0) > lax.broadcasted_iota(
        jnp.int32, (rows, rows), 1
    )
    before = jnp.dot(earlier.astype(BF16), one_hot.astype(BF16), preferred_element_type=F32)
    return routes * CAP + jnp.sum(before * one_hot, axis=1, keepdims=True)


def block_map(slots, expert, chunk):
    spot = lax.broadcasted_iota(jnp.int32, (slots.shape[0], EXPERTS * ROWS), 1)
    inner = (spot & (ROWS - 1)) - CAP * chunk
    target = ((spot >> 4) ^ expert) * CAP + inner
    target = jnp.where((inner >= 0) & (inner < CAP), target, -1)
    return (slots == target.astype(F32)).astype(BF16)


def normalize(values, gain):
    inv_scale = lax.rsqrt(jnp.mean(values * values, axis=-1, keepdims=True) + EPS)
    return (values * inv_scale * gain).astype(BF16)


def write_blocks(normed, slots, expert, block_refs):
    width = normed.shape[1]
    pieces = []
    for chunk in range(CHUNKS):
        start, span = chunk_span(width, chunk)
        piece = lax.dot_general(
            block_map(slots, expert, chunk),
            normed[:, start : start + span],
            (((0,), (0,)), ((), ())),
            preferred_element_type=F32,
        )
        if span < chunk_width(width):
            piece = jnp.concatenate(
                [piece, jnp.zeros((piece.shape[0], chunk_width(width) - span), F32)], axis=1
            )
        pieces.append(piece)
    packed = sum(pieces[1:], pieces[0]).astype(BF16)
    for k, ref in enumerate(block_refs):
        ref[...] = packed[k * ROWS : (k + 1) * ROWS]


def my_expert(group):
    return lax.axis_index("expert") // group


def pack_kernel(group, x_ref, gain_ref, routes_ref, gates_ref, meta_ref, *block_refs):
    slots = slots_of(upright(routes_ref[...].astype(F32)))
    gates = upright(gates_ref[...])
    lane = lax.broadcasted_iota(jnp.int32, meta_ref.shape, 1)
    meta_ref[...] = jnp.where(lane == 0, slots, jnp.where(lane == 1, gates, 0.0))
    normed = normalize(x_ref[...].astype(F32), gain_ref[...])
    write_blocks(normed, slots, my_expert(group), block_refs)


def residual(x, slots, gates, expert, blocks):
    width = x.shape[1]
    found = []
    for chunk in range(CHUNKS):
        _, span = chunk_span(width, chunk)
        found.append(
            jnp.dot(
                block_map(slots, expert, chunk), blocks[:, :span], preferred_element_type=F32
            )
        )
    update = (gates * jnp.concatenate(found, axis=1)).astype(BF16)
    return x.astype(F32) + update.astype(F32)


def middle_kernel(group, x_ref, meta_ref, b0, b1, b2, b3, gain_ref, routes_ref, first_ref, *block_refs):
    blocks = jnp.concatenate([b0[...], b1[...], b2[...], b3[...]], axis=0)
    expert = my_expert(group)
    first = residual(x_ref[...], meta_ref[:, 0:1], meta_ref[:, 1:2], expert, blocks).astype(BF16)
    first_ref[...] = first
    slots = slots_of(upright(routes_ref[...].astype(F32)))
    normed = normalize(first.astype(F32), gain_ref[...])
    write_blocks(normed, slots, expert, block_refs)


def last_kernel(group, x_ref, b0, b1, b2, b3, routes_ref, gates_ref, out_ref):
    blocks = jnp.concatenate([b0[...], b1[...], b2[...], b3[...]], axis=0)
    slots = slots_of(upright(routes_ref[...].astype(F32)))
    gates = upright(gates_ref[...])
    out_ref[...] = residual(x_ref[...], slots, gates, my_expert(group), blocks).astype(BF16)


def compact_map(shape, compact_dim, chunk):
    compact = lax.broadcasted_iota(jnp.int32, shape, compact_dim)
    spot = lax.broadcasted_iota(jnp.int32, shape, 1 - compact_dim)
    block = fifth(compact)
    wanted = block * ROWS + CAP * chunk + compact - CAP * block
    return (wanted == spot).astype(BF16)


def expert_kernel(count, w_gate, w_up, w_down, *refs):
    ins, outs, (x_ref, part_ref) = refs[:count], refs[count:-2], refs[-2:]
    width, units = w_gate.shape
    rows = x_ref.shape[0]
    blocks = jnp.concatenate([ref[...] for ref in ins], axis=0)
    for chunk in range(CHUNKS):
        start, span = chunk_span(width, chunk)
        x_ref[:, start : start + span] = jnp.dot(
            compact_map((rows, count * ROWS), 0, chunk),
            blocks[:, :span],
            preferred_element_type=F32,
        ).astype(BF16)
    x = x_ref[...]
    gate_val = jnp.dot(x, w_gate[...], preferred_element_type=F32)
    up_val = jnp.dot(x, w_up[...], preferred_element_type=F32)
    hidden = (gate_val / (1.0 + jnp.exp(-gate_val)) * up_val).astype(BF16)
    part_ref[...] = jnp.dot(hidden, w_down[...], preferred_element_type=F32).astype(BF16)
    total = None
    for chunk in range(CHUNKS):
        start, span = chunk_span(width, chunk)
        piece = jnp.dot(
            compact_map((count * ROWS, rows), 1, chunk),
            part_ref[:, start : start + span],
            preferred_element_type=F32,
        )
        if span < chunk_width(width):
            piece = jnp.concatenate(
                [piece, jnp.zeros((piece.shape[0], chunk_width(width) - span), F32)], axis=1
            )
        total = piece if total is None else total + piece
    total = total.astype(BF16)
    for m, ref in enumerate(outs):
        ref[...] = total[m * EXPERTS * ROWS : (m + 1) * EXPERTS * ROWS]


def sum_kernel(*refs):
    ins, outs = refs[:-EXPERTS], refs[-EXPERTS:]
    total = ins[0][...].astype(F32)
    for ref in ins[1:]:
        total = total + ref[...].astype(F32)
    total = total.astype(BF16)
    for k, ref in enumerate(outs):
        ref[...] = total[k * ROWS : (k + 1) * ROWS]


def call(body, outs, ins, megabytes, scratch=(), flops=0):
    moved = sum(a.size * a.dtype.itemsize for a in (*ins, *outs))
    return pl.pallas_call(
        body,
        out_shape=outs,
        in_specs=[VMEM] * len(ins),
        out_specs=[VMEM] * len(outs),
        scratch_shapes=list(scratch),
        compiler_params=pltpu.CompilerParams(vmem_limit_bytes=megabytes << 20),
        cost_estimate=pl.CostEstimate(flops=flops, bytes_accessed=moved, transcendentals=0),
    )(*ins)


def on_device(tokens, gain, routes_1, gates_1, routes_2, gates_2, gate_proj, up_proj, down_proj):
    sections, devices = lax.axis_size("section"), lax.axis_size("expert")
    group = devices // EXPERTS
    rows, width = tokens.shape[1:]
    weights = (gate_proj[0, 0], up_proj[0, 0], down_proj[0, 0])
    wide = chunk_width(width)
    block = jax.ShapeDtypeStruct((ROWS, wide), BF16)
    stack = jax.ShapeDtypeStruct((EXPERTS * ROWS, wide), BF16)
    whole = jax.ShapeDtypeStruct((rows, width), BF16)
    meta = jax.ShapeDtypeStruct((rows, 128), F32)
    routes_1, gates_1, routes_2, gates_2 = (
        a.reshape(1, rows) for a in (routes_1, gates_1, routes_2, gates_2)
    )

    def to_expert(k):
        return [(i, (i // group ^ k) * group + i % group) for i in range(devices)]

    def within(shift):
        return [(i, i // group * group + (i + shift) % group) for i in range(devices)]

    def onward(k):
        return [
            (s * devices + i, (s + 1) % sections * devices + j)
            for s in range(sections)
            for i, j in to_expert(k)
        ]

    def experts(blocks):
        arrived = [None] * EXPERTS
        for k in (3, 2, 1):
            arrived[k] = lax.ppermute(blocks[k], "expert", to_expert(k))
        arrived[0] = blocks[0]
        ins = list(arrived)
        for m in range(1, group):
            ins += [lax.ppermute(a, "expert", within(m)) for a in arrived]
        count = EXPERTS * group
        held = -(-count * CAP // ROWS) * ROWS
        sums = call(
            functools.partial(expert_kernel, count),
            [stack] * group,
            [*weights, *ins],
            24,
            [pltpu.VMEM((held, width), BF16), pltpu.VMEM((held, width), BF16)],
            flops=6 * held * width * weights[0].shape[1],
        )
        terms = [sums[0]] + [lax.ppermute(sums[m], "expert", within(-m)) for m in range(1, group)]
        return call(sum_kernel, [block] * EXPERTS, terms, 8)

    slots, *blocks = call(
        functools.partial(pack_kernel, group),
        [meta] + [block] * EXPERTS,
        [tokens[0], gain, routes_1, gates_1],
        8,
    )
    ahead = [(i, (i + 1) % sections) for i in range(sections)]
    slots = lax.ppermute(slots, "section", ahead)
    before = lax.ppermute(tokens[0], "section", ahead)
    sums = experts(blocks)
    home = [lax.ppermute(sums[k], ("section", "expert"), onward(k)) for k in range(EXPERTS)]
    first, *blocks = call(
        functools.partial(middle_kernel, group),
        [whole] + [block] * EXPERTS,
        [before, slots, *home, gain, routes_2],
        8,
    )
    sums = experts(blocks)
    home = [sums[0]] + [lax.ppermute(sums[k], "expert", to_expert(k)) for k in (1, 2, 3)]
    (mixed,) = call(
        functools.partial(last_kernel, group), [whole], [first, *home, routes_2, gates_2], 8
    )
    return mixed[None]


def solution(mesh):
    rows = P("section", "expert", None)
    slabs = P("section", "expert", None, None)
    return jax.shard_map(
        on_device,
        mesh=mesh,
        in_specs=(rows, P("section", None), rows, rows, rows, rows, slabs, slabs, slabs),
        out_specs=rows,
        check_vma=False,
    )
```

```python
import functools

import jax
import jax.numpy as jnp
from jax import lax
from jax.experimental import pallas as pl
from jax.experimental.pallas import tpu as pltpu
from jax.sharding import PartitionSpec as P

EXPERTS = 4
CAP = 5
ROWS = 16
CHUNKS = 3
EPS = 1e-06
F32 = jnp.float32
BF16 = jnp.bfloat16
VMEM = pl.BlockSpec(memory_space=pltpu.VMEM)
HBM = pl.BlockSpec(memory_space=pltpu.HBM)


def distance(place):
    return EXPERTS - 1 - place


def fifth(value):
    return (value * 205) >> 10


def chunk_width(width):
    return -(-width // (CHUNKS * 128)) * 128


def chunk_span(width, chunk):
    start = chunk * chunk_width(width)
    return start, min(width, start + chunk_width(width)) - start


def upright(row):
    rows = row.shape[1]
    same = lax.broadcasted_iota(jnp.int32, (rows, rows), 0) == lax.broadcasted_iota(
        jnp.int32, (rows, rows), 1
    )
    return jnp.sum(jnp.where(same, row, 0.0), axis=1, keepdims=True)


def slots_of(routes):
    rows = routes.shape[0]
    lanes = lax.broadcasted_iota(jnp.int32, (rows, 128), 1).astype(F32)
    one_hot = (routes == lanes).astype(F32)
    earlier = lax.broadcasted_iota(jnp.int32, (rows, rows), 0) > lax.broadcasted_iota(
        jnp.int32, (rows, rows), 1
    )
    before = jnp.dot(earlier.astype(BF16), one_hot.astype(BF16), preferred_element_type=F32)
    return routes * CAP + jnp.sum(before * one_hot, axis=1, keepdims=True)


def block_map(slots, expert, chunk):
    spot = lax.broadcasted_iota(jnp.int32, (slots.shape[0], EXPERTS * ROWS), 1)
    inner = (spot & (ROWS - 1)) - CAP * chunk
    target = (distance(spot >> 4) ^ expert) * CAP + inner
    target = jnp.where((inner >= 0) & (inner < CAP), target, -1)
    return (slots == target.astype(F32)).astype(BF16)


def normalize(values, gain):
    inv_scale = lax.rsqrt(jnp.mean(values * values, axis=-1, keepdims=True) + EPS)
    return (values * inv_scale * gain).astype(BF16)


def write_blocks(normed, slots, expert, block_refs):
    width = normed.shape[1]
    pieces = []
    for chunk in range(CHUNKS):
        start, span = chunk_span(width, chunk)
        piece = lax.dot_general(
            block_map(slots, expert, chunk),
            normed[:, start : start + span],
            (((0,), (0,)), ((), ())),
            preferred_element_type=F32,
        )
        if span < chunk_width(width):
            piece = jnp.concatenate(
                [piece, jnp.zeros((piece.shape[0], chunk_width(width) - span), F32)], axis=1
            )
        pieces.append(piece)
    packed = sum(pieces[1:], pieces[0]).astype(BF16)
    for k, ref in enumerate(block_refs):
        ref[...] = packed[k * ROWS : (k + 1) * ROWS]


def my_expert(group):
    return lax.axis_index("expert") // group


def split_parts(values):
    parts = []
    for _ in range(3):
        parts.append(values.astype(BF16))
        values = values - parts[-1].astype(F32)
    return parts


def pack_kernel(group, *refs):
    sources, block_refs, ahead_ref = refs[:4], refs[4 : 4 + EXPERTS], refs[4 + EXPERTS]
    held, sems = refs[5 + EXPERTS : -1], refs[-1]
    copies = [
        pltpu.make_async_copy(source, place, sems.at[i])
        for i, (source, place) in enumerate(zip(sources, held))
    ]
    for copy in copies:
        copy.start()
    for copy in copies:
        copy.wait()
    x_ref, gain_ref, routes_ref, gates_ref = held
    rows, width = x_ref.shape
    slots = slots_of(upright(routes_ref[...].astype(F32)))
    lane = lax.broadcasted_iota(jnp.int32, (rows, 128), 1)
    meta = jnp.zeros((rows, 128), F32)
    for i, column in enumerate([slots, *split_parts(upright(gates_ref[...]))]):
        meta = jnp.where(lane == i, column.astype(F32), meta)
    ahead_ref[:, :width] = x_ref[...]
    ahead_ref[:, width:] = meta.astype(BF16)
    normed = normalize(x_ref[...].astype(F32), gain_ref[...])
    write_blocks(normed, slots, my_expert(group), block_refs)


def residual(x, slots, gates, expert, blocks):
    width = x.shape[1]
    found = []
    for chunk in range(CHUNKS):
        _, span = chunk_span(width, chunk)
        found.append(
            jnp.dot(
                block_map(slots, expert, chunk), blocks[:, :span], preferred_element_type=F32
            )
        )
    update = (gates * jnp.concatenate(found, axis=1)).astype(BF16)
    return x.astype(F32) + update.astype(F32)


def middle_kernel(group, b0, b1, b2, b3, ahead_ref, gain_ref, routes_ref, first_ref, *block_refs):
    blocks = jnp.concatenate([b0[...], b1[...], b2[...], b3[...]], axis=0)
    expert = my_expert(group)
    width = first_ref.shape[1]
    meta = ahead_ref[:, width:].astype(F32)
    gates = meta[:, 1:2] + meta[:, 2:3] + meta[:, 3:4]
    first = residual(ahead_ref[:, :width], meta[:, 0:1], gates, expert, blocks).astype(BF16)
    first_ref[...] = first
    slots = slots_of(upright(routes_ref[...].astype(F32)))
    normed = normalize(first.astype(F32), gain_ref[...])
    write_blocks(normed, slots, expert, block_refs)


def last_kernel(group, x_ref, b0, b1, b2, b3, routes_ref, gates_ref, out_ref):
    blocks = jnp.concatenate([b0[...], b1[...], b2[...], b3[...]], axis=0)
    slots = slots_of(upright(routes_ref[...].astype(F32)))
    gates = upright(gates_ref[...])
    out_ref[...] = residual(x_ref[...], slots, gates, my_expert(group), blocks).astype(BF16)


def compact_map(shape, compact_dim, chunk):
    compact = lax.broadcasted_iota(jnp.int32, shape, compact_dim)
    spot = lax.broadcasted_iota(jnp.int32, shape, 1 - compact_dim)
    block = fifth(compact)
    wanted = block * ROWS + CAP * chunk + compact - CAP * block
    return (wanted == spot).astype(BF16)


def expert_kernel(count, w_gate, w_up, w_down, *refs):
    ins, outs, (x_ref, part_ref) = refs[:count], refs[count:-2], refs[-2:]
    width, units = w_gate.shape
    rows = x_ref.shape[0]
    blocks = jnp.concatenate([ref[...] for ref in ins], axis=0)
    for chunk in range(CHUNKS):
        start, span = chunk_span(width, chunk)
        x_ref[:, start : start + span] = jnp.dot(
            compact_map((rows, count * ROWS), 0, chunk),
            blocks[:, :span],
            preferred_element_type=F32,
        ).astype(BF16)
    x = x_ref[...]
    gate_val = jnp.dot(x, w_gate[...], preferred_element_type=F32)
    up_val = jnp.dot(x, w_up[...], preferred_element_type=F32)
    hidden = (gate_val / (1.0 + jnp.exp(-gate_val)) * up_val).astype(BF16)
    part_ref[...] = jnp.dot(hidden, w_down[...], preferred_element_type=F32).astype(BF16)
    total = None
    for chunk in range(CHUNKS):
        start, span = chunk_span(width, chunk)
        piece = jnp.dot(
            compact_map((count * ROWS, rows), 1, chunk),
            part_ref[:, start : start + span],
            preferred_element_type=F32,
        )
        if span < chunk_width(width):
            piece = jnp.concatenate(
                [piece, jnp.zeros((piece.shape[0], chunk_width(width) - span), F32)], axis=1
            )
        total = piece if total is None else total + piece
    total = total.astype(BF16)
    for m, ref in enumerate(outs):
        ref[...] = total[m * EXPERTS * ROWS : (m + 1) * EXPERTS * ROWS]


def sum_kernel(*refs):
    ins, outs = refs[:-EXPERTS], refs[-EXPERTS:]
    total = ins[0][...].astype(F32)
    for ref in ins[1:]:
        total = total + ref[...].astype(F32)
    total = total.astype(BF16)
    for k, ref in enumerate(outs):
        ref[...] = total[k * ROWS : (k + 1) * ROWS]


def call(body, outs, ins, megabytes, scratch=(), flops=0, space=VMEM):
    moved = sum(a.size * a.dtype.itemsize for a in (*ins, *outs))
    return pl.pallas_call(
        body,
        out_shape=outs,
        in_specs=[space] * len(ins),
        out_specs=[VMEM] * len(outs),
        scratch_shapes=list(scratch),
        compiler_params=pltpu.CompilerParams(vmem_limit_bytes=megabytes << 20),
        cost_estimate=pl.CostEstimate(flops=flops, bytes_accessed=moved, transcendentals=0),
    )(*ins)


def on_device(tokens, gain, routes_1, gates_1, routes_2, gates_2, gate_proj, up_proj, down_proj):
    sections, devices = lax.axis_size("section"), lax.axis_size("expert")
    group = devices // EXPERTS
    rows, width = tokens.shape[1:]
    weights = (gate_proj[0, 0], up_proj[0, 0], down_proj[0, 0])
    wide = chunk_width(width)
    block = jax.ShapeDtypeStruct((ROWS, wide), BF16)
    stack = jax.ShapeDtypeStruct((EXPERTS * ROWS, wide), BF16)
    whole = jax.ShapeDtypeStruct((rows, width), BF16)
    ahead = jax.ShapeDtypeStruct((rows, width + 128), BF16)
    routes_1, gates_1, routes_2, gates_2 = (
        a.reshape(1, rows) for a in (routes_1, gates_1, routes_2, gates_2)
    )

    def to_expert(place):
        far = distance(place)
        return [(i, (i // group ^ far) * group + i % group) for i in range(devices)]

    def within(shift):
        return [(i, i // group * group + (i + shift) % group) for i in range(devices)]

    def onward(place):
        return [
            (s * devices + i, (s + 1) % sections * devices + j)
            for s in range(sections)
            for i, j in to_expert(place)
        ]

    def across(blocks):
        arrived = [lax.ppermute(blocks[i], "expert", to_expert(i)) for i in range(EXPERTS - 1)]
        return arrived + [blocks[EXPERTS - 1]]

    def shared(arrived):
        ins = list(arrived)
        for m in range(1, group):
            ins += [lax.ppermute(a, "expert", within(m)) for a in arrived]
        return ins

    def experts(ins):
        count = EXPERTS * group
        held = -(-count * CAP // ROWS) * ROWS
        sums = call(
            functools.partial(expert_kernel, count),
            [stack] * group,
            [*weights, *ins],
            24,
            [pltpu.VMEM((held, width), BF16), pltpu.VMEM((held, width), BF16)],
            flops=6 * held * width * weights[0].shape[1],
        )
        terms = [sums[0]] + [lax.ppermute(sums[m], "expert", within(-m)) for m in range(1, group)]
        return call(sum_kernel, [block] * EXPERTS, terms, 8)

    sources = [
        pltpu.with_memory_space_constraint(a, pltpu.HBM)
        for a in (tokens[0], gain, routes_1, gates_1)
    ]
    *blocks, travelling = call(
        functools.partial(pack_kernel, group),
        [block] * EXPERTS + [ahead],
        sources,
        8,
        [pltpu.VMEM(a.shape, a.dtype) for a in sources]
        + [pltpu.SemaphoreType.DMA((len(sources),))],
        flops=10**10,
        space=HBM,
    )
    arrived = across(blocks)
    arrived[0], travelling = lax.optimization_barrier((arrived[0], travelling))
    ins = shared(arrived)
    before = lax.ppermute(travelling, "section", [(i, (i + 1) % sections) for i in range(sections)])
    *ins, before = lax.optimization_barrier((*ins, before))
    sums = experts(ins)
    home = [lax.ppermute(sums[i], ("section", "expert"), onward(i)) for i in range(EXPERTS)]
    first, *blocks = call(
        functools.partial(middle_kernel, group),
        [whole] + [block] * EXPERTS,
        [*home, before, gain, routes_2],
        8,
    )
    sums = experts(shared(across(blocks)))
    home = [lax.ppermute(sums[i], "expert", to_expert(i)) for i in range(EXPERTS - 1)]
    (mixed,) = call(
        functools.partial(last_kernel, group),
        [whole],
        [first, *home, sums[EXPERTS - 1], routes_2, gates_2],
        8,
    )
    return mixed[None]


def solution(mesh):
    rows = P("section", "expert", None)
    slabs = P("section", "expert", None, None)
    return jax.shard_map(
        on_device,
        mesh=mesh,
        in_specs=(rows, P("section", None), rows, rows, rows, rows, slabs, slabs, slabs),
        out_specs=rows,
        check_vma=False,
    )
```

```python
import functools

import jax
import jax.numpy as jnp
from jax import lax
from jax.experimental import pallas as pl
from jax.experimental.pallas import tpu as pltpu
from jax.sharding import PartitionSpec as P

EXPERTS = 4
CAP = 5
ROWS = 16
CHUNKS = 3
EPS = 1e-06
F32 = jnp.float32
BF16 = jnp.bfloat16
VMEM = pl.BlockSpec(memory_space=pltpu.VMEM)
HBM = pl.BlockSpec(memory_space=pltpu.HBM)


def distance(place):
    return EXPERTS - 1 - place


def fifth(value):
    return (value * 205) >> 10


def chunk_width(width):
    return -(-width // (CHUNKS * 128)) * 128


def chunk_span(width, chunk):
    start = chunk * chunk_width(width)
    return start, min(width, start + chunk_width(width)) - start


def upright(row):
    rows = row.shape[1]
    same = lax.broadcasted_iota(jnp.int32, (rows, rows), 0) == lax.broadcasted_iota(
        jnp.int32, (rows, rows), 1
    )
    return jnp.sum(jnp.where(same, row, 0.0), axis=1, keepdims=True)


def slots_of(routes):
    rows = routes.shape[0]
    lanes = lax.broadcasted_iota(jnp.int32, (rows, 128), 1).astype(F32)
    one_hot = (routes == lanes).astype(F32)
    earlier = lax.broadcasted_iota(jnp.int32, (rows, rows), 0) > lax.broadcasted_iota(
        jnp.int32, (rows, rows), 1
    )
    before = jnp.dot(earlier.astype(BF16), one_hot.astype(BF16), preferred_element_type=F32)
    return routes * CAP + jnp.sum(before * one_hot, axis=1, keepdims=True)


def block_map(slots, expert, chunk):
    spot = lax.broadcasted_iota(jnp.int32, (slots.shape[0], EXPERTS * ROWS), 1)
    inner = (spot & (ROWS - 1)) - CAP * chunk
    holder = spot >> 4
    if expert is not None:
        holder = distance(holder) ^ expert
    target = holder * CAP + inner
    target = jnp.where((inner >= 0) & (inner < CAP), target, -1)
    return (slots == target.astype(F32)).astype(BF16)


def normalize(values, gain):
    inv_scale = lax.rsqrt(jnp.mean(values * values, axis=-1, keepdims=True) + EPS)
    return (values * inv_scale * gain).astype(BF16)


def write_blocks(normed, slots, expert, block_refs):
    width = normed.shape[1]
    pieces = []
    for chunk in range(CHUNKS):
        start, span = chunk_span(width, chunk)
        piece = lax.dot_general(
            block_map(slots, expert, chunk),
            normed[:, start : start + span],
            (((0,), (0,)), ((), ())),
            preferred_element_type=F32,
        )
        if span < chunk_width(width):
            piece = jnp.concatenate(
                [piece, jnp.zeros((piece.shape[0], chunk_width(width) - span), F32)], axis=1
            )
        pieces.append(piece)
    packed = sum(pieces[1:], pieces[0]).astype(BF16)
    hand_out(packed, block_refs)


def hand_out(values, refs):
    start = 0
    for ref in refs:
        ref[...] = values[start : start + ref.shape[0]]
        start += ref.shape[0]


def my_expert(group):
    return lax.axis_index("expert") // group


def split_parts(values):
    parts = []
    for _ in range(3):
        parts.append(values.astype(BF16))
        values = values - parts[-1].astype(F32)
    return parts


def pack_kernel(group, *refs):
    sources, block_refs, ahead_ref = refs[:4], refs[4 : 4 + EXPERTS], refs[4 + EXPERTS]
    held, sems = refs[5 + EXPERTS : -1], refs[-1]
    copies = [
        pltpu.make_async_copy(source, place, sems.at[i])
        for i, (source, place) in enumerate(zip(sources, held))
    ]
    for copy in copies:
        copy.start()
    for copy in copies:
        copy.wait()
    x_ref, gain_ref, routes_ref, gates_ref = held
    rows, width = x_ref.shape
    slots = slots_of(upright(routes_ref[...].astype(F32)))
    lane = lax.broadcasted_iota(jnp.int32, (rows, 128), 1)
    meta = jnp.zeros((rows, 128), F32)
    for i, column in enumerate([slots, *split_parts(upright(gates_ref[...]))]):
        meta = jnp.where(lane == i, column.astype(F32), meta)
    ahead_ref[:, :width] = x_ref[...]
    ahead_ref[:, width:] = meta.astype(BF16)
    normed = normalize(x_ref[...].astype(F32), gain_ref[...])
    write_blocks(normed, slots, my_expert(group), block_refs)


def residual(x, slots, gates, expert, blocks):
    width = x.shape[1]
    found = []
    for chunk in range(CHUNKS):
        _, span = chunk_span(width, chunk)
        found.append(
            jnp.dot(
                block_map(slots, expert, chunk), blocks[:, :span], preferred_element_type=F32
            )
        )
    update = (gates * jnp.concatenate(found, axis=1)).astype(BF16)
    return x.astype(F32) + update.astype(F32)


def middle_kernel(group, b0, b1, b2, b3, ahead_ref, gain_ref, routes_ref, first_ref, *block_refs):
    blocks = jnp.concatenate([b0[...], b1[...], b2[...], b3[...]], axis=0)
    expert = my_expert(group)
    width = first_ref.shape[1]
    meta = ahead_ref[:, width:].astype(F32)
    gates = meta[:, 1:2] + meta[:, 2:3] + meta[:, 3:4]
    first = residual(ahead_ref[:, :width], meta[:, 0:1], gates, expert, blocks).astype(BF16)
    first_ref[...] = first
    slots = slots_of(upright(routes_ref[...].astype(F32)))
    normed = normalize(first.astype(F32), gain_ref[...])
    write_blocks(normed, slots, None, block_refs)


def last_kernel(x_ref, blocks_ref, routes_ref, gates_ref, out_ref):
    blocks = blocks_ref[...]
    slots = slots_of(upright(routes_ref[...].astype(F32)))
    gates = upright(gates_ref[...])
    out_ref[...] = residual(x_ref[...], slots, gates, None, blocks).astype(BF16)


def compact_map(shape, compact_dim, chunk):
    compact = lax.broadcasted_iota(jnp.int32, shape, compact_dim)
    spot = lax.broadcasted_iota(jnp.int32, shape, 1 - compact_dim)
    block = fifth(compact)
    wanted = block * ROWS + CAP * chunk + compact - CAP * block
    return (wanted == spot).astype(BF16)


def expert_kernel(given, w_gate, w_up, w_down, *refs):
    ins, outs, (x_ref, part_ref) = refs[:given], refs[given:-2], refs[-2:]
    count = sum(ref.shape[0] for ref in ins) // ROWS
    width, units = w_gate.shape
    rows = x_ref.shape[0]
    blocks = jnp.concatenate([ref[...] for ref in ins], axis=0)
    for chunk in range(CHUNKS):
        start, span = chunk_span(width, chunk)
        x_ref[:, start : start + span] = jnp.dot(
            compact_map((rows, count * ROWS), 0, chunk),
            blocks[:, :span],
            preferred_element_type=F32,
        ).astype(BF16)
    x = x_ref[...]
    gate_val = jnp.dot(x, w_gate[...], preferred_element_type=F32)
    up_val = jnp.dot(x, w_up[...], preferred_element_type=F32)
    hidden = (gate_val / (1.0 + jnp.exp(-gate_val)) * up_val).astype(BF16)
    part_ref[...] = jnp.dot(hidden, w_down[...], preferred_element_type=F32).astype(BF16)
    total = None
    for chunk in range(CHUNKS):
        start, span = chunk_span(width, chunk)
        piece = jnp.dot(
            compact_map((count * ROWS, rows), 1, chunk),
            part_ref[:, start : start + span],
            preferred_element_type=F32,
        )
        if span < chunk_width(width):
            piece = jnp.concatenate(
                [piece, jnp.zeros((piece.shape[0], chunk_width(width) - span), F32)], axis=1
            )
        total = piece if total is None else total + piece
    total = total.astype(BF16)
    hand_out(total, outs)


def sum_kernel(count, *refs):
    ins, outs = refs[:count], refs[count:]
    total = ins[0][...].astype(F32)
    for ref in ins[1:]:
        total = total + ref[...].astype(F32)
    hand_out(total.astype(BF16), outs)


def call(body, outs, ins, megabytes, scratch=(), flops=0, space=VMEM):
    moved = sum(a.size * a.dtype.itemsize for a in (*ins, *outs))
    return pl.pallas_call(
        body,
        out_shape=outs,
        in_specs=[space] * len(ins),
        out_specs=[VMEM] * len(outs),
        scratch_shapes=list(scratch),
        compiler_params=pltpu.CompilerParams(vmem_limit_bytes=megabytes << 20),
        cost_estimate=pl.CostEstimate(flops=flops, bytes_accessed=moved, transcendentals=0),
    )(*ins)


def on_device(tokens, gain, routes_1, gates_1, routes_2, gates_2, gate_proj, up_proj, down_proj):
    sections, devices = lax.axis_size("section"), lax.axis_size("expert")
    group = devices // EXPERTS
    rows, width = tokens.shape[1:]
    weights = (gate_proj[0, 0], up_proj[0, 0], down_proj[0, 0])
    wide = chunk_width(width)
    block = jax.ShapeDtypeStruct((ROWS, wide), BF16)
    stack = jax.ShapeDtypeStruct((EXPERTS * ROWS, wide), BF16)
    whole = jax.ShapeDtypeStruct((rows, width), BF16)
    ahead = jax.ShapeDtypeStruct((rows, width + 128), BF16)
    routes_1, gates_1, routes_2, gates_2 = (
        a.reshape(1, rows) for a in (routes_1, gates_1, routes_2, gates_2)
    )

    def to_expert(place):
        far = distance(place)
        return [(i, (i // group ^ far) * group + i % group) for i in range(devices)]

    def within(shift):
        return [(i, i // group * group + (i + shift) % group) for i in range(devices)]

    def onward(place):
        return [
            (s * devices + i, (s + 1) % sections * devices + j)
            for s in range(sections)
            for i, j in to_expert(place)
        ]

    def across(blocks):
        arrived = [lax.ppermute(blocks[i], "expert", to_expert(i)) for i in range(EXPERTS - 1)]
        return arrived + [blocks[EXPERTS - 1]]

    def shared(arrived):
        ins = list(arrived)
        for m in range(1, group):
            ins += [lax.ppermute(a, "expert", within(m)) for a in arrived]
        return ins

    def swapped(stacked):
        chips = [[e * group + j for e in range(EXPERTS)] for j in range(group)]
        return lax.all_to_all(
            stacked, "expert", 0, 0, axis_index_groups=chips, tiled=True
        )

    def experts(ins, parts):
        count = EXPERTS * group
        held = -(-count * CAP // ROWS) * ROWS
        sums = call(
            functools.partial(expert_kernel, len(ins)),
            [stack] * group,
            [*weights, *ins],
            24,
            [pltpu.VMEM((held, width), BF16), pltpu.VMEM((held, width), BF16)],
            flops=6 * held * width * weights[0].shape[1],
        )
        terms = [sums[0]] + [lax.ppermute(sums[m], "expert", within(-m)) for m in range(1, group)]
        return call(functools.partial(sum_kernel, group), parts, terms, 8)

    sources = [
        pltpu.with_memory_space_constraint(a, pltpu.HBM)
        for a in (tokens[0], gain, routes_1, gates_1)
    ]
    *blocks, travelling = call(
        functools.partial(pack_kernel, group),
        [block] * EXPERTS + [ahead],
        sources,
        8,
        [pltpu.VMEM(a.shape, a.dtype) for a in sources]
        + [pltpu.SemaphoreType.DMA((len(sources),))],
        flops=10**10,
        space=HBM,
    )
    ins = shared(across(blocks))
    before = lax.ppermute(travelling, "section", [(i, (i + 1) % sections) for i in range(sections)])
    *ins, before = lax.optimization_barrier((*ins, before))
    sums = experts(ins, [block] * EXPERTS)
    home = [lax.ppermute(sums[i], ("section", "expert"), onward(i)) for i in range(EXPERTS)]
    first, blocks = call(
        functools.partial(middle_kernel, group), [whole, stack], [*home, before, gain, routes_2], 8
    )
    (sums,) = experts(shared([swapped(blocks)]), [stack])
    (mixed,) = call(last_kernel, [whole], [first, swapped(sums), routes_2, gates_2], 8)
    return mixed[None]


def solution(mesh):
    rows = P("section", "expert", None)
    slabs = P("section", "expert", None, None)
    return jax.shard_map(
        on_device,
        mesh=mesh,
        in_specs=(rows, P("section", None), rows, rows, rows, rows, slabs, slabs, slabs),
        out_specs=rows,
        check_vma=False,
    )
```

```python
import functools

import jax
import jax.numpy as jnp
from jax import lax
from jax.experimental import pallas as pl
from jax.experimental.pallas import tpu as pltpu
from jax.sharding import PartitionSpec as P

EXPERTS = 4
CAP = 5
ROWS = 16
CHUNKS = 3
EPS = 1e-06
F32 = jnp.float32
BF16 = jnp.bfloat16
VMEM = pl.BlockSpec(memory_space=pltpu.VMEM)
HBM = pl.BlockSpec(memory_space=pltpu.HBM)


def distance(place):
    return EXPERTS - 1 - place


def fifth(value):
    return (value * 205) >> 10


def chunk_width(width):
    return -(-width // (CHUNKS * 128)) * 128


def chunk_span(width, chunk):
    start = chunk * chunk_width(width)
    return start, min(width, start + chunk_width(width)) - start


def upright(row):
    rows = row.shape[1]
    same = lax.broadcasted_iota(jnp.int32, (rows, rows), 0) == lax.broadcasted_iota(
        jnp.int32, (rows, rows), 1
    )
    return jnp.sum(jnp.where(same, row, 0.0), axis=1, keepdims=True)


def slots_of(routes):
    rows = routes.shape[0]
    lanes = lax.broadcasted_iota(jnp.int32, (rows, 128), 1).astype(F32)
    one_hot = (routes == lanes).astype(F32)
    earlier = lax.broadcasted_iota(jnp.int32, (rows, rows), 0) > lax.broadcasted_iota(
        jnp.int32, (rows, rows), 1
    )
    before = jnp.dot(earlier.astype(BF16), one_hot.astype(BF16), preferred_element_type=F32)
    return routes * CAP + jnp.sum(before * one_hot, axis=1, keepdims=True)


def block_map(slots, expert, chunk):
    spot = lax.broadcasted_iota(jnp.int32, (slots.shape[0], EXPERTS * ROWS), 1)
    inner = (spot & (ROWS - 1)) - CAP * chunk
    target = (distance(spot >> 4) ^ expert) * CAP + inner
    target = jnp.where((inner >= 0) & (inner < CAP), target, -1)
    return (slots == target.astype(F32)).astype(BF16)


def normalize(values, gain):
    inv_scale = lax.rsqrt(jnp.mean(values * values, axis=-1, keepdims=True) + EPS)
    return (values * inv_scale * gain).astype(BF16)


def write_blocks(normed, slots, expert, block_refs):
    width = normed.shape[1]
    pieces = []
    for chunk in range(CHUNKS):
        start, span = chunk_span(width, chunk)
        piece = lax.dot_general(
            block_map(slots, expert, chunk),
            normed[:, start : start + span],
            (((0,), (0,)), ((), ())),
            preferred_element_type=F32,
        )
        if span < chunk_width(width):
            piece = jnp.concatenate(
                [piece, jnp.zeros((piece.shape[0], chunk_width(width) - span), F32)], axis=1
            )
        pieces.append(piece)
    packed = sum(pieces[1:], pieces[0]).astype(BF16)
    hand_out(packed, block_refs)


def hand_out(values, refs):
    start = 0
    for ref in refs:
        ref[...] = values[start : start + ref.shape[0]]
        start += ref.shape[0]


def my_expert(group):
    return lax.axis_index("expert") // group


def split_parts(values):
    parts = []
    for _ in range(3):
        parts.append(values.astype(BF16))
        values = values - parts[-1].astype(F32)
    return parts


def pack_kernel(group, *refs):
    sources, block_refs, ahead_ref = refs[:4], refs[4 : 4 + EXPERTS], refs[4 + EXPERTS]
    held, sems = refs[5 + EXPERTS : -1], refs[-1]
    copies = [
        pltpu.make_async_copy(source, place, sems.at[i])
        for i, (source, place) in enumerate(zip(sources, held))
    ]
    for copy in copies:
        copy.start()
    for copy in copies:
        copy.wait()
    x_ref, gain_ref, routes_ref, gates_ref = held
    rows, width = x_ref.shape
    slots = slots_of(upright(routes_ref[...].astype(F32)))
    lane = lax.broadcasted_iota(jnp.int32, (rows, 128), 1)
    meta = jnp.zeros((rows, 128), F32)
    for i, column in enumerate([slots, *split_parts(upright(gates_ref[...]))]):
        meta = jnp.where(lane == i, column.astype(F32), meta)
    ahead_ref[:, :width] = x_ref[...]
    ahead_ref[:, width:] = meta.astype(BF16)
    normed = normalize(x_ref[...].astype(F32), gain_ref[...])
    write_blocks(normed, slots, my_expert(group), block_refs)


def residual(x, slots, gates, expert, blocks):
    width = x.shape[1]
    found = []
    for chunk in range(CHUNKS):
        _, span = chunk_span(width, chunk)
        found.append(
            jnp.dot(
                block_map(slots, expert, chunk), blocks[:, :span], preferred_element_type=F32
            )
        )
    update = (gates * jnp.concatenate(found, axis=1)).astype(BF16)
    return x.astype(F32) + update.astype(F32)


def middle_kernel(group, b0, b1, b2, carried_ref, gain_ref, routes_ref, first_ref, *block_refs):
    expert = my_expert(group)
    width = first_ref.shape[1]
    blocks = jnp.concatenate([b0[...], b1[...], b2[...], carried_ref[:, width + 128 :]], axis=0)
    meta = carried_ref[:, width : width + 128].astype(F32)
    gates = meta[:, 1:2] + meta[:, 2:3] + meta[:, 3:4]
    first = residual(carried_ref[:, :width], meta[:, 0:1], gates, expert, blocks).astype(BF16)
    first_ref[...] = first
    slots = slots_of(upright(routes_ref[...].astype(F32)))
    normed = normalize(first.astype(F32), gain_ref[...])
    write_blocks(normed, slots, expert, block_refs)


def last_kernel(group, x_ref, b0, b1, b2, b3, routes_ref, gates_ref, out_ref):
    blocks = jnp.concatenate([b0[...], b1[...], b2[...], b3[...]], axis=0)
    slots = slots_of(upright(routes_ref[...].astype(F32)))
    gates = upright(gates_ref[...])
    out_ref[...] = residual(x_ref[...], slots, gates, my_expert(group), blocks).astype(BF16)


def compact_map(shape, compact_dim, chunk):
    compact = lax.broadcasted_iota(jnp.int32, shape, compact_dim)
    spot = lax.broadcasted_iota(jnp.int32, shape, 1 - compact_dim)
    block = fifth(compact)
    wanted = block * ROWS + CAP * chunk + compact - CAP * block
    return (wanted == spot).astype(BF16)


def expert_kernel(given, w_gate, w_up, w_down, *refs):
    ins, outs, (x_ref, part_ref) = refs[:given], refs[given:-2], refs[-2:]
    count = sum(ref.shape[0] for ref in ins) // ROWS
    width, units = w_gate.shape
    rows = x_ref.shape[0]
    blocks = jnp.concatenate([ref[...] for ref in ins], axis=0)
    for chunk in range(CHUNKS):
        start, span = chunk_span(width, chunk)
        x_ref[:, start : start + span] = jnp.dot(
            compact_map((rows, count * ROWS), 0, chunk),
            blocks[:, :span],
            preferred_element_type=F32,
        ).astype(BF16)
    x = x_ref[...]
    gate_val = jnp.dot(x, w_gate[...], preferred_element_type=F32)
    up_val = jnp.dot(x, w_up[...], preferred_element_type=F32)
    hidden = (gate_val / (1.0 + jnp.exp(-gate_val)) * up_val).astype(BF16)
    part_ref[...] = jnp.dot(hidden, w_down[...], preferred_element_type=F32).astype(BF16)
    total = None
    for chunk in range(CHUNKS):
        start, span = chunk_span(width, chunk)
        piece = jnp.dot(
            compact_map((count * ROWS, rows), 1, chunk),
            part_ref[:, start : start + span],
            preferred_element_type=F32,
        )
        if span < chunk_width(width):
            piece = jnp.concatenate(
                [piece, jnp.zeros((piece.shape[0], chunk_width(width) - span), F32)], axis=1
            )
        total = piece if total is None else total + piece
    total = total.astype(BF16)
    hand_out(total, outs)


def summed(refs):
    total = refs[0][...].astype(F32)
    for ref in refs[1:]:
        total = total + ref[...].astype(F32)
    return total.astype(BF16)


def sum_kernel(given, *refs):
    hand_out(summed(refs[:given]), refs[given:])


def carry_kernel(ahead_ref, *refs):
    ins, out_ref = refs[:-1], refs[-1]
    width = ahead_ref.shape[1]
    out_ref[:, :width] = ahead_ref[...]
    out_ref[:, width:] = summed(ins)


def call(body, outs, ins, megabytes, scratch=(), flops=0, space=VMEM):
    moved = sum(a.size * a.dtype.itemsize for a in (*ins, *outs))
    return pl.pallas_call(
        body,
        out_shape=outs,
        in_specs=[space] * len(ins),
        out_specs=[VMEM] * len(outs),
        scratch_shapes=list(scratch),
        compiler_params=pltpu.CompilerParams(vmem_limit_bytes=megabytes << 20),
        cost_estimate=pl.CostEstimate(flops=flops, bytes_accessed=moved, transcendentals=0),
    )(*ins)


def on_device(tokens, gain, routes_1, gates_1, routes_2, gates_2, gate_proj, up_proj, down_proj):
    sections, devices = lax.axis_size("section"), lax.axis_size("expert")
    group = devices // EXPERTS
    rows, width = tokens.shape[1:]
    weights = (gate_proj[0, 0], up_proj[0, 0], down_proj[0, 0])
    wide = chunk_width(width)
    block = jax.ShapeDtypeStruct((ROWS, wide), BF16)
    whole = jax.ShapeDtypeStruct((rows, width), BF16)
    ahead = jax.ShapeDtypeStruct((rows, width + 128), BF16)
    routes_1, gates_1, routes_2, gates_2 = (
        a.reshape(1, rows) for a in (routes_1, gates_1, routes_2, gates_2)
    )

    def to_expert(place):
        far = distance(place)
        return [(i, (i // group ^ far) * group + i % group) for i in range(devices)]

    def within(shift):
        return [(i, i // group * group + (i + shift) % group) for i in range(devices)]

    def onward(place):
        return [
            (s * devices + i, (s + 1) % sections * devices + j)
            for s in range(sections)
            for i, j in to_expert(place)
        ]

    def across(blocks):
        return [lax.ppermute(blocks[i], "expert", to_expert(i)) for i in range(EXPERTS - 1)]

    def shared(arrived):
        return arrived + [
            lax.ppermute(a, "expert", within(m)) for m in range(1, group) for a in arrived
        ]

    def experts(ins):
        count = sum(a.shape[0] for a in ins) // ROWS
        held = -(-count * CAP // ROWS) * ROWS
        sums = call(
            functools.partial(expert_kernel, len(ins)),
            [jax.ShapeDtypeStruct((count // group * ROWS, wide), BF16)] * group,
            [*weights, *ins],
            24,
            [pltpu.VMEM((held, width), BF16), pltpu.VMEM((held, width), BF16)],
            flops=6 * 256 * width * weights[0].shape[1],
        )
        return [sums[0]] + [
            lax.ppermute(sums[m], "expert", within(-m)) for m in range(1, group)
        ]

    def added(terms):
        parts = terms[0].shape[0] // ROWS
        return call(functools.partial(sum_kernel, group), [block] * parts, terms, 8)

    sources = [
        pltpu.with_memory_space_constraint(a, pltpu.HBM)
        for a in (tokens[0], gain, routes_1, gates_1)
    ]
    *blocks, travelling = call(
        functools.partial(pack_kernel, group),
        [block] * EXPERTS + [ahead],
        sources,
        8,
        [pltpu.VMEM(a.shape, a.dtype) for a in sources]
        + [pltpu.SemaphoreType.DMA((len(sources),))],
        flops=10**10,
        space=HBM,
    )
    arrived = across(blocks[:-1])
    (carry,) = call(
        carry_kernel,
        [jax.ShapeDtypeStruct((rows, width + 128 + wide), BF16)],
        [travelling, *experts(shared(blocks[-1:]))],
        8,
    )
    *ins, carry = lax.optimization_barrier((*shared(arrived), carry))
    carried = lax.ppermute(carry, "section", [(i, (i + 1) % sections) for i in range(sections)])
    sums = added(experts(ins))
    home = [lax.ppermute(sums[i], ("section", "expert"), onward(i)) for i in range(EXPERTS - 1)]
    first, *blocks = call(
        functools.partial(middle_kernel, group),
        [whole] + [block] * EXPERTS,
        [*home, carried, gain, routes_2],
        8,
    )
    sums = added(experts(shared(across(blocks[:-1]) + blocks[-1:])))
    home = across(sums[:-1])
    (mixed,) = call(
        functools.partial(last_kernel, group),
        [whole],
        [first, *home, sums[-1], routes_2, gates_2],
        8,
    )
    return mixed[None]


def solution(mesh):
    rows = P("section", "expert", None)
    slabs = P("section", "expert", None, None)
    return jax.shard_map(
        on_device,
        mesh=mesh,
        in_specs=(rows, P("section", None), rows, rows, rows, rows, slabs, slabs, slabs),
        out_specs=rows,
        check_vma=False,
    )
```

```python
import functools

import jax
import jax.numpy as jnp
from jax import lax
from jax.experimental import pallas as pl
from jax.experimental.pallas import tpu as pltpu
from jax.sharding import PartitionSpec as P

EXPERTS = 4
CAP = 5
ROWS = 16
LANES = 256
EPS = 1e-06
F32 = jnp.float32
BF16 = jnp.bfloat16
VMEM = pl.BlockSpec(memory_space=pltpu.VMEM)
HBM = pl.BlockSpec(memory_space=pltpu.HBM)


def distance(place):
    return EXPERTS - 1 - place


def fifth(value):
    return (value * 205) >> 10


def pad_rows(count):
    return -(-count // ROWS) * ROWS


def block_shape(width):
    return CAP * width // LANES, LANES


def spread_scratch(rows, width):
    return pltpu.VMEM((LANES // 128, rows * width // LANES, 128), F32)


def spread(values, spread_ref):
    rows, width = values.shape
    pieces = width // LANES
    for tile in range(width // 128):
        piece, half = divmod(tile, LANES // 128)
        spread_ref[half, pl.ds(piece, rows, stride=pieces), :] = values[
            :, tile * 128 : (tile + 1) * 128
        ]


def gathered(spread_ref, rows, width):
    pieces = width // LANES
    tiles = []
    for tile in range(width // 128):
        piece, half = divmod(tile, LANES // 128)
        tiles.append(spread_ref[half, pl.ds(piece, rows, stride=pieces), :].astype(BF16))
    return jnp.concatenate(tiles, axis=1)


def to_blocks(spread_ref, refs):
    start = 0
    for ref in refs:
        stop = start + ref.shape[0]
        for half in range(LANES // 128):
            ref[:, half * 128 : (half + 1) * 128] = spread_ref[half, start:stop, :].astype(BF16)
        start = stop


def from_blocks(arrays, spread_ref):
    start = 0
    for array in arrays:
        stop = start + array.shape[0]
        for half in range(LANES // 128):
            spread_ref[half, start:stop, :] = array[:, half * 128 : (half + 1) * 128].astype(F32)
        start = stop
    return start


def upright(row):
    rows = row.shape[1]
    same = lax.broadcasted_iota(jnp.int32, (rows, rows), 0) == lax.broadcasted_iota(
        jnp.int32, (rows, rows), 1
    )
    return jnp.sum(jnp.where(same, row, 0.0), axis=1, keepdims=True)


def slots_of(routes):
    rows = routes.shape[0]
    lanes = lax.broadcasted_iota(jnp.int32, (rows, 128), 1).astype(F32)
    one_hot = (routes == lanes).astype(F32)
    earlier = lax.broadcasted_iota(jnp.int32, (rows, rows), 0) > lax.broadcasted_iota(
        jnp.int32, (rows, rows), 1
    )
    before = jnp.dot(earlier.astype(BF16), one_hot.astype(BF16), preferred_element_type=F32)
    return routes * CAP + jnp.sum(before * one_hot, axis=1, keepdims=True)


def block_map(slots, expert):
    place = lax.broadcasted_iota(jnp.int32, (slots.shape[0], pad_rows(EXPERTS * CAP)), 1)
    block = fifth(place)
    target = (distance(block) ^ expert) * CAP + place - CAP * block
    target = jnp.where(block < EXPERTS, target, -1)
    return (slots == target.astype(F32)).astype(BF16)


def normalize(values, gain):
    inv_scale = lax.rsqrt(jnp.mean(values * values, axis=-1, keepdims=True) + EPS)
    return (values * inv_scale * gain).astype(BF16)


def write_blocks(normed, slots, expert, spread_ref, block_refs):
    packed = lax.dot_general(
        block_map(slots, expert),
        normed,
        (((0,), (0,)), ((), ())),
        preferred_element_type=F32,
    )
    spread(packed, spread_ref)
    to_blocks(spread_ref, block_refs)


def hand_out(values, refs):
    start = 0
    for ref in refs:
        ref[...] = values[start : start + ref.shape[0]]
        start += ref.shape[0]


def my_expert(group):
    return lax.axis_index("expert") // group


def split_parts(values):
    parts = []
    for _ in range(3):
        parts.append(values.astype(BF16))
        values = values - parts[-1].astype(F32)
    return parts


def pack_kernel(group, *refs):
    sources, block_refs, ahead_ref = refs[:4], refs[4 : 4 + EXPERTS], refs[4 + EXPERTS]
    held, spread_ref, sems = refs[5 + EXPERTS : -2], refs[-2], refs[-1]
    copies = [
        pltpu.make_async_copy(source, place, sems.at[i])
        for i, (source, place) in enumerate(zip(sources, held))
    ]
    for copy in copies:
        copy.start()
    for copy in copies:
        copy.wait()
    x_ref, gain_ref, routes_ref, gates_ref = held
    rows, width = x_ref.shape
    slots = slots_of(upright(routes_ref[...].astype(F32)))
    lane = lax.broadcasted_iota(jnp.int32, (rows, LANES), 1)
    meta = jnp.zeros((rows, LANES), F32)
    for i, column in enumerate([slots, *split_parts(upright(gates_ref[...]))]):
        meta = jnp.where(lane == i, column.astype(F32), meta)
    for piece in range(width // LANES):
        ahead_ref[piece * rows : (piece + 1) * rows] = x_ref[:, piece * LANES : (piece + 1) * LANES]
    ahead_ref[width // LANES * rows :] = meta.astype(BF16)
    normed = normalize(x_ref[...].astype(F32), gain_ref[...])
    write_blocks(normed, slots, my_expert(group), spread_ref, block_refs)


def residual(x, slots, gates, expert, blocks, spread_ref):
    width = x.shape[1]
    filled = from_blocks(blocks, spread_ref)
    spread_ref[:, filled:, :] = jnp.zeros(
        (spread_ref.shape[0], spread_ref.shape[1] - filled, 128), F32
    )
    found = jnp.dot(
        block_map(slots, expert),
        gathered(spread_ref, pad_rows(EXPERTS * CAP), width),
        preferred_element_type=F32,
    )
    update = (gates * found).astype(BF16)
    return x.astype(F32) + update.astype(F32)


def middle_kernel(group, *refs):
    block_ins, carried_ref, gain_ref, routes_ref = refs[: EXPERTS - 1], *refs[EXPERTS - 1 : EXPERTS + 2]
    first_ref, block_refs, spread_ref = refs[EXPERTS + 2], refs[EXPERTS + 3 : -1], refs[-1]
    expert = my_expert(group)
    rows, width = first_ref.shape
    pieces = width // LANES
    x = jnp.concatenate(
        [carried_ref[piece * rows : (piece + 1) * rows] for piece in range(pieces)], axis=1
    )
    meta = carried_ref[pieces * rows : (pieces + 1) * rows].astype(F32)
    gates = meta[:, 1:2] + meta[:, 2:3] + meta[:, 3:4]
    blocks = [ref[...] for ref in block_ins] + [carried_ref[(pieces + 1) * rows :]]
    first = residual(x, meta[:, 0:1], gates, expert, blocks, spread_ref).astype(BF16)
    first_ref[...] = first
    slots = slots_of(upright(routes_ref[...].astype(F32)))
    normed = normalize(first.astype(F32), gain_ref[...])
    write_blocks(normed, slots, expert, spread_ref, block_refs)


def last_kernel(group, x_ref, b0, b1, b2, b3, routes_ref, gates_ref, out_ref, spread_ref):
    slots = slots_of(upright(routes_ref[...].astype(F32)))
    gates = upright(gates_ref[...])
    blocks = [ref[...] for ref in (b0, b1, b2, b3)]
    mixed = residual(x_ref[...], slots, gates, my_expert(group), blocks, spread_ref)
    out_ref[...] = mixed.astype(BF16)


def expert_kernel(given, w_gate, w_up, w_down, *refs):
    ins, outs, spread_ref = refs[:given], refs[given:-1], refs[-1]
    width = w_gate.shape[0]
    rows = spread_ref.shape[1] * LANES // width
    from_blocks([ref[...] for ref in ins], spread_ref)
    x = gathered(spread_ref, rows, width)
    gate_val = jnp.dot(x, w_gate[...], preferred_element_type=F32)
    up_val = jnp.dot(x, w_up[...], preferred_element_type=F32)
    hidden = (gate_val / (1.0 + jnp.exp(-gate_val)) * up_val).astype(BF16)
    spread(jnp.dot(hidden, w_down[...], preferred_element_type=F32), spread_ref)
    to_blocks(spread_ref, outs)


def summed(refs):
    total = refs[0][...].astype(F32)
    for ref in refs[1:]:
        total = total + ref[...].astype(F32)
    return total.astype(BF16)


def sum_kernel(given, *refs):
    hand_out(summed(refs[:given]), refs[given:])


def carry_kernel(ahead_ref, *refs):
    ins, out_ref = refs[:-1], refs[-1]
    rows = ahead_ref.shape[0]
    out_ref[:rows] = ahead_ref[...]
    out_ref[rows:] = summed(ins)


def call(body, outs, ins, megabytes, scratch=(), flops=0, space=VMEM):
    moved = sum(a.size * a.dtype.itemsize for a in (*ins, *outs))
    return pl.pallas_call(
        body,
        out_shape=outs,
        in_specs=[space] * len(ins),
        out_specs=[VMEM] * len(outs),
        scratch_shapes=list(scratch),
        compiler_params=pltpu.CompilerParams(vmem_limit_bytes=megabytes << 20),
        cost_estimate=pl.CostEstimate(flops=flops, bytes_accessed=moved, transcendentals=0),
    )(*ins)


def on_device(tokens, gain, routes_1, gates_1, routes_2, gates_2, gate_proj, up_proj, down_proj):
    sections, devices = lax.axis_size("section"), lax.axis_size("expert")
    group = devices // EXPERTS
    rows, width = tokens.shape[1:]
    weights = (gate_proj[0, 0], up_proj[0, 0], down_proj[0, 0])
    tall, wide = block_shape(width)
    block = jax.ShapeDtypeStruct((tall, wide), BF16)
    packing = spread_scratch(pad_rows(EXPERTS * CAP), width)
    whole = jax.ShapeDtypeStruct((rows, width), BF16)
    ahead = (width // LANES + 1) * rows
    routes_1, gates_1, routes_2, gates_2 = (
        a.reshape(1, rows) for a in (routes_1, gates_1, routes_2, gates_2)
    )

    def to_expert(place):
        far = distance(place)
        return [(i, (i // group ^ far) * group + i % group) for i in range(devices)]

    def within(shift):
        return [(i, i // group * group + (i + shift) % group) for i in range(devices)]

    def onward(place):
        return [
            (s * devices + i, (s + 1) % sections * devices + j)
            for s in range(sections)
            for i, j in to_expert(place)
        ]

    def across(blocks):
        return [lax.ppermute(blocks[i], "expert", to_expert(i)) for i in range(EXPERTS - 1)]

    def shared(arrived):
        return arrived + [
            lax.ppermute(a, "expert", within(m)) for m in range(1, group) for a in arrived
        ]

    def experts(ins):
        count = sum(a.shape[0] for a in ins) // tall
        sums = call(
            functools.partial(expert_kernel, len(ins)),
            [jax.ShapeDtypeStruct((count // group * tall, wide), BF16)] * group,
            [*weights, *ins],
            24,
            [spread_scratch(pad_rows(count * CAP), width)],
            flops=6 * 256 * width * weights[0].shape[1],
        )
        return [sums[0]] + [
            lax.ppermute(sums[m], "expert", within(-m)) for m in range(1, group)
        ]

    def added(terms):
        parts = terms[0].shape[0] // tall
        return call(functools.partial(sum_kernel, group), [block] * parts, terms, 8)

    sources = [
        pltpu.with_memory_space_constraint(a, pltpu.HBM)
        for a in (tokens[0], gain, routes_1, gates_1)
    ]
    *blocks, travelling = call(
        functools.partial(pack_kernel, group),
        [block] * EXPERTS + [jax.ShapeDtypeStruct((ahead, LANES), BF16)],
        sources,
        8,
        [pltpu.VMEM(a.shape, a.dtype) for a in sources]
        + [packing, pltpu.SemaphoreType.DMA((len(sources),))],
        flops=10**10,
        space=HBM,
    )
    arrived = across(blocks[:-1])
    (carry,) = call(
        carry_kernel,
        [jax.ShapeDtypeStruct((ahead + tall, LANES), BF16)],
        [travelling, *experts(shared(blocks[-1:]))],
        8,
    )
    *ins, carry = lax.optimization_barrier((*shared(arrived), carry))
    carried = lax.ppermute(carry, "section", [(i, (i + 1) % sections) for i in range(sections)])
    sums = added(experts(ins))
    home = [lax.ppermute(sums[i], ("section", "expert"), onward(i)) for i in range(EXPERTS - 1)]
    first, *blocks = call(
        functools.partial(middle_kernel, group),
        [whole] + [block] * EXPERTS,
        [*home, carried, gain, routes_2],
        8,
        [packing],
    )
    sums = added(experts(shared(across(blocks[:-1]) + blocks[-1:])))
    home = across(sums[:-1])
    (mixed,) = call(
        functools.partial(last_kernel, group),
        [whole],
        [first, *home, sums[-1], routes_2, gates_2],
        8,
        [packing],
    )
    return mixed[None]


def solution(mesh):
    rows = P("section", "expert", None)
    slabs = P("section", "expert", None, None)
    return jax.shard_map(
        on_device,
        mesh=mesh,
        in_specs=(rows, P("section", None), rows, rows, rows, rows, slabs, slabs, slabs),
        out_specs=rows,
        check_vma=False,
    )
```

```python
import functools

import jax
import jax.numpy as jnp
from jax import lax
from jax.experimental import pallas as pl
from jax.experimental.pallas import tpu as pltpu
from jax.sharding import PartitionSpec as P

EXPERTS = 4
CAP = 5
ROWS = 16
LANES = 256
PIECE = 512
PARTS = 4
EPS = 1e-06
F32 = jnp.float32
BF16 = jnp.bfloat16
VMEM = pl.BlockSpec(memory_space=pltpu.VMEM)
HBM = pl.BlockSpec(memory_space=pltpu.HBM)


def distance(place):
    return EXPERTS - 1 - place


def fifth(value):
    return (value * 205) >> 10


def pad_rows(count):
    return -(-count // ROWS) * ROWS


def block_shape(width):
    return CAP * width // LANES, LANES


def spread_scratch(rows, width):
    return pltpu.VMEM((LANES // 128, rows * width // LANES, 128), F32)


def spread(values, spread_ref, width, start=0):
    rows, columns = values.shape
    pieces = width // LANES
    for tile in range(columns // 128):
        piece, half = divmod(start // 128 + tile, LANES // 128)
        spread_ref[half, pl.ds(piece, rows, stride=pieces), :] = values[
            :, tile * 128 : (tile + 1) * 128
        ]


def gathered(spread_ref, rows, width, start=0, columns=None):
    pieces = width // LANES
    tiles = []
    for tile in range(start // 128, (start + (columns or width)) // 128):
        piece, half = divmod(tile, LANES // 128)
        tiles.append(spread_ref[half, pl.ds(piece, rows, stride=pieces), :].astype(BF16))
    return jnp.concatenate(tiles, axis=1)


def to_blocks(spread_ref, refs):
    start = 0
    for ref in refs:
        stop = start + ref.shape[0]
        for half in range(LANES // 128):
            ref[:, half * 128 : (half + 1) * 128] = spread_ref[half, start:stop, :].astype(BF16)
        start = stop


def from_blocks(arrays, spread_ref):
    start = 0
    for array in arrays:
        stop = start + array.shape[0]
        for half in range(LANES // 128):
            spread_ref[half, start:stop, :] = array[:, half * 128 : (half + 1) * 128].astype(F32)
        start = stop
    return start


def upright(row):
    rows = row.shape[1]
    same = lax.broadcasted_iota(jnp.int32, (rows, rows), 0) == lax.broadcasted_iota(
        jnp.int32, (rows, rows), 1
    )
    return jnp.sum(jnp.where(same, row, 0.0), axis=1, keepdims=True)


def slots_of(routes):
    rows = routes.shape[0]
    lanes = lax.broadcasted_iota(jnp.int32, (rows, 128), 1).astype(F32)
    one_hot = (routes == lanes).astype(F32)
    earlier = lax.broadcasted_iota(jnp.int32, (rows, rows), 0) > lax.broadcasted_iota(
        jnp.int32, (rows, rows), 1
    )
    before = jnp.dot(earlier.astype(BF16), one_hot.astype(BF16), preferred_element_type=F32)
    return routes * CAP + jnp.sum(before * one_hot, axis=1, keepdims=True)


def block_map(slots, expert):
    place = lax.broadcasted_iota(jnp.int32, (slots.shape[0], pad_rows(EXPERTS * CAP)), 1)
    block = fifth(place)
    target = (distance(block) ^ expert) * CAP + place - CAP * block
    target = jnp.where(block < EXPERTS, target, -1)
    return (slots == target.astype(F32)).astype(BF16)


def normalize(values, gain):
    inv_scale = lax.rsqrt(jnp.mean(values * values, axis=-1, keepdims=True) + EPS)
    return (values * inv_scale * gain).astype(BF16)


def write_blocks(normed, slots, expert, spread_ref, block_refs):
    packed = lax.dot_general(
        block_map(slots, expert),
        normed,
        (((0,), (0,)), ((), ())),
        preferred_element_type=F32,
    )
    spread(packed, spread_ref, normed.shape[1])
    to_blocks(spread_ref, block_refs)


def hand_out(values, refs):
    start = 0
    for ref in refs:
        ref[...] = values[start : start + ref.shape[0]]
        start += ref.shape[0]


def my_expert(group):
    return lax.axis_index("expert") // group


def split_parts(values):
    parts = []
    for _ in range(3):
        parts.append(values.astype(BF16))
        values = values - parts[-1].astype(F32)
    return parts


def pack_kernel(group, *refs):
    sources, block_refs, ahead_ref = refs[:4], refs[4 : 4 + EXPERTS], refs[4 + EXPERTS]
    held, spread_ref, sems = refs[5 + EXPERTS : -2], refs[-2], refs[-1]
    copies = [
        pltpu.make_async_copy(source, place, sems.at[i])
        for i, (source, place) in enumerate(zip(sources, held))
    ]
    for copy in copies:
        copy.start()
    for copy in copies:
        copy.wait()
    x_ref, gain_ref, routes_ref, gates_ref = held
    rows, width = x_ref.shape
    slots = slots_of(upright(routes_ref[...].astype(F32)))
    lane = lax.broadcasted_iota(jnp.int32, (rows, LANES), 1)
    meta = jnp.zeros((rows, LANES), F32)
    for i, column in enumerate([slots, *split_parts(upright(gates_ref[...]))]):
        meta = jnp.where(lane == i, column.astype(F32), meta)
    for piece in range(width // LANES):
        ahead_ref[piece * rows : (piece + 1) * rows] = x_ref[:, piece * LANES : (piece + 1) * LANES]
    ahead_ref[width // LANES * rows :] = meta.astype(BF16)
    normed = normalize(x_ref[...].astype(F32), gain_ref[...])
    write_blocks(normed, slots, my_expert(group), spread_ref, block_refs)


def fill(blocks, spread_ref):
    filled = from_blocks(blocks, spread_ref)
    spread_ref[:, filled:, :] = jnp.zeros(
        (spread_ref.shape[0], spread_ref.shape[1] - filled, 128), F32
    )


def residual(x, gates, chosen, spread_ref, width, start=0):
    found = jnp.dot(
        chosen,
        gathered(spread_ref, chosen.shape[1], width, start, x.shape[1]),
        preferred_element_type=F32,
    )
    update = (gates * found).astype(BF16)
    return (x.astype(F32) + update.astype(F32)).astype(BF16)


def middle_kernel(group, *refs):
    block_ins, carried_ref, gain_ref, routes_ref = refs[: EXPERTS - 1], *refs[EXPERTS - 1 : EXPERTS + 2]
    first_ref, block_refs, spread_ref = refs[EXPERTS + 2], refs[EXPERTS + 3 : -1], refs[-1]
    expert = my_expert(group)
    rows, width = first_ref.shape
    pieces = width // LANES
    x = jnp.concatenate(
        [carried_ref[piece * rows : (piece + 1) * rows] for piece in range(pieces)], axis=1
    )
    meta = carried_ref[pieces * rows : (pieces + 1) * rows].astype(F32)
    gates = meta[:, 1:2] + meta[:, 2:3] + meta[:, 3:4]
    blocks = [ref[...] for ref in block_ins] + [carried_ref[(pieces + 1) * rows :]]
    fill(blocks, spread_ref)
    first = residual(x, gates, block_map(meta[:, 0:1], expert), spread_ref, width)
    first_ref[...] = first
    slots = slots_of(upright(routes_ref[...].astype(F32)))
    normed = normalize(first.astype(F32), gain_ref[...])
    write_blocks(normed, slots, expert, spread_ref, block_refs)


def last_kernel(group, x_ref, b0, b1, b2, b3, routes_ref, gates_ref, out_ref, spread_ref, done_ref, sems):
    chosen = block_map(slots_of(upright(routes_ref[...].astype(F32))), my_expert(group))
    gates = upright(gates_ref[...])
    fill([ref[...] for ref in (b0, b1, b2, b3)], spread_ref)
    width = x_ref.shape[1]
    copies = []
    for i in range(PARTS):
        span = slice(i * width // PARTS, (i + 1) * width // PARTS)
        done_ref[:, span] = residual(x_ref[:, span], gates, chosen, spread_ref, width, span.start)
        copies.append(
            pltpu.make_async_copy(done_ref.at[:, span], out_ref.at[:, span], sems.at[i])
        )
        copies[-1].start()
    for copy in copies:
        copy.wait()


def expert_kernel(given, w_gate, w_up, w_down, *refs):
    ins, outs, spread_ref = refs[:given], refs[given:-1], refs[-1]
    width = w_gate.shape[0]
    rows = spread_ref.shape[1] * LANES // width
    from_blocks([ref[...] for ref in ins], spread_ref)
    x = gathered(spread_ref, rows, width)
    gate_val = jnp.dot(x, w_gate[...], preferred_element_type=F32)
    up_val = jnp.dot(x, w_up[...], preferred_element_type=F32)
    hidden = (gate_val / (1.0 + jnp.exp(-gate_val)) * up_val).astype(BF16)
    for start in range(0, width, PIECE):
        piece = jnp.dot(hidden, w_down[:, start : start + PIECE], preferred_element_type=F32)
        spread(piece, spread_ref, width, start)
    to_blocks(spread_ref, outs)


def summed(refs):
    total = refs[0][...].astype(F32)
    for ref in refs[1:]:
        total = total + ref[...].astype(F32)
    return total.astype(BF16)


def sum_kernel(given, *refs):
    hand_out(summed(refs[:given]), refs[given:])


def carry_kernel(ahead_ref, *refs):
    ins, out_ref = refs[:-1], refs[-1]
    rows = ahead_ref.shape[0]
    out_ref[:rows] = ahead_ref[...]
    out_ref[rows:] = summed(ins)


def call(body, outs, ins, megabytes, scratch=(), flops=0, space=VMEM, out_space=VMEM):
    moved = sum(a.size * a.dtype.itemsize for a in (*ins, *outs))
    return pl.pallas_call(
        body,
        out_shape=outs,
        in_specs=[space] * len(ins),
        out_specs=[out_space] * len(outs),
        scratch_shapes=list(scratch),
        compiler_params=pltpu.CompilerParams(vmem_limit_bytes=megabytes << 20),
        cost_estimate=pl.CostEstimate(flops=flops, bytes_accessed=moved, transcendentals=0),
    )(*ins)


def on_device(tokens, gain, routes_1, gates_1, routes_2, gates_2, gate_proj, up_proj, down_proj):
    sections, devices = lax.axis_size("section"), lax.axis_size("expert")
    group = devices // EXPERTS
    rows, width = tokens.shape[1:]
    weights = (gate_proj[0, 0], up_proj[0, 0], down_proj[0, 0])
    tall, wide = block_shape(width)
    block = jax.ShapeDtypeStruct((tall, wide), BF16)
    packing = spread_scratch(pad_rows(EXPERTS * CAP), width)
    whole = jax.ShapeDtypeStruct((rows, width), BF16)
    ahead = (width // LANES + 1) * rows
    routes_1, gates_1, routes_2, gates_2 = (
        a.reshape(1, rows) for a in (routes_1, gates_1, routes_2, gates_2)
    )

    def to_expert(place):
        far = distance(place)
        return [(i, (i // group ^ far) * group + i % group) for i in range(devices)]

    def within(shift):
        return [(i, i // group * group + (i + shift) % group) for i in range(devices)]

    def onward(place):
        return [
            (s * devices + i, (s + 1) % sections * devices + j)
            for s in range(sections)
            for i, j in to_expert(place)
        ]

    def across(blocks):
        return [lax.ppermute(blocks[i], "expert", to_expert(i)) for i in range(EXPERTS - 1)]

    def shared(arrived):
        return arrived + [
            lax.ppermute(a, "expert", within(m)) for m in range(1, group) for a in arrived
        ]

    def experts(ins):
        count = sum(a.shape[0] for a in ins) // tall
        return call(
            functools.partial(expert_kernel, len(ins)),
            [jax.ShapeDtypeStruct((count // group * tall, wide), BF16)] * group,
            [*weights, *ins],
            24,
            [spread_scratch(pad_rows(count * CAP), width)],
            flops=6 * 256 * width * weights[0].shape[1],
        )

    def exchanged(sums):
        return [sums[0]] + [
            lax.ppermute(sums[m], "expert", within(-m)) for m in range(1, group)
        ]

    def added(terms):
        parts = terms[0].shape[0] // tall
        return call(
            functools.partial(sum_kernel, group), [block] * parts, terms, 8, flops=10**9
        )

    sources = [
        pltpu.with_memory_space_constraint(a, pltpu.HBM)
        for a in (tokens[0], gain, routes_1, gates_1)
    ]
    *blocks, travelling = call(
        functools.partial(pack_kernel, group),
        [block] * EXPERTS + [jax.ShapeDtypeStruct((ahead, LANES), BF16)],
        sources,
        8,
        [pltpu.VMEM(a.shape, a.dtype) for a in sources]
        + [packing, pltpu.SemaphoreType.DMA((len(sources),))],
        flops=10**10,
        space=HBM,
    )
    arrived = across(blocks[:-1])
    (carry,) = call(
        carry_kernel,
        [jax.ShapeDtypeStruct((ahead + tall, LANES), BF16)],
        [travelling, *exchanged(experts(shared(blocks[-1:])))],
        8,
    )
    *ins, carry = lax.optimization_barrier((*shared(arrived), carry))
    *sums, carry = lax.optimization_barrier((*experts(ins), carry))
    terms = exchanged(sums)
    carried = lax.ppermute(carry, "section", [(i, (i + 1) % sections) for i in range(sections)])
    sums = added(terms)
    home = [lax.ppermute(sums[i], ("section", "expert"), onward(i)) for i in range(EXPERTS - 1)]
    first, *blocks = call(
        functools.partial(middle_kernel, group),
        [whole] + [block] * EXPERTS,
        [*home, carried, gain, routes_2],
        8,
        [packing],
    )
    sums = added(exchanged(experts(shared(across(blocks[:-1]) + blocks[-1:]))))
    home = across(sums[:-1])
    (mixed,) = call(
        functools.partial(last_kernel, group),
        [whole],
        [first, *home, sums[-1], routes_2, gates_2],
        8,
        [packing, pltpu.VMEM((rows, width), BF16), pltpu.SemaphoreType.DMA((PARTS,))],
        out_space=HBM,
    )
    return mixed[None]


def solution(mesh):
    rows = P("section", "expert", None)
    slabs = P("section", "expert", None, None)
    return jax.shard_map(
        on_device,
        mesh=mesh,
        in_specs=(rows, P("section", None), rows, rows, rows, rows, slabs, slabs, slabs),
        out_specs=rows,
        check_vma=False,
    )
```

```python
import functools

import jax
import jax.numpy as jnp
from jax import lax
from jax.experimental import pallas as pl
from jax.experimental.pallas import tpu as pltpu
from jax.sharding import PartitionSpec as P

EXPERTS = 4
CAP = 5
ROWS = 16
LANES = 256
PIECE = 512
PARTS = 4
EPS = 1e-06
F32 = jnp.float32
BF16 = jnp.bfloat16
VMEM = pl.BlockSpec(memory_space=pltpu.VMEM)
HBM = pl.BlockSpec(memory_space=pltpu.HBM)


def distance(place):
    return place ^ (2 + (place >> 1))


def fifth(value):
    return (value * 205) >> 10


def pad_rows(count):
    return -(-count // ROWS) * ROWS


def block_shape(width):
    return CAP * width // LANES, LANES


def spread_scratch(rows, width):
    return pltpu.VMEM((LANES // 128, rows * width // LANES, 128), F32)


def spread(values, spread_ref, width, start=0):
    rows, columns = values.shape
    pieces = width // LANES
    for tile in range(columns // 128):
        piece, half = divmod(start // 128 + tile, LANES // 128)
        spread_ref[half, pl.ds(piece, rows, stride=pieces), :] = values[
            :, tile * 128 : (tile + 1) * 128
        ]


def gathered(spread_ref, rows, width, start=0, columns=None):
    pieces = width // LANES
    tiles = []
    for tile in range(start // 128, (start + (columns or width)) // 128):
        piece, half = divmod(tile, LANES // 128)
        tiles.append(spread_ref[half, pl.ds(piece, rows, stride=pieces), :].astype(BF16))
    return jnp.concatenate(tiles, axis=1)


def to_blocks(spread_ref, refs):
    start = 0
    for ref in refs:
        stop = start + ref.shape[0]
        for half in range(LANES // 128):
            ref[:, half * 128 : (half + 1) * 128] = spread_ref[half, start:stop, :].astype(BF16)
        start = stop


def from_blocks(arrays, spread_ref):
    start = 0
    for array in arrays:
        stop = start + array.shape[0]
        for half in range(LANES // 128):
            spread_ref[half, start:stop, :] = array[:, half * 128 : (half + 1) * 128].astype(F32)
        start = stop
    return start


def upright(row):
    rows = row.shape[1]
    same = lax.broadcasted_iota(jnp.int32, (rows, rows), 0) == lax.broadcasted_iota(
        jnp.int32, (rows, rows), 1
    )
    return jnp.sum(jnp.where(same, row, 0.0), axis=1, keepdims=True)


def slots_of(routes):
    rows = routes.shape[0]
    lanes = lax.broadcasted_iota(jnp.int32, (rows, 128), 1).astype(F32)
    one_hot = (routes == lanes).astype(F32)
    earlier = lax.broadcasted_iota(jnp.int32, (rows, rows), 0) > lax.broadcasted_iota(
        jnp.int32, (rows, rows), 1
    )
    before = jnp.dot(earlier.astype(BF16), one_hot.astype(BF16), preferred_element_type=F32)
    return routes * CAP + jnp.sum(before * one_hot, axis=1, keepdims=True)


def block_map(slots, expert):
    place = lax.broadcasted_iota(jnp.int32, (slots.shape[0], pad_rows(EXPERTS * CAP)), 1)
    block = fifth(place)
    target = (distance(block) ^ expert) * CAP + place - CAP * block
    target = jnp.where(block < EXPERTS, target, -1)
    return (slots == target.astype(F32)).astype(BF16)


def normalize(values, gain):
    inv_scale = lax.rsqrt(jnp.mean(values * values, axis=-1, keepdims=True) + EPS)
    return (values * inv_scale * gain).astype(BF16)


def write_blocks(normed, chosen, spread_ref, block_refs):
    packed = lax.dot_general(
        chosen, normed, (((0,), (0,)), ((), ())), preferred_element_type=F32
    )
    spread(packed, spread_ref, normed.shape[1])
    to_blocks(spread_ref, block_refs)


def hand_out(values, refs):
    start = 0
    for ref in refs:
        ref[...] = values[start : start + ref.shape[0]]
        start += ref.shape[0]


def my_expert(group):
    return lax.axis_index("expert") // group


def split_parts(values):
    parts = []
    for _ in range(3):
        parts.append(values.astype(BF16))
        values = values - parts[-1].astype(F32)
    return parts


def pack_kernel(group, *refs):
    sources, block_refs, ahead_ref = refs[:4], refs[4 : 4 + EXPERTS], refs[4 + EXPERTS]
    held, spread_ref, sems = refs[5 + EXPERTS : -2], refs[-2], refs[-1]
    copies = [
        pltpu.make_async_copy(source, place, sems.at[i])
        for i, (source, place) in enumerate(zip(sources, held))
    ]
    for copy in copies:
        copy.start()
    x_ref, gain_ref, routes_ref, gates_ref = held
    rows, width = x_ref.shape
    for copy in copies[2:]:
        copy.wait()
    slots = slots_of(upright(routes_ref[...].astype(F32)))
    lane = lax.broadcasted_iota(jnp.int32, (rows, LANES), 1)
    meta = jnp.zeros((rows, LANES), F32)
    for i, column in enumerate([slots, *split_parts(upright(gates_ref[...]))]):
        meta = jnp.where(lane == i, column.astype(F32), meta)
    chosen = block_map(slots, my_expert(group))
    for copy in copies[:2]:
        copy.wait()
    for piece in range(width // LANES):
        ahead_ref[piece * rows : (piece + 1) * rows] = x_ref[:, piece * LANES : (piece + 1) * LANES]
    ahead_ref[width // LANES * rows :] = meta.astype(BF16)
    normed = normalize(x_ref[...].astype(F32), gain_ref[...])
    write_blocks(normed, chosen, spread_ref, block_refs)


def fill(blocks, spread_ref):
    filled = from_blocks(blocks, spread_ref)
    spread_ref[:, filled:, :] = jnp.zeros(
        (spread_ref.shape[0], spread_ref.shape[1] - filled, 128), F32
    )


def residual(x, gates, chosen, spread_ref, width, start=0):
    found = jnp.dot(
        chosen,
        gathered(spread_ref, chosen.shape[1], width, start, x.shape[1]),
        preferred_element_type=F32,
    )
    update = (gates * found).astype(BF16)
    return (x.astype(F32) + update.astype(F32)).astype(BF16)


def middle_kernel(group, *refs):
    block_ins, carried_ref, gain_ref, map_ref = refs[: EXPERTS - 1], *refs[EXPERTS - 1 : EXPERTS + 2]
    first_ref, block_refs, spread_ref = refs[EXPERTS + 2], refs[EXPERTS + 3 : -1], refs[-1]
    expert = my_expert(group)
    rows, width = first_ref.shape
    pieces = width // LANES
    x = jnp.concatenate(
        [carried_ref[piece * rows : (piece + 1) * rows] for piece in range(pieces)], axis=1
    )
    meta = carried_ref[pieces * rows : (pieces + 1) * rows].astype(F32)
    gates = meta[:, 1:2] + meta[:, 2:3] + meta[:, 3:4]
    blocks = [ref[...] for ref in block_ins] + [carried_ref[(pieces + 1) * rows :]]
    fill(blocks, spread_ref)
    first = residual(x, gates, block_map(meta[:, 0:1], expert), spread_ref, width)
    first_ref[...] = first
    normed = normalize(first.astype(F32), gain_ref[...])
    write_blocks(normed, map_ref[...], spread_ref, block_refs)


def last_kernel(x_ref, b0, b1, b2, b3, map_ref, gates_ref, out_ref, spread_ref, done_ref, sems):
    chosen = map_ref[...]
    gates = gates_ref[:, 0:1]
    fill([ref[...] for ref in (b0, b1, b2, b3)], spread_ref)
    width = x_ref.shape[1]
    copies = []
    for i in range(PARTS):
        span = slice(i * width // PARTS, (i + 1) * width // PARTS)
        done_ref[:, span] = residual(x_ref[:, span], gates, chosen, spread_ref, width, span.start)
        copies.append(
            pltpu.make_async_copy(done_ref.at[:, span], out_ref.at[:, span], sems.at[i])
        )
        copies[-1].start()
    for copy in copies:
        copy.wait()


def expert_kernel(given, w_gate, w_up, w_down, *refs):
    ins, outs, spread_ref = refs[:given], refs[given:-1], refs[-1]
    width = w_gate.shape[0]
    rows = spread_ref.shape[1] * LANES // width
    from_blocks([ref[...] for ref in ins], spread_ref)
    x = gathered(spread_ref, rows, width)
    gate_val = jnp.dot(x, w_gate[...], preferred_element_type=F32)
    up_val = jnp.dot(x, w_up[...], preferred_element_type=F32)
    hidden = (gate_val / (1.0 + jnp.exp(-gate_val)) * up_val).astype(BF16)
    for start in range(0, width, PIECE):
        piece = jnp.dot(hidden, w_down[:, start : start + PIECE], preferred_element_type=F32)
        spread(piece, spread_ref, width, start)
    to_blocks(spread_ref, outs)


def summed(refs):
    total = refs[0][...].astype(F32)
    for ref in refs[1:]:
        total = total + ref[...].astype(F32)
    return total.astype(BF16)


def sum_kernel(given, *refs):
    hand_out(summed(refs[:given]), refs[given:])


def carry_kernel(group, routes_ref, gates_ref, ahead_ref, *refs):
    ins, (out_ref, map_ref, column_ref) = refs[:-3], refs[-3:]
    rows = ahead_ref.shape[0]
    out_ref[:rows] = ahead_ref[...]
    out_ref[rows:] = summed(ins)
    slots = slots_of(upright(routes_ref[...].astype(F32)))
    map_ref[...] = block_map(slots, my_expert(group))
    column_ref[...] = jnp.broadcast_to(upright(gates_ref[...]), column_ref.shape)


def call(body, outs, ins, megabytes, scratch=(), flops=0, space=VMEM, out_space=VMEM):
    moved = sum(a.size * a.dtype.itemsize for a in (*ins, *outs))
    return pl.pallas_call(
        body,
        out_shape=outs,
        in_specs=[space] * len(ins),
        out_specs=[out_space] * len(outs),
        scratch_shapes=list(scratch),
        compiler_params=pltpu.CompilerParams(vmem_limit_bytes=megabytes << 20),
        cost_estimate=pl.CostEstimate(flops=flops, bytes_accessed=moved, transcendentals=0),
    )(*ins)


def on_device(tokens, gain, routes_1, gates_1, routes_2, gates_2, gate_proj, up_proj, down_proj):
    sections, devices = lax.axis_size("section"), lax.axis_size("expert")
    group = devices // EXPERTS
    rows, width = tokens.shape[1:]
    weights = (gate_proj[0, 0], up_proj[0, 0], down_proj[0, 0])
    tall, wide = block_shape(width)
    block = jax.ShapeDtypeStruct((tall, wide), BF16)
    packing = spread_scratch(pad_rows(EXPERTS * CAP), width)
    whole = jax.ShapeDtypeStruct((rows, width), BF16)
    ahead = (width // LANES + 1) * rows
    routes_1, gates_1, routes_2, gates_2 = (
        a.reshape(1, rows) for a in (routes_1, gates_1, routes_2, gates_2)
    )

    def to_expert(place):
        far = distance(place)
        return [(i, (i // group ^ far) * group + i % group) for i in range(devices)]

    def within(shift):
        return [(i, i // group * group + (i + shift) % group) for i in range(devices)]

    def onward(place):
        return [
            (s * devices + i, (s + 1) % sections * devices + j)
            for s in range(sections)
            for i, j in to_expert(place)
        ]

    def across(blocks):
        return [lax.ppermute(blocks[i], "expert", to_expert(i)) for i in range(EXPERTS - 1)]

    def shared(arrived):
        return arrived + [
            lax.ppermute(a, "expert", within(m)) for m in range(1, group) for a in arrived
        ]

    def experts(ins):
        count = sum(a.shape[0] for a in ins) // tall
        return call(
            functools.partial(expert_kernel, len(ins)),
            [jax.ShapeDtypeStruct((count // group * tall, wide), BF16)] * group,
            [*weights, *ins],
            24,
            [spread_scratch(pad_rows(count * CAP), width)],
            flops=6 * 256 * width * weights[0].shape[1],
        )

    def exchanged(sums):
        return [sums[0]] + [
            lax.ppermute(sums[m], "expert", within(-m)) for m in range(1, group)
        ]

    def added(terms):
        parts = terms[0].shape[0] // tall
        return call(
            functools.partial(sum_kernel, group), [block] * parts, terms, 8, flops=10**9
        )

    sources = [
        pltpu.with_memory_space_constraint(a, pltpu.HBM)
        for a in (tokens[0], gain, routes_1, gates_1)
    ]
    *blocks, travelling = call(
        functools.partial(pack_kernel, group),
        [block] * EXPERTS + [jax.ShapeDtypeStruct((ahead, LANES), BF16)],
        sources,
        8,
        [pltpu.VMEM(a.shape, a.dtype) for a in sources]
        + [packing, pltpu.SemaphoreType.DMA((len(sources),))],
        flops=10**10,
        space=HBM,
    )
    arrived = across(blocks[:-1])
    carry, second_map, second_gates = call(
        functools.partial(carry_kernel, group),
        [
            jax.ShapeDtypeStruct((ahead + tall, LANES), BF16),
            jax.ShapeDtypeStruct((rows, pad_rows(EXPERTS * CAP)), BF16),
            jax.ShapeDtypeStruct((rows, 128), F32),
        ],
        [routes_2, gates_2, travelling, *exchanged(experts(shared(blocks[-1:])))],
        8,
    )
    *ins, carry = lax.optimization_barrier((*shared(arrived), carry))
    *sums, carry = lax.optimization_barrier((*experts(ins), carry))
    terms = exchanged(sums)
    carried = lax.ppermute(carry, "section", [(i, (i + 1) % sections) for i in range(sections)])
    sums = added(terms)
    home = [lax.ppermute(sums[i], ("section", "expert"), onward(i)) for i in range(EXPERTS - 1)]
    first, *blocks = call(
        functools.partial(middle_kernel, group),
        [whole] + [block] * EXPERTS,
        [*home, carried, gain, second_map],
        8,
        [packing],
    )
    sums = added(exchanged(experts(shared(across(blocks[:-1]) + blocks[-1:]))))
    home = across(sums[:-1])
    (mixed,) = call(
        last_kernel,
        [whole],
        [first, *home, sums[-1], second_map, second_gates],
        8,
        [packing, pltpu.VMEM((rows, width), BF16), pltpu.SemaphoreType.DMA((PARTS,))],
        out_space=HBM,
    )
    return mixed[None]


def solution(mesh):
    rows = P("section", "expert", None)
    slabs = P("section", "expert", None, None)
    return jax.shard_map(
        on_device,
        mesh=mesh,
        in_specs=(rows, P("section", None), rows, rows, rows, rows, slabs, slabs, slabs),
        out_specs=rows,
        check_vma=False,
    )
```

```python
import functools

import jax
import jax.numpy as jnp
from jax import lax
from jax.experimental import pallas as pl
from jax.experimental.pallas import tpu as pltpu
from jax.sharding import PartitionSpec as P

EXPERTS = 4
CAP = 5
ROWS = 16
LANES = 256
PIECE = 512
PARTS = 4
EPS = 1e-06
F32 = jnp.float32
BF16 = jnp.bfloat16
VMEM = pl.BlockSpec(memory_space=pltpu.VMEM)
HBM = pl.BlockSpec(memory_space=pltpu.HBM)


def distance(place):
    return place ^ (2 + (place >> 1))


def fifth(value):
    return (value * 205) >> 10


def pad_rows(count):
    return -(-count // ROWS) * ROWS


def block_shape(width):
    return CAP * width // LANES, LANES


def spread_scratch(rows, width):
    return pltpu.VMEM((LANES // 128, rows * width // LANES, 128), F32)


def spread(values, spread_ref, width, start=0):
    rows, columns = values.shape
    pieces = width // LANES
    for tile in range(columns // 128):
        piece, half = divmod(start // 128 + tile, LANES // 128)
        spread_ref[half, pl.ds(piece, rows, stride=pieces), :] = values[
            :, tile * 128 : (tile + 1) * 128
        ]


def gathered(spread_ref, rows, width, start=0, columns=None):
    pieces = width // LANES
    tiles = []
    for tile in range(start // 128, (start + (columns or width)) // 128):
        piece, half = divmod(tile, LANES // 128)
        tiles.append(spread_ref[half, pl.ds(piece, rows, stride=pieces), :].astype(BF16))
    return jnp.concatenate(tiles, axis=1)


def to_blocks(spread_ref, refs):
    start = 0
    for ref in refs:
        stop = start + ref.shape[0]
        for half in range(LANES // 128):
            ref[:, half * 128 : (half + 1) * 128] = spread_ref[half, start:stop, :].astype(BF16)
        start = stop


def from_blocks(arrays, spread_ref):
    start = 0
    for array in arrays:
        stop = start + array.shape[0]
        for half in range(LANES // 128):
            spread_ref[half, start:stop, :] = array[:, half * 128 : (half + 1) * 128].astype(F32)
        start = stop
    return start


def upright(row):
    rows = row.shape[1]
    same = lax.broadcasted_iota(jnp.int32, (rows, rows), 0) == lax.broadcasted_iota(
        jnp.int32, (rows, rows), 1
    )
    return jnp.sum(jnp.where(same, row, 0.0), axis=1, keepdims=True)


def slots_of(routes):
    rows = routes.shape[0]
    lanes = lax.broadcasted_iota(jnp.int32, (rows, 128), 1).astype(F32)
    one_hot = (routes == lanes).astype(F32)
    earlier = lax.broadcasted_iota(jnp.int32, (rows, rows), 0) > lax.broadcasted_iota(
        jnp.int32, (rows, rows), 1
    )
    before = jnp.dot(earlier.astype(BF16), one_hot.astype(BF16), preferred_element_type=F32)
    return routes * CAP + jnp.sum(before * one_hot, axis=1, keepdims=True)


def block_map(slots, expert):
    place = lax.broadcasted_iota(jnp.int32, (slots.shape[0], pad_rows(EXPERTS * CAP)), 1)
    block = fifth(place)
    target = (distance(block) ^ expert) * CAP + place - CAP * block
    target = jnp.where(block < EXPERTS, target, -1)
    return (slots == target.astype(F32)).astype(BF16)


def normalize(values, gain):
    inv_scale = lax.rsqrt(jnp.mean(values * values, axis=-1, keepdims=True) + EPS)
    return (values * inv_scale * gain).astype(BF16)


def write_blocks(normed, chosen, spread_ref, block_refs):
    packed = lax.dot_general(
        chosen, normed, (((0,), (0,)), ((), ())), preferred_element_type=F32
    )
    spread(packed, spread_ref, normed.shape[1])
    to_blocks(spread_ref, block_refs)


def hand_out(values, refs):
    start = 0
    for ref in refs:
        ref[...] = values[start : start + ref.shape[0]]
        start += ref.shape[0]


def my_expert(group):
    return lax.axis_index("expert") // group


def split_parts(values):
    parts = []
    for _ in range(3):
        parts.append(values.astype(BF16))
        values = values - parts[-1].astype(F32)
    return parts


def pack_kernel(group, *refs):
    sources, block_refs, ahead_ref = refs[:4], refs[4 : 4 + EXPERTS], refs[4 + EXPERTS]
    held, spread_ref, sems = refs[5 + EXPERTS : -2], refs[-2], refs[-1]
    copies = [
        pltpu.make_async_copy(source, place, sems.at[i])
        for i, (source, place) in enumerate(zip(sources, held))
    ]
    for copy in copies:
        copy.start()
    x_ref, gain_ref, routes_ref, gates_ref = held
    rows, width = x_ref.shape
    for copy in copies[2:]:
        copy.wait()
    slots = slots_of(upright(routes_ref[...].astype(F32)))
    lane = lax.broadcasted_iota(jnp.int32, (rows, LANES), 1)
    meta = jnp.zeros((rows, LANES), F32)
    for i, column in enumerate([slots, *split_parts(upright(gates_ref[...]))]):
        meta = jnp.where(lane == i, column.astype(F32), meta)
    chosen = block_map(slots, my_expert(group))
    for copy in copies[:2]:
        copy.wait()
    for piece in range(width // LANES):
        ahead_ref[piece * rows : (piece + 1) * rows] = x_ref[:, piece * LANES : (piece + 1) * LANES]
    ahead_ref[width // LANES * rows :] = meta.astype(BF16)
    normed = normalize(x_ref[...].astype(F32), gain_ref[...])
    write_blocks(normed, chosen, spread_ref, block_refs)


def fill(blocks, spread_ref):
    filled = from_blocks(blocks, spread_ref)
    spread_ref[:, filled:, :] = jnp.zeros(
        (spread_ref.shape[0], spread_ref.shape[1] - filled, 128), F32
    )


def residual(x, gates, chosen, spread_ref, width, start=0):
    found = jnp.dot(
        chosen,
        gathered(spread_ref, chosen.shape[1], width, start, x.shape[1]),
        preferred_element_type=F32,
    )
    update = (gates * found).astype(BF16)
    return (x.astype(F32) + update.astype(F32)).astype(BF16)


def middle_kernel(group, *refs):
    block_ins, carried_ref, gain_ref, map_ref = refs[: EXPERTS - 1], *refs[EXPERTS - 1 : EXPERTS + 2]
    first_ref, block_refs, spread_ref = refs[EXPERTS + 2], refs[EXPERTS + 3 : -1], refs[-1]
    expert = my_expert(group)
    rows, width = first_ref.shape
    pieces = width // LANES
    x = jnp.concatenate(
        [carried_ref[piece * rows : (piece + 1) * rows] for piece in range(pieces)], axis=1
    )
    meta = carried_ref[pieces * rows : (pieces + 1) * rows].astype(F32)
    gates = meta[:, 1:2] + meta[:, 2:3] + meta[:, 3:4]
    blocks = [ref[...] for ref in block_ins] + [carried_ref[(pieces + 1) * rows :]]
    fill(blocks, spread_ref)
    first = residual(x, gates, block_map(meta[:, 0:1], expert), spread_ref, width)
    first_ref[...] = first
    normed = normalize(first.astype(F32), gain_ref[...])
    write_blocks(normed, map_ref[...], spread_ref, block_refs)


def last_kernel(x_ref, b0, b1, b2, b3, map_ref, gates_ref, out_ref, spread_ref, done_ref, sems):
    chosen = map_ref[...]
    gates = gates_ref[:, 0:1]
    fill([ref[...] for ref in (b0, b1, b2, b3)], spread_ref)
    width = x_ref.shape[1]
    copies = []
    for i in range(PARTS):
        span = slice(i * width // PARTS, (i + 1) * width // PARTS)
        done_ref[:, span] = residual(x_ref[:, span], gates, chosen, spread_ref, width, span.start)
        copies.append(
            pltpu.make_async_copy(done_ref.at[:, span], out_ref.at[:, span], sems.at[i])
        )
        copies[-1].start()
    for copy in copies:
        copy.wait()


def expert_kernel(given, w_gate, w_up, w_down, *refs):
    ins, outs, spread_ref = refs[:given], refs[given:-1], refs[-1]
    width = w_gate.shape[0]
    rows = spread_ref.shape[1] * LANES // width
    from_blocks([ref[...] for ref in ins], spread_ref)
    x = gathered(spread_ref, rows, width)
    gate_val = jnp.dot(x, w_gate[...], preferred_element_type=F32)
    up_val = jnp.dot(x, w_up[...], preferred_element_type=F32)
    hidden = (gate_val / (1.0 + jnp.exp(-gate_val)) * up_val).astype(BF16)
    for start in range(0, width, PIECE):
        piece = jnp.dot(hidden, w_down[:, start : start + PIECE], preferred_element_type=F32)
        spread(piece, spread_ref, width, start)
    to_blocks(spread_ref, outs)


def summed(refs):
    total = refs[0][...].astype(F32)
    for ref in refs[1:]:
        total = total + ref[...].astype(F32)
    return total.astype(BF16)


def sum_kernel(given, *refs):
    hand_out(summed(refs[:given]), refs[given:])


def carry_kernel(group, routes_ref, gates_ref, ahead_ref, *refs):
    ins, (out_ref, map_ref, column_ref) = refs[:-3], refs[-3:]
    rows = ahead_ref.shape[0]
    out_ref[:rows] = ahead_ref[...]
    out_ref[rows:] = summed(ins)
    slots = slots_of(upright(routes_ref[...].astype(F32)))
    map_ref[...] = block_map(slots, my_expert(group))
    column_ref[...] = jnp.broadcast_to(upright(gates_ref[...]), column_ref.shape)


def call(body, outs, ins, megabytes, scratch=(), flops=0, space=VMEM, out_space=VMEM):
    moved = sum(a.size * a.dtype.itemsize for a in (*ins, *outs))
    return pl.pallas_call(
        body,
        out_shape=outs,
        in_specs=[space] * len(ins),
        out_specs=[out_space] * len(outs),
        scratch_shapes=list(scratch),
        compiler_params=pltpu.CompilerParams(vmem_limit_bytes=megabytes << 20),
        cost_estimate=pl.CostEstimate(flops=flops, bytes_accessed=moved, transcendentals=0),
    )(*ins)


def on_device(tokens, gain, routes_1, gates_1, routes_2, gates_2, gate_proj, up_proj, down_proj):
    sections, devices = lax.axis_size("section"), lax.axis_size("expert")
    group = devices // EXPERTS
    rows, width = tokens.shape[1:]
    weights = (gate_proj[0, 0], up_proj[0, 0], down_proj[0, 0])
    tall, wide = block_shape(width)
    block = jax.ShapeDtypeStruct((tall, wide), BF16)
    packing = spread_scratch(pad_rows(EXPERTS * CAP), width)
    whole = jax.ShapeDtypeStruct((rows, width), BF16)
    ahead = (width // LANES + 1) * rows
    routes_1, gates_1, routes_2, gates_2 = (
        a.reshape(1, rows) for a in (routes_1, gates_1, routes_2, gates_2)
    )

    def to_expert(place):
        far = distance(place)
        return [(i, (i // group ^ far) * group + i % group) for i in range(devices)]

    def within(shift):
        return [(i, i // group * group + (i + shift) % group) for i in range(devices)]

    def onward(place):
        return [
            (s * devices + i, (s + 1) % sections * devices + j)
            for s in range(sections)
            for i, j in to_expert(place)
        ]

    def across(blocks, order=(0, 1, 2)):
        sent = {i: lax.ppermute(blocks[i], "expert", to_expert(i)) for i in order}
        return [sent[i] for i in range(EXPERTS - 1)]

    def swapped(parts):
        return [parts[0], parts[2], parts[1], *parts[3:]]

    def shared(arrived):
        return arrived + [
            lax.ppermute(a, "expert", within(m)) for m in range(1, group) for a in arrived
        ]

    def experts(ins):
        count = sum(a.shape[0] for a in ins) // tall
        return call(
            functools.partial(expert_kernel, len(ins)),
            [jax.ShapeDtypeStruct((count // group * tall, wide), BF16)] * group,
            [*weights, *ins],
            24,
            [spread_scratch(pad_rows(count * CAP), width)],
            flops=6 * 256 * width * weights[0].shape[1],
        )

    def exchanged(sums):
        return [sums[0]] + [
            lax.ppermute(sums[m], "expert", within(-m)) for m in range(1, group)
        ]

    def added(terms):
        parts = terms[0].shape[0] // tall
        return call(
            functools.partial(sum_kernel, group), [block] * parts, terms, 8, flops=10**9
        )

    sources = [
        pltpu.with_memory_space_constraint(a, pltpu.HBM)
        for a in (tokens[0], gain, routes_1, gates_1)
    ]
    *blocks, travelling = call(
        functools.partial(pack_kernel, group),
        [block] * EXPERTS + [jax.ShapeDtypeStruct((ahead, LANES), BF16)],
        sources,
        8,
        [pltpu.VMEM(a.shape, a.dtype) for a in sources]
        + [packing, pltpu.SemaphoreType.DMA((len(sources),))],
        flops=10**10,
        space=HBM,
    )
    arrived = swapped(across(blocks, (0, 2, 1)))
    carry, second_map, second_gates = call(
        functools.partial(carry_kernel, group),
        [
            jax.ShapeDtypeStruct((ahead + tall, LANES), BF16),
            jax.ShapeDtypeStruct((rows, pad_rows(EXPERTS * CAP)), BF16),
            jax.ShapeDtypeStruct((rows, 128), F32),
        ],
        [routes_2, gates_2, travelling, *exchanged(experts(shared(blocks[-1:])))],
        8,
    )
    *ins, carry = lax.optimization_barrier((*shared(arrived), carry))
    *sums, carry = lax.optimization_barrier((*experts(ins), carry))
    terms = exchanged(sums)
    carried = lax.ppermute(carry, "section", [(i, (i + 1) % sections) for i in range(sections)])
    sums = swapped(added(terms))
    home = [lax.ppermute(sums[i], ("section", "expert"), onward(i)) for i in range(EXPERTS - 1)]
    first, *blocks = call(
        functools.partial(middle_kernel, group),
        [whole] + [block] * EXPERTS,
        [*home, carried, gain, second_map],
        8,
        [packing],
    )
    ins = shared(swapped(across(blocks, (0, 2, 1)) + blocks[-1:]))
    sums = swapped(added(exchanged(experts(ins))))
    home = across(sums)
    (mixed,) = call(
        last_kernel,
        [whole],
        [first, *home, sums[-1], second_map, second_gates],
        8,
        [packing, pltpu.VMEM((rows, width), BF16), pltpu.SemaphoreType.DMA((PARTS,))],
        out_space=HBM,
    )
    return mixed[None]


def solution(mesh):
    rows = P("section", "expert", None)
    slabs = P("section", "expert", None, None)
    return jax.shard_map(
        on_device,
        mesh=mesh,
        in_specs=(rows, P("section", None), rows, rows, rows, rows, slabs, slabs, slabs),
        out_specs=rows,
        check_vma=False,
    )
```

```python
import functools

import jax
import jax.numpy as jnp
from jax import lax
from jax.experimental import pallas as pl
from jax.experimental.pallas import tpu as pltpu
from jax.sharding import PartitionSpec as P

EXPERTS = 4
CAP = 5
ROWS = 16
LANES = 256
PIECE = 512
PARTS = 4
LATER = 10**9
EPS = 1e-06
F32 = jnp.float32
BF16 = jnp.bfloat16
VMEM = pl.BlockSpec(memory_space=pltpu.VMEM)
HBM = pl.BlockSpec(memory_space=pltpu.HBM)


def distance(place):
    return place ^ (2 + (place >> 1))


def fifth(value):
    return (value * 205) >> 10


def pad_rows(count):
    return -(-count // ROWS) * ROWS


def block_shape(width):
    return CAP * width // LANES, LANES


def spread_scratch(rows, width):
    return pltpu.VMEM((LANES // 128, rows * width // LANES, 128), F32)


def spread(values, spread_ref, width, start=0):
    rows, columns = values.shape
    pieces = width // LANES
    for tile in range(columns // 128):
        piece, half = divmod(start // 128 + tile, LANES // 128)
        spread_ref[half, pl.ds(piece, rows, stride=pieces), :] = values[
            :, tile * 128 : (tile + 1) * 128
        ]


def gathered(spread_ref, rows, width, start=0, columns=None):
    pieces = width // LANES
    tiles = []
    for tile in range(start // 128, (start + (columns or width)) // 128):
        piece, half = divmod(tile, LANES // 128)
        tiles.append(spread_ref[half, pl.ds(piece, rows, stride=pieces), :].astype(BF16))
    return jnp.concatenate(tiles, axis=1)


def to_blocks(spread_ref, refs):
    start = 0
    for ref in refs:
        stop = start + ref.shape[0]
        for half in range(LANES // 128):
            ref[:, half * 128 : (half + 1) * 128] = spread_ref[half, start:stop, :].astype(BF16)
        start = stop


def from_blocks(arrays, spread_ref):
    start = 0
    for array in arrays:
        stop = start + array.shape[0]
        for half in range(LANES // 128):
            spread_ref[half, start:stop, :] = array[:, half * 128 : (half + 1) * 128].astype(F32)
        start = stop
    return start


def upright(row):
    rows = row.shape[1]
    same = lax.broadcasted_iota(jnp.int32, (rows, rows), 0) == lax.broadcasted_iota(
        jnp.int32, (rows, rows), 1
    )
    return jnp.sum(jnp.where(same, row, 0.0), axis=1, keepdims=True)


def slots_of(routes):
    rows = routes.shape[0]
    lanes = lax.broadcasted_iota(jnp.int32, (rows, 128), 1).astype(F32)
    one_hot = (routes == lanes).astype(F32)
    earlier = lax.broadcasted_iota(jnp.int32, (rows, rows), 0) > lax.broadcasted_iota(
        jnp.int32, (rows, rows), 1
    )
    before = jnp.dot(earlier.astype(BF16), one_hot.astype(BF16), preferred_element_type=F32)
    return routes * CAP + jnp.sum(before * one_hot, axis=1, keepdims=True)


def block_map(slots, expert):
    place = lax.broadcasted_iota(jnp.int32, (slots.shape[0], pad_rows(EXPERTS * CAP)), 1)
    block = fifth(place)
    target = (distance(block) ^ expert) * CAP + place - CAP * block
    target = jnp.where(block < EXPERTS, target, -1)
    return (slots == target.astype(F32)).astype(BF16)


def normalize(values, gain):
    inv_scale = lax.rsqrt(jnp.mean(values * values, axis=-1, keepdims=True) + EPS)
    return (values * inv_scale * gain).astype(BF16)


def write_blocks(normed, chosen, spread_ref, block_refs):
    packed = lax.dot_general(
        chosen, normed, (((0,), (0,)), ((), ())), preferred_element_type=F32
    )
    spread(packed, spread_ref, normed.shape[1])
    to_blocks(spread_ref, block_refs)


def hand_out(values, refs):
    start = 0
    for ref in refs:
        ref[...] = values[start : start + ref.shape[0]]
        start += ref.shape[0]


def my_expert(group):
    return lax.axis_index("expert") // group


def split_parts(values):
    parts = []
    for _ in range(3):
        parts.append(values.astype(BF16))
        values = values - parts[-1].astype(F32)
    return parts


def pack_kernel(group, *refs):
    sources, block_refs, ahead_ref = refs[:4], refs[4 : 4 + EXPERTS], refs[4 + EXPERTS]
    held, spread_ref, sems = refs[5 + EXPERTS : -2], refs[-2], refs[-1]
    copies = [
        pltpu.make_async_copy(source, place, sems.at[i])
        for i, (source, place) in enumerate(zip(sources, held))
    ]
    for copy in copies:
        copy.start()
    x_ref, gain_ref, routes_ref, gates_ref = held
    rows, width = x_ref.shape
    for copy in copies[2:]:
        copy.wait()
    slots = slots_of(upright(routes_ref[...].astype(F32)))
    lane = lax.broadcasted_iota(jnp.int32, (rows, LANES), 1)
    meta = jnp.zeros((rows, LANES), F32)
    for i, column in enumerate([slots, *split_parts(upright(gates_ref[...]))]):
        meta = jnp.where(lane == i, column.astype(F32), meta)
    chosen = block_map(slots, my_expert(group))
    for copy in copies[:2]:
        copy.wait()
    for piece in range(width // LANES):
        ahead_ref[piece * rows : (piece + 1) * rows] = x_ref[:, piece * LANES : (piece + 1) * LANES]
    ahead_ref[width // LANES * rows :] = meta.astype(BF16)
    normed = normalize(x_ref[...].astype(F32), gain_ref[...])
    write_blocks(normed, chosen, spread_ref, block_refs)


def fill(blocks, spread_ref):
    filled = from_blocks(blocks, spread_ref)
    spread_ref[:, filled:, :] = jnp.zeros(
        (spread_ref.shape[0], spread_ref.shape[1] - filled, 128), F32
    )


def residual(x, gates, chosen, spread_ref, width, start=0):
    found = jnp.dot(
        chosen,
        gathered(spread_ref, chosen.shape[1], width, start, x.shape[1]),
        preferred_element_type=F32,
    )
    update = (gates * found).astype(BF16)
    return (x.astype(F32) + update.astype(F32)).astype(BF16)


def middle_kernel(group, *refs):
    block_ins, carried_ref, gain_ref, map_ref = refs[: EXPERTS - 1], *refs[EXPERTS - 1 : EXPERTS + 2]
    first_ref, block_refs, spread_ref = refs[EXPERTS + 2], refs[EXPERTS + 3 : -1], refs[-1]
    expert = my_expert(group)
    rows, width = first_ref.shape
    pieces = width // LANES
    x = jnp.concatenate(
        [carried_ref[piece * rows : (piece + 1) * rows] for piece in range(pieces)], axis=1
    )
    meta = carried_ref[pieces * rows : (pieces + 1) * rows].astype(F32)
    gates = meta[:, 1:2] + meta[:, 2:3] + meta[:, 3:4]
    blocks = [ref[...] for ref in block_ins] + [carried_ref[(pieces + 1) * rows :]]
    fill(blocks, spread_ref)
    first = residual(x, gates, block_map(meta[:, 0:1], expert), spread_ref, width)
    first_ref[...] = first
    normed = normalize(first.astype(F32), gain_ref[...])
    write_blocks(normed, map_ref[...], spread_ref, block_refs)


def last_kernel(x_ref, b0, b1, b2, b3, map_ref, gates_ref, out_ref, spread_ref, done_ref, sems):
    chosen = map_ref[...]
    gates = gates_ref[:, 0:1]
    fill([ref[...] for ref in (b0, b1, b2, b3)], spread_ref)
    width = x_ref.shape[1]
    copies = []
    for i in range(PARTS):
        span = slice(i * width // PARTS, (i + 1) * width // PARTS)
        done_ref[:, span] = residual(x_ref[:, span], gates, chosen, spread_ref, width, span.start)
        copies.append(
            pltpu.make_async_copy(done_ref.at[:, span], out_ref.at[:, span], sems.at[i])
        )
        copies[-1].start()
    for copy in copies:
        copy.wait()


def expert_kernel(given, w_gate, w_up, w_down, *refs):
    ins, outs, spread_ref = refs[:given], refs[given:-1], refs[-1]
    width = w_gate.shape[0]
    rows = spread_ref.shape[1] * LANES // width
    from_blocks([ref[...] for ref in ins], spread_ref)
    x = gathered(spread_ref, rows, width)
    gate_val = jnp.dot(x, w_gate[...], preferred_element_type=F32)
    up_val = jnp.dot(x, w_up[...], preferred_element_type=F32)
    hidden = (gate_val / (1.0 + jnp.exp(-gate_val)) * up_val).astype(BF16)
    for start in range(0, width, PIECE):
        piece = jnp.dot(hidden, w_down[:, start : start + PIECE], preferred_element_type=F32)
        spread(piece, spread_ref, width, start)
    to_blocks(spread_ref, outs)


def summed(refs):
    total = refs[0][...].astype(F32)
    for ref in refs[1:]:
        total = total + ref[...].astype(F32)
    return total.astype(BF16)


def sum_kernel(given, *refs):
    hand_out(summed(refs[:given]), refs[given:])


def later_kernel(group, routes_ref, gates_ref, map_ref, column_ref):
    slots = slots_of(upright(routes_ref[...].astype(F32)))
    map_ref[...] = block_map(slots, my_expert(group))
    column_ref[...] = jnp.broadcast_to(upright(gates_ref[...]), column_ref.shape)


def carry_kernel(ahead_ref, *refs):
    ins, out_ref = refs[:-1], refs[-1]
    rows = ahead_ref.shape[0]
    out_ref[:rows] = ahead_ref[...]
    out_ref[rows:] = summed(ins)


def call(body, outs, ins, megabytes, scratch=(), flops=0, space=VMEM, out_space=VMEM):
    moved = sum(a.size * a.dtype.itemsize for a in (*ins, *outs))
    return pl.pallas_call(
        body,
        out_shape=outs,
        in_specs=[space] * len(ins),
        out_specs=[out_space] * len(outs),
        scratch_shapes=list(scratch),
        compiler_params=pltpu.CompilerParams(vmem_limit_bytes=megabytes << 20),
        cost_estimate=pl.CostEstimate(flops=flops, bytes_accessed=moved, transcendentals=0),
    )(*ins)


def on_device(tokens, gain, routes_1, gates_1, routes_2, gates_2, gate_proj, up_proj, down_proj):
    sections, devices = lax.axis_size("section"), lax.axis_size("expert")
    group = devices // EXPERTS
    rows, width = tokens.shape[1:]
    weights = (gate_proj[0, 0], up_proj[0, 0], down_proj[0, 0])
    tall, wide = block_shape(width)
    block = jax.ShapeDtypeStruct((tall, wide), BF16)
    packing = spread_scratch(pad_rows(EXPERTS * CAP), width)
    whole = jax.ShapeDtypeStruct((rows, width), BF16)
    ahead = (width // LANES + 1) * rows
    routes_1, gates_1, routes_2, gates_2 = (
        a.reshape(1, rows) for a in (routes_1, gates_1, routes_2, gates_2)
    )

    def to_expert(place):
        far = distance(place)
        return [(i, (i // group ^ far) * group + i % group) for i in range(devices)]

    def within(shift):
        return [(i, i // group * group + (i + shift) % group) for i in range(devices)]

    def onward(place):
        return [
            (s * devices + i, (s + 1) % sections * devices + j)
            for s in range(sections)
            for i, j in to_expert(place)
        ]

    def across(blocks):
        return [lax.ppermute(blocks[i], "expert", to_expert(i)) for i in range(EXPERTS - 1)]

    def forwarded(block):
        return [lax.ppermute(block, "expert", within(m)) for m in range(1, group)]

    def shared(arrived):
        return arrived + [
            lax.ppermute(a, "expert", within(m)) for m in range(1, group) for a in arrived
        ]

    def experts(ins):
        count = sum(a.shape[0] for a in ins) // tall
        return call(
            functools.partial(expert_kernel, len(ins)),
            [jax.ShapeDtypeStruct((count // group * tall, wide), BF16)] * group,
            [*weights, *ins],
            24,
            [spread_scratch(pad_rows(count * CAP), width)],
            flops=6 * 256 * width * weights[0].shape[1],
        )

    def exchanged(sums):
        return [sums[0]] + [
            lax.ppermute(sums[m], "expert", within(-m)) for m in range(1, group)
        ]

    def added(terms):
        parts = terms[0].shape[0] // tall
        return call(
            functools.partial(sum_kernel, group), [block] * parts, terms, 8, flops=10**9
        )

    sources = [
        pltpu.with_memory_space_constraint(a, pltpu.HBM)
        for a in (tokens[0], gain, routes_1, gates_1)
    ]
    *blocks, travelling = call(
        functools.partial(pack_kernel, group),
        [block] * EXPERTS + [jax.ShapeDtypeStruct((ahead, LANES), BF16)],
        sources,
        8,
        [pltpu.VMEM(a.shape, a.dtype) for a in sources]
        + [packing, pltpu.SemaphoreType.DMA((len(sources),))],
        flops=10**10,
        space=HBM,
    )
    arrived = across(blocks[:-1])
    second_map, second_gates = call(
        functools.partial(later_kernel, group),
        [
            jax.ShapeDtypeStruct((rows, pad_rows(EXPERTS * CAP)), BF16),
            jax.ShapeDtypeStruct((rows, 128), F32),
        ],
        [routes_2, gates_2],
        8,
        flops=LATER,
    )
    near = [blocks[-1], *forwarded(blocks[-1])]
    near[0], second_map = lax.optimization_barrier((near[0], second_map))
    (carry,) = call(
        carry_kernel,
        [jax.ShapeDtypeStruct((ahead + tall, LANES), BF16)],
        [travelling, *exchanged(experts(near))],
        8,
    )
    *ins, carry = lax.optimization_barrier((*shared(arrived), carry))
    *sums, carry = lax.optimization_barrier((*experts(ins), carry))
    terms = exchanged(sums)
    carried = lax.ppermute(carry, "section", [(i, (i + 1) % sections) for i in range(sections)])
    sums = added(terms)
    home = [lax.ppermute(sums[i], ("section", "expert"), onward(i)) for i in range(EXPERTS - 1)]
    first, *blocks = call(
        functools.partial(middle_kernel, group),
        [whole] + [block] * EXPERTS,
        [*home, carried, gain, second_map],
        8,
        [packing],
    )
    sums = added(exchanged(experts(shared(across(blocks[:-1]) + blocks[-1:]))))
    home = across(sums[:-1])
    (mixed,) = call(
        last_kernel,
        [whole],
        [first, *home, sums[-1], second_map, second_gates],
        8,
        [packing, pltpu.VMEM((rows, width), BF16), pltpu.SemaphoreType.DMA((PARTS,))],
        out_space=HBM,
    )
    return mixed[None]


def solution(mesh):
    rows = P("section", "expert", None)
    slabs = P("section", "expert", None, None)
    return jax.shard_map(
        on_device,
        mesh=mesh,
        in_specs=(rows, P("section", None), rows, rows, rows, rows, slabs, slabs, slabs),
        out_specs=rows,
        check_vma=False,
    )
```

```python
import functools

import jax
import jax.numpy as jnp
from jax import lax
from jax.experimental import pallas as pl
from jax.experimental.pallas import tpu as pltpu
from jax.sharding import PartitionSpec as P

EXPERTS = 4
CAP = 5
ROWS = 16
LANES = 256
PIECE = 512
DEPTH = 1024
PARTS = 4
EPS = 1e-06
F32 = jnp.float32
BF16 = jnp.bfloat16
VMEM = pl.BlockSpec(memory_space=pltpu.VMEM)
HBM = pl.BlockSpec(memory_space=pltpu.HBM)


def distance(place):
    return place ^ (2 + (place >> 1))


def fifth(value):
    return (value * 205) >> 10


def pad_rows(count):
    return -(-count // ROWS) * ROWS


def block_shape(width):
    return CAP * width // LANES, LANES


def spread_scratch(rows, width):
    return pltpu.VMEM((LANES // 128, rows * width // LANES, 128), F32)


def spread(values, spread_ref, width, start=0):
    rows, columns = values.shape
    pieces = width // LANES
    for tile in range(columns // 128):
        piece, half = divmod(start // 128 + tile, LANES // 128)
        spread_ref[half, pl.ds(piece, rows, stride=pieces), :] = values[
            :, tile * 128 : (tile + 1) * 128
        ]


def gathered(spread_ref, rows, width, start=0, columns=None):
    pieces = width // LANES
    tiles = []
    for tile in range(start // 128, (start + (columns or width)) // 128):
        piece, half = divmod(tile, LANES // 128)
        tiles.append(spread_ref[half, pl.ds(piece, rows, stride=pieces), :].astype(BF16))
    return jnp.concatenate(tiles, axis=1)


def to_blocks(spread_ref, refs):
    start = 0
    for ref in refs:
        stop = start + ref.shape[0]
        for half in range(LANES // 128):
            ref[:, half * 128 : (half + 1) * 128] = spread_ref[half, start:stop, :].astype(BF16)
        start = stop


def from_blocks(arrays, spread_ref):
    start = 0
    for array in arrays:
        stop = start + array.shape[0]
        for half in range(LANES // 128):
            spread_ref[half, start:stop, :] = array[:, half * 128 : (half + 1) * 128].astype(F32)
        start = stop
    return start


def upright(row):
    rows = row.shape[1]
    same = lax.broadcasted_iota(jnp.int32, (rows, rows), 0) == lax.broadcasted_iota(
        jnp.int32, (rows, rows), 1
    )
    return jnp.sum(jnp.where(same, row, 0.0), axis=1, keepdims=True)


def slots_of(routes):
    rows = routes.shape[0]
    lanes = lax.broadcasted_iota(jnp.int32, (rows, 128), 1).astype(F32)
    one_hot = (routes == lanes).astype(F32)
    earlier = lax.broadcasted_iota(jnp.int32, (rows, rows), 0) > lax.broadcasted_iota(
        jnp.int32, (rows, rows), 1
    )
    before = jnp.dot(earlier.astype(BF16), one_hot.astype(BF16), preferred_element_type=F32)
    return routes * CAP + jnp.sum(before * one_hot, axis=1, keepdims=True)


def block_map(slots, expert):
    place = lax.broadcasted_iota(jnp.int32, (slots.shape[0], pad_rows(EXPERTS * CAP)), 1)
    block = fifth(place)
    target = (distance(block) ^ expert) * CAP + place - CAP * block
    target = jnp.where(block < EXPERTS, target, -1)
    return (slots == target.astype(F32)).astype(BF16)


def normalize(values, gain):
    inv_scale = lax.rsqrt(jnp.mean(values * values, axis=-1, keepdims=True) + EPS)
    return (values * inv_scale * gain).astype(BF16)


def write_blocks(normed, chosen, spread_ref, block_refs):
    packed = lax.dot_general(
        chosen, normed, (((0,), (0,)), ((), ())), preferred_element_type=F32
    )
    spread(packed, spread_ref, normed.shape[1])
    to_blocks(spread_ref, block_refs)


def hand_out(values, refs):
    start = 0
    for ref in refs:
        ref[...] = values[start : start + ref.shape[0]]
        start += ref.shape[0]


def my_expert(group):
    return lax.axis_index("expert") // group


def split_parts(values):
    parts = []
    for _ in range(3):
        parts.append(values.astype(BF16))
        values = values - parts[-1].astype(F32)
    return parts


def pack_kernel(group, *refs):
    sources, block_refs, ahead_ref = refs[:4], refs[4 : 4 + EXPERTS], refs[4 + EXPERTS]
    held, spread_ref, sems = refs[5 + EXPERTS : -2], refs[-2], refs[-1]
    copies = [
        pltpu.make_async_copy(source, place, sems.at[i])
        for i, (source, place) in enumerate(zip(sources, held))
    ]
    for copy in copies:
        copy.start()
    x_ref, gain_ref, routes_ref, gates_ref = held
    rows, width = x_ref.shape
    for copy in copies[2:]:
        copy.wait()
    slots = slots_of(upright(routes_ref[...].astype(F32)))
    lane = lax.broadcasted_iota(jnp.int32, (rows, LANES), 1)
    meta = jnp.zeros((rows, LANES), F32)
    for i, column in enumerate([slots, *split_parts(upright(gates_ref[...]))]):
        meta = jnp.where(lane == i, column.astype(F32), meta)
    chosen = block_map(slots, my_expert(group))
    for copy in copies[:2]:
        copy.wait()
    for piece in range(width // LANES):
        ahead_ref[piece * rows : (piece + 1) * rows] = x_ref[:, piece * LANES : (piece + 1) * LANES]
    ahead_ref[width // LANES * rows :] = meta.astype(BF16)
    normed = normalize(x_ref[...].astype(F32), gain_ref[...])
    write_blocks(normed, chosen, spread_ref, block_refs)


def fill(blocks, spread_ref):
    filled = from_blocks(blocks, spread_ref)
    spread_ref[:, filled:, :] = jnp.zeros(
        (spread_ref.shape[0], spread_ref.shape[1] - filled, 128), F32
    )


def residual(x, gates, chosen, spread_ref, width, start=0):
    found = jnp.dot(
        chosen,
        gathered(spread_ref, chosen.shape[1], width, start, x.shape[1]),
        preferred_element_type=F32,
    )
    update = (gates * found).astype(BF16)
    return (x.astype(F32) + update.astype(F32)).astype(BF16)


def middle_kernel(group, *refs):
    block_ins, carried_ref, gain_ref, map_ref = refs[: EXPERTS - 1], *refs[EXPERTS - 1 : EXPERTS + 2]
    first_ref, block_refs, spread_ref = refs[EXPERTS + 2], refs[EXPERTS + 3 : -1], refs[-1]
    expert = my_expert(group)
    rows, width = first_ref.shape
    pieces = width // LANES
    x = jnp.concatenate(
        [carried_ref[piece * rows : (piece + 1) * rows] for piece in range(pieces)], axis=1
    )
    meta = carried_ref[pieces * rows : (pieces + 1) * rows].astype(F32)
    gates = meta[:, 1:2] + meta[:, 2:3] + meta[:, 3:4]
    blocks = [ref[...] for ref in block_ins] + [carried_ref[(pieces + 1) * rows :]]
    fill(blocks, spread_ref)
    first = residual(x, gates, block_map(meta[:, 0:1], expert), spread_ref, width)
    first_ref[...] = first
    normed = normalize(first.astype(F32), gain_ref[...])
    write_blocks(normed, map_ref[...], spread_ref, block_refs)


def last_kernel(x_ref, b0, b1, b2, b3, map_ref, gates_ref, out_ref, spread_ref, done_ref, sems):
    chosen = map_ref[...]
    gates = gates_ref[:, 0:1]
    fill([ref[...] for ref in (b0, b1, b2, b3)], spread_ref)
    width = x_ref.shape[1]
    copies = []
    for i in range(PARTS):
        span = slice(i * width // PARTS, (i + 1) * width // PARTS)
        done_ref[:, span] = residual(x_ref[:, span], gates, chosen, spread_ref, width, span.start)
        copies.append(
            pltpu.make_async_copy(done_ref.at[:, span], out_ref.at[:, span], sems.at[i])
        )
        copies[-1].start()
    for copy in copies:
        copy.wait()


def expert_kernel(given, w_gate, w_up, w_down, *refs):
    ins, outs, spread_ref = refs[:given], refs[given:-1], refs[-1]
    width = w_gate.shape[0]
    rows = spread_ref.shape[1] * LANES // width
    from_blocks([ref[...] for ref in ins], spread_ref)
    gate_val = up_val = jnp.zeros((rows, w_gate.shape[1]), F32)
    for start in range(0, width, DEPTH):
        x = gathered(spread_ref, rows, width, start, DEPTH)
        gate_val += jnp.dot(x, w_gate[start : start + DEPTH], preferred_element_type=F32)
        up_val += jnp.dot(x, w_up[start : start + DEPTH], preferred_element_type=F32)
    hidden = (gate_val / (1.0 + jnp.exp(-gate_val)) * up_val).astype(BF16)
    for start in range(0, width, PIECE):
        piece = jnp.dot(hidden, w_down[:, start : start + PIECE], preferred_element_type=F32)
        spread(piece, spread_ref, width, start)
    to_blocks(spread_ref, outs)


def summed(refs):
    total = refs[0][...].astype(F32)
    for ref in refs[1:]:
        total = total + ref[...].astype(F32)
    return total.astype(BF16)


def sum_kernel(given, *refs):
    hand_out(summed(refs[:given]), refs[given:])


def carry_kernel(group, routes_ref, gates_ref, ahead_ref, *refs):
    ins, (out_ref, map_ref, column_ref) = refs[:-3], refs[-3:]
    rows = ahead_ref.shape[0]
    out_ref[:rows] = ahead_ref[...]
    out_ref[rows:] = summed(ins)
    slots = slots_of(upright(routes_ref[...].astype(F32)))
    map_ref[...] = block_map(slots, my_expert(group))
    column_ref[...] = jnp.broadcast_to(upright(gates_ref[...]), column_ref.shape)


def call(body, outs, ins, megabytes, scratch=(), flops=0, space=VMEM, out_space=VMEM):
    moved = sum(a.size * a.dtype.itemsize for a in (*ins, *outs))
    return pl.pallas_call(
        body,
        out_shape=outs,
        in_specs=[space] * len(ins),
        out_specs=[out_space] * len(outs),
        scratch_shapes=list(scratch),
        compiler_params=pltpu.CompilerParams(vmem_limit_bytes=megabytes << 20),
        cost_estimate=pl.CostEstimate(flops=flops, bytes_accessed=moved, transcendentals=0),
    )(*ins)


def on_device(tokens, gain, routes_1, gates_1, routes_2, gates_2, gate_proj, up_proj, down_proj):
    sections, devices = lax.axis_size("section"), lax.axis_size("expert")
    group = devices // EXPERTS
    rows, width = tokens.shape[1:]
    weights = (gate_proj[0, 0], up_proj[0, 0], down_proj[0, 0])
    tall, wide = block_shape(width)
    block = jax.ShapeDtypeStruct((tall, wide), BF16)
    packing = spread_scratch(pad_rows(EXPERTS * CAP), width)
    whole = jax.ShapeDtypeStruct((rows, width), BF16)
    ahead = (width // LANES + 1) * rows
    routes_1, gates_1, routes_2, gates_2 = (
        a.reshape(1, rows) for a in (routes_1, gates_1, routes_2, gates_2)
    )

    def to_expert(place):
        far = distance(place)
        return [(i, (i // group ^ far) * group + i % group) for i in range(devices)]

    def within(shift):
        return [(i, i // group * group + (i + shift) % group) for i in range(devices)]

    def onward(place):
        return [
            (s * devices + i, (s + 1) % sections * devices + j)
            for s in range(sections)
            for i, j in to_expert(place)
        ]

    def across(blocks):
        return [lax.ppermute(blocks[i], "expert", to_expert(i)) for i in range(EXPERTS - 1)]

    def shared(arrived):
        return arrived + [
            lax.ppermute(a, "expert", within(m)) for m in range(1, group) for a in arrived
        ]

    def experts(ins):
        count = sum(a.shape[0] for a in ins) // tall
        return call(
            functools.partial(expert_kernel, len(ins)),
            [jax.ShapeDtypeStruct((count // group * tall, wide), BF16)] * group,
            [*weights, *ins],
            24,
            [spread_scratch(pad_rows(count * CAP), width)],
            flops=6 * 256 * width * weights[0].shape[1],
        )

    def exchanged(sums):
        return [sums[0]] + [
            lax.ppermute(sums[m], "expert", within(-m)) for m in range(1, group)
        ]

    def added(terms):
        parts = terms[0].shape[0] // tall
        return call(
            functools.partial(sum_kernel, group), [block] * parts, terms, 8, flops=10**9
        )

    sources = [
        pltpu.with_memory_space_constraint(a, pltpu.HBM)
        for a in (tokens[0], gain, routes_1, gates_1)
    ]
    *blocks, travelling = call(
        functools.partial(pack_kernel, group),
        [block] * EXPERTS + [jax.ShapeDtypeStruct((ahead, LANES), BF16)],
        sources,
        8,
        [pltpu.VMEM(a.shape, a.dtype) for a in sources]
        + [packing, pltpu.SemaphoreType.DMA((len(sources),))],
        flops=10**10,
        space=HBM,
    )
    arrived = across(blocks[:-1])
    carry, second_map, second_gates = call(
        functools.partial(carry_kernel, group),
        [
            jax.ShapeDtypeStruct((ahead + tall, LANES), BF16),
            jax.ShapeDtypeStruct((rows, pad_rows(EXPERTS * CAP)), BF16),
            jax.ShapeDtypeStruct((rows, 128), F32),
        ],
        [routes_2, gates_2, travelling, *exchanged(experts(shared(blocks[-1:])))],
        8,
    )
    *ins, carry = lax.optimization_barrier((*shared(arrived), carry))
    *sums, carry = lax.optimization_barrier((*experts(ins), carry))
    terms = exchanged(sums)
    carried = lax.ppermute(carry, "section", [(i, (i + 1) % sections) for i in range(sections)])
    sums = added(terms)
    home = [lax.ppermute(sums[i], ("section", "expert"), onward(i)) for i in range(EXPERTS - 1)]
    first, *blocks = call(
        functools.partial(middle_kernel, group),
        [whole] + [block] * EXPERTS,
        [*home, carried, gain, second_map],
        8,
        [packing],
    )
    sums = added(exchanged(experts(shared(across(blocks[:-1]) + blocks[-1:]))))
    home = across(sums[:-1])
    (mixed,) = call(
        last_kernel,
        [whole],
        [first, *home, sums[-1], second_map, second_gates],
        8,
        [packing, pltpu.VMEM((rows, width), BF16), pltpu.SemaphoreType.DMA((PARTS,))],
        out_space=HBM,
    )
    return mixed[None]


def solution(mesh):
    rows = P("section", "expert", None)
    slabs = P("section", "expert", None, None)
    return jax.shard_map(
        on_device,
        mesh=mesh,
        in_specs=(rows, P("section", None), rows, rows, rows, rows, slabs, slabs, slabs),
        out_specs=rows,
        check_vma=False,
    )
```

```python
import functools

import jax
import jax.numpy as jnp
from jax import lax
from jax.experimental import pallas as pl
from jax.experimental.pallas import tpu as pltpu
from jax.sharding import PartitionSpec as P

EXPERTS = 4
CAP = 5
ROWS = 16
LANES = 256
PIECE = 512
DEPTH = 1024
PARTS = 4
EPS = 1e-06
F32 = jnp.float32
BF16 = jnp.bfloat16
VMEM = pl.BlockSpec(memory_space=pltpu.VMEM)
HBM = pl.BlockSpec(memory_space=pltpu.HBM)


def distance(place):
    return place ^ (2 + (place >> 1))


def fifth(value):
    return (value * 205) >> 10


def pad_rows(count):
    return -(-count // ROWS) * ROWS


def block_shape(width):
    return CAP * width // LANES, LANES


def spread_scratch(rows, width):
    return pltpu.VMEM((LANES // 128, rows * width // LANES, 128), F32)


def spread(values, spread_ref, width, start=0):
    rows, columns = values.shape
    pieces = width // LANES
    for tile in range(columns // 128):
        piece, half = divmod(start // 128 + tile, LANES // 128)
        spread_ref[half, pl.ds(piece, rows, stride=pieces), :] = values[
            :, tile * 128 : (tile + 1) * 128
        ]


def gathered(spread_ref, rows, width, start=0, columns=None):
    pieces = width // LANES
    tiles = []
    for tile in range(start // 128, (start + (columns or width)) // 128):
        piece, half = divmod(tile, LANES // 128)
        tiles.append(spread_ref[half, pl.ds(piece, rows, stride=pieces), :].astype(BF16))
    return jnp.concatenate(tiles, axis=1)


def to_blocks(spread_ref, refs):
    start = 0
    for ref in refs:
        stop = start + ref.shape[0]
        for half in range(LANES // 128):
            ref[:, half * 128 : (half + 1) * 128] = spread_ref[half, start:stop, :].astype(BF16)
        start = stop


def from_blocks(arrays, spread_ref):
    start = 0
    for array in arrays:
        stop = start + array.shape[0]
        for half in range(LANES // 128):
            spread_ref[half, start:stop, :] = array[:, half * 128 : (half + 1) * 128].astype(F32)
        start = stop
    return start


def upright(row):
    rows = row.shape[1]
    same = lax.broadcasted_iota(jnp.int32, (rows, rows), 0) == lax.broadcasted_iota(
        jnp.int32, (rows, rows), 1
    )
    return jnp.sum(jnp.where(same, row, 0.0), axis=1, keepdims=True)


def slots_of(routes):
    rows = routes.shape[0]
    lanes = lax.broadcasted_iota(jnp.int32, (rows, 128), 1).astype(F32)
    one_hot = (routes == lanes).astype(F32)
    earlier = lax.broadcasted_iota(jnp.int32, (rows, rows), 0) > lax.broadcasted_iota(
        jnp.int32, (rows, rows), 1
    )
    before = jnp.dot(earlier.astype(BF16), one_hot.astype(BF16), preferred_element_type=F32)
    return routes * CAP + jnp.sum(before * one_hot, axis=1, keepdims=True)


def block_map(slots, expert):
    place = lax.broadcasted_iota(jnp.int32, (slots.shape[0], pad_rows(EXPERTS * CAP)), 1)
    block = fifth(place)
    target = (distance(block) ^ expert) * CAP + place - CAP * block
    target = jnp.where(block < EXPERTS, target, -1)
    return (slots == target.astype(F32)).astype(BF16)


def normalize(values, gain):
    inv_scale = lax.rsqrt(jnp.mean(values * values, axis=-1, keepdims=True) + EPS)
    return (values * inv_scale * gain).astype(BF16)


def write_blocks(normed, chosen, spread_ref, block_refs):
    packed = lax.dot_general(
        chosen, normed, (((0,), (0,)), ((), ())), preferred_element_type=F32
    )
    spread(packed, spread_ref, normed.shape[1])
    to_blocks(spread_ref, block_refs)


def hand_out(values, refs):
    start = 0
    for ref in refs:
        ref[...] = values[start : start + ref.shape[0]]
        start += ref.shape[0]


def my_expert(group):
    return lax.axis_index("expert") // group


def split_parts(values):
    parts = []
    for _ in range(3):
        parts.append(values.astype(BF16))
        values = values - parts[-1].astype(F32)
    return parts


def pack_kernel(group, *refs):
    sources, block_refs = refs[:3], refs[3 : 3 + EXPERTS]
    held, spread_ref, sems = refs[3 + EXPERTS : -2], refs[-2], refs[-1]
    copies = [
        pltpu.make_async_copy(source, place, sems.at[i])
        for i, (source, place) in enumerate(zip(sources, held))
    ]
    for copy in copies:
        copy.start()
    x_ref, gain_ref, routes_ref = held
    copies[2].wait()
    slots = slots_of(upright(routes_ref[...].astype(F32)))
    chosen = block_map(slots, my_expert(group))
    for copy in copies[:2]:
        copy.wait()
    normed = normalize(x_ref[...].astype(F32), gain_ref[...])
    write_blocks(normed, chosen, spread_ref, block_refs)


def fill(blocks, spread_ref):
    filled = from_blocks(blocks, spread_ref)
    spread_ref[:, filled:, :] = jnp.zeros(
        (spread_ref.shape[0], spread_ref.shape[1] - filled, 128), F32
    )


def residual(x, gates, chosen, spread_ref, width, start=0):
    found = jnp.dot(
        chosen,
        gathered(spread_ref, chosen.shape[1], width, start, x.shape[1]),
        preferred_element_type=F32,
    )
    update = (gates * found).astype(BF16)
    return (x.astype(F32) + update.astype(F32)).astype(BF16)


def middle_kernel(group, *refs):
    block_ins, carried_ref, gain_ref, map_ref = refs[: EXPERTS - 1], *refs[EXPERTS - 1 : EXPERTS + 2]
    first_ref, block_refs, spread_ref = refs[EXPERTS + 2], refs[EXPERTS + 3 : -1], refs[-1]
    expert = my_expert(group)
    rows, width = first_ref.shape
    pieces = width // LANES
    x = jnp.concatenate(
        [carried_ref[piece * rows : (piece + 1) * rows] for piece in range(pieces)], axis=1
    )
    meta = carried_ref[pieces * rows : (pieces + 1) * rows].astype(F32)
    gates = meta[:, 1:2] + meta[:, 2:3] + meta[:, 3:4]
    blocks = [ref[...] for ref in block_ins] + [carried_ref[(pieces + 1) * rows :]]
    fill(blocks, spread_ref)
    first = residual(x, gates, block_map(meta[:, 0:1], expert), spread_ref, width)
    first_ref[...] = first
    normed = normalize(first.astype(F32), gain_ref[...])
    write_blocks(normed, map_ref[...], spread_ref, block_refs)


def last_kernel(x_ref, b0, b1, b2, b3, map_ref, gates_ref, out_ref, spread_ref, done_ref, sems):
    chosen = map_ref[...]
    gates = gates_ref[:, 0:1]
    fill([ref[...] for ref in (b0, b1, b2, b3)], spread_ref)
    width = x_ref.shape[1]
    copies = []
    for i in range(PARTS):
        span = slice(i * width // PARTS, (i + 1) * width // PARTS)
        done_ref[:, span] = residual(x_ref[:, span], gates, chosen, spread_ref, width, span.start)
        copies.append(
            pltpu.make_async_copy(done_ref.at[:, span], out_ref.at[:, span], sems.at[i])
        )
        copies[-1].start()
    for copy in copies:
        copy.wait()


def expert_kernel(given, w_gate, w_up, w_down, *refs):
    ins, outs, spread_ref = refs[:given], refs[given:-1], refs[-1]
    width = w_gate.shape[0]
    rows = spread_ref.shape[1] * LANES // width
    from_blocks([ref[...] for ref in ins], spread_ref)
    gate_val = up_val = jnp.zeros((rows, w_gate.shape[1]), F32)
    for start in range(0, width, DEPTH):
        x = gathered(spread_ref, rows, width, start, DEPTH)
        gate_val += jnp.dot(x, w_gate[start : start + DEPTH], preferred_element_type=F32)
        up_val += jnp.dot(x, w_up[start : start + DEPTH], preferred_element_type=F32)
    hidden = (gate_val / (1.0 + jnp.exp(-gate_val)) * up_val).astype(BF16)
    for start in range(0, width, PIECE):
        piece = jnp.dot(hidden, w_down[:, start : start + PIECE], preferred_element_type=F32)
        spread(piece, spread_ref, width, start)
    to_blocks(spread_ref, outs)


def summed(refs):
    total = refs[0][...].astype(F32)
    for ref in refs[1:]:
        total = total + ref[...].astype(F32)
    return total.astype(BF16)


def sum_kernel(given, *refs):
    hand_out(summed(refs[:given]), refs[given:])


def carry_kernel(group, x_ref, first_routes, first_gates, routes_ref, gates_ref, *refs):
    ins, (out_ref, map_ref, column_ref) = refs[:-3], refs[-3:]
    rows, width = x_ref.shape
    for piece in range(width // LANES):
        out_ref[piece * rows : (piece + 1) * rows] = x_ref[:, piece * LANES : (piece + 1) * LANES]
    filled = width // LANES * rows
    slots = slots_of(upright(first_routes[...].astype(F32)))
    lane = lax.broadcasted_iota(jnp.int32, (rows, LANES), 1)
    meta = jnp.zeros((rows, LANES), F32)
    for i, column in enumerate([slots, *split_parts(upright(first_gates[...]))]):
        meta = jnp.where(lane == i, column.astype(F32), meta)
    out_ref[filled : filled + rows] = meta.astype(BF16)
    out_ref[filled + rows :] = summed(ins)
    slots = slots_of(upright(routes_ref[...].astype(F32)))
    map_ref[...] = block_map(slots, my_expert(group))
    column_ref[...] = jnp.broadcast_to(upright(gates_ref[...]), column_ref.shape)


def call(body, outs, ins, megabytes, scratch=(), flops=0, space=VMEM, out_space=VMEM):
    moved = sum(a.size * a.dtype.itemsize for a in (*ins, *outs))
    return pl.pallas_call(
        body,
        out_shape=outs,
        in_specs=[space] * len(ins),
        out_specs=[out_space] * len(outs),
        scratch_shapes=list(scratch),
        compiler_params=pltpu.CompilerParams(vmem_limit_bytes=megabytes << 20),
        cost_estimate=pl.CostEstimate(flops=flops, bytes_accessed=moved, transcendentals=0),
    )(*ins)


def on_device(tokens, gain, routes_1, gates_1, routes_2, gates_2, gate_proj, up_proj, down_proj):
    sections, devices = lax.axis_size("section"), lax.axis_size("expert")
    group = devices // EXPERTS
    rows, width = tokens.shape[1:]
    weights = (gate_proj[0, 0], up_proj[0, 0], down_proj[0, 0])
    tall, wide = block_shape(width)
    block = jax.ShapeDtypeStruct((tall, wide), BF16)
    packing = spread_scratch(pad_rows(EXPERTS * CAP), width)
    whole = jax.ShapeDtypeStruct((rows, width), BF16)
    ahead = (width // LANES + 1) * rows
    routes_1, gates_1, routes_2, gates_2 = (
        a.reshape(1, rows) for a in (routes_1, gates_1, routes_2, gates_2)
    )

    def to_expert(place):
        far = distance(place)
        return [(i, (i // group ^ far) * group + i % group) for i in range(devices)]

    def within(shift):
        return [(i, i // group * group + (i + shift) % group) for i in range(devices)]

    def onward(place):
        return [
            (s * devices + i, (s + 1) % sections * devices + j)
            for s in range(sections)
            for i, j in to_expert(place)
        ]

    def across(blocks):
        return [lax.ppermute(blocks[i], "expert", to_expert(i)) for i in range(EXPERTS - 1)]

    def shared(arrived):
        return arrived + [
            lax.ppermute(a, "expert", within(m)) for m in range(1, group) for a in arrived
        ]

    def experts(ins):
        count = sum(a.shape[0] for a in ins) // tall
        return call(
            functools.partial(expert_kernel, len(ins)),
            [jax.ShapeDtypeStruct((count // group * tall, wide), BF16)] * group,
            [*weights, *ins],
            24,
            [spread_scratch(pad_rows(count * CAP), width)],
            flops=6 * 256 * width * weights[0].shape[1],
        )

    def exchanged(sums):
        return [sums[0]] + [
            lax.ppermute(sums[m], "expert", within(-m)) for m in range(1, group)
        ]

    def added(terms):
        parts = terms[0].shape[0] // tall
        return call(
            functools.partial(sum_kernel, group), [block] * parts, terms, 8, flops=10**9
        )

    sources = [
        pltpu.with_memory_space_constraint(a, pltpu.HBM)
        for a in (tokens[0], gain, routes_1)
    ]
    *blocks, own = call(
        functools.partial(pack_kernel, group),
        [block] * EXPERTS,
        sources,
        8,
        [pltpu.VMEM(a.shape, a.dtype) for a in sources]
        + [packing, pltpu.SemaphoreType.DMA((len(sources),))],
        flops=10**10,
        space=HBM,
    )
    arrived = across(blocks)
    carry, second_map, second_gates = call(
        functools.partial(carry_kernel, group),
        [
            jax.ShapeDtypeStruct((ahead + tall, LANES), BF16),
            jax.ShapeDtypeStruct((rows, pad_rows(EXPERTS * CAP)), BF16),
            jax.ShapeDtypeStruct((rows, 128), F32),
        ],
        [tokens[0], routes_1, gates_1, routes_2, gates_2, *exchanged(experts(shared([own])))],
        8,
    )
    *ins, carry = lax.optimization_barrier((*shared(arrived), carry))
    *sums, carry = lax.optimization_barrier((*experts(ins), carry))
    terms = exchanged(sums)
    carried = lax.ppermute(carry, "section", [(i, (i + 1) % sections) for i in range(sections)])
    sums = added(terms)
    home = [lax.ppermute(sums[i], ("section", "expert"), onward(i)) for i in range(EXPERTS - 1)]
    first, *blocks = call(
        functools.partial(middle_kernel, group),
        [whole] + [block] * EXPERTS,
        [*home, carried, gain, second_map],
        8,
        [packing],
    )
    sums = added(exchanged(experts(shared(across(blocks[:-1]) + blocks[-1:]))))
    home = across(sums[:-1])
    (mixed,) = call(
        last_kernel,
        [whole],
        [first, *home, sums[-1], second_map, second_gates],
        8,
        [packing, pltpu.VMEM((rows, width), BF16), pltpu.SemaphoreType.DMA((PARTS,))],
        out_space=HBM,
    )
    return mixed[None]


def solution(mesh):
    rows = P("section", "expert", None)
    slabs = P("section", "expert", None, None)
    return jax.shard_map(
        on_device,
        mesh=mesh,
        in_specs=(rows, P("section", None), rows, rows, rows, rows, slabs, slabs, slabs),
        out_specs=rows,
        check_vma=False,
    )
```

```python
import functools

import jax
import jax.numpy as jnp
from jax import lax
from jax.experimental import pallas as pl
from jax.experimental.pallas import tpu as pltpu
from jax.sharding import PartitionSpec as P

EXPERTS = 4
CAP = 5
ROWS = 16
LANES = 256
PIECE = 512
PARTS = 4
EPS = 1e-06
F32 = jnp.float32
BF16 = jnp.bfloat16
VMEM = pl.BlockSpec(memory_space=pltpu.VMEM)
HBM = pl.BlockSpec(memory_space=pltpu.HBM)


def distance(place):
    return place ^ (2 + (place >> 1))


def fifth(value):
    return (value * 205) >> 10


def pad_rows(count):
    return -(-count // ROWS) * ROWS


def block_shape(width):
    return CAP * width // LANES, LANES


def spread_scratch(rows, width):
    return pltpu.VMEM((LANES // 128, (rows + 1) * width // LANES, 128), F32)


def spread(values, spread_ref, width, start=0):
    rows, columns = values.shape
    pieces = width // LANES
    for tile in range(columns // 128):
        piece, half = divmod(start // 128 + tile, LANES // 128)
        spread_ref[half, pl.ds(piece, rows, stride=pieces), :] = values[
            :, tile * 128 : (tile + 1) * 128
        ]


def gathered(spread_ref, rows, width, start=0, columns=None):
    pieces = width // LANES
    tiles = []
    for tile in range(start // 128, (start + (columns or width)) // 128):
        piece, half = divmod(tile, LANES // 128)
        tiles.append(spread_ref[half, pl.ds(piece, rows, stride=pieces), :].astype(BF16))
    return jnp.concatenate(tiles, axis=1)


def to_blocks(spread_ref, refs):
    start = 0
    for ref in refs:
        stop = start + ref.shape[0]
        for half in range(LANES // 128):
            ref[:, half * 128 : (half + 1) * 128] = spread_ref[half, start:stop, :].astype(BF16)
        start = stop


def from_blocks(arrays, spread_ref):
    start = 0
    for array in arrays:
        stop = start + array.shape[0]
        for half in range(LANES // 128):
            spread_ref[half, start:stop, :] = array[:, half * 128 : (half + 1) * 128].astype(F32)
        start = stop
    return start


def upright(row):
    rows = row.shape[1]
    same = lax.broadcasted_iota(jnp.int32, (rows, rows), 0) == lax.broadcasted_iota(
        jnp.int32, (rows, rows), 1
    )
    return jnp.sum(jnp.where(same, row, 0.0), axis=1, keepdims=True)


def slots_of(routes):
    rows = routes.shape[0]
    lanes = lax.broadcasted_iota(jnp.int32, (rows, 128), 1).astype(F32)
    one_hot = (routes == lanes).astype(F32)
    earlier = lax.broadcasted_iota(jnp.int32, (rows, rows), 0) > lax.broadcasted_iota(
        jnp.int32, (rows, rows), 1
    )
    before = jnp.dot(earlier.astype(BF16), one_hot.astype(BF16), preferred_element_type=F32)
    return routes * CAP + jnp.sum(before * one_hot, axis=1, keepdims=True)


def block_map(slots, expert):
    place = lax.broadcasted_iota(jnp.int32, (slots.shape[0], pad_rows(EXPERTS * CAP)), 1)
    block = fifth(place)
    target = (distance(block) ^ expert) * CAP + place - CAP * block
    target = jnp.where(block < EXPERTS, target, -1)
    return (slots == target.astype(F32)).astype(BF16)


def normalize(values, gain):
    inv_scale = lax.rsqrt(jnp.mean(values * values, axis=-1, keepdims=True) + EPS)
    return (values * inv_scale * gain).astype(BF16)


def write_blocks(normed, chosen, spread_ref, block_refs):
    packed = lax.dot_general(
        chosen, normed, (((0,), (0,)), ((), ())), preferred_element_type=F32
    )
    spread(packed, spread_ref, normed.shape[1])
    to_blocks(spread_ref, block_refs)


def hand_out(values, refs):
    start = 0
    for ref in refs:
        ref[...] = values[start : start + ref.shape[0]]
        start += ref.shape[0]


def my_expert(group):
    return lax.axis_index("expert") // group


def split_parts(values):
    parts = []
    for _ in range(3):
        parts.append(values.astype(BF16))
        values = values - parts[-1].astype(F32)
    return parts


def pack_kernel(group, *refs):
    sources, block_refs, ahead_ref = refs[:4], refs[4 : 4 + EXPERTS], refs[4 + EXPERTS]
    held, spread_ref, sems = refs[5 + EXPERTS : -2], refs[-2], refs[-1]
    copies = [
        pltpu.make_async_copy(source, place, sems.at[i])
        for i, (source, place) in enumerate(zip(sources, held))
    ]
    for copy in copies:
        copy.start()
    x_ref, gain_ref, routes_ref, gates_ref = held
    rows, width = x_ref.shape
    for copy in copies[2:]:
        copy.wait()
    slots = slots_of(upright(routes_ref[...].astype(F32)))
    lane = lax.broadcasted_iota(jnp.int32, (rows, LANES), 1)
    meta = jnp.zeros((rows, LANES), F32)
    for i, column in enumerate([slots, *split_parts(upright(gates_ref[...]))]):
        meta = jnp.where(lane == i, column.astype(F32), meta)
    chosen = block_map(slots, my_expert(group))
    for copy in copies[:2]:
        copy.wait()
    for piece in range(width // LANES):
        ahead_ref[piece * rows : (piece + 1) * rows] = x_ref[:, piece * LANES : (piece + 1) * LANES]
    ahead_ref[width // LANES * rows :] = meta.astype(BF16)
    normed = normalize(x_ref[...].astype(F32), gain_ref[...])
    write_blocks(normed, chosen, spread_ref, block_refs)


def fill(blocks, spread_ref):
    filled = from_blocks(blocks, spread_ref)
    spread_ref[:, filled:, :] = jnp.zeros(
        (spread_ref.shape[0], spread_ref.shape[1] - filled, 128), F32
    )


def residual(x, gates, chosen, spread_ref, width, start=0):
    found = jnp.dot(
        chosen,
        gathered(spread_ref, chosen.shape[1], width, start, x.shape[1]),
        preferred_element_type=F32,
    )
    update = (gates * found).astype(BF16)
    return (x.astype(F32) + update.astype(F32)).astype(BF16)


def middle_kernel(group, *refs):
    block_ins, carried_ref, gain_ref, map_ref = refs[: EXPERTS - 1], *refs[EXPERTS - 1 : EXPERTS + 2]
    first_ref, block_refs, spread_ref = refs[EXPERTS + 2], refs[EXPERTS + 3 : -1], refs[-1]
    expert = my_expert(group)
    rows, width = first_ref.shape
    pieces = width // LANES
    x = jnp.concatenate(
        [carried_ref[piece * rows : (piece + 1) * rows] for piece in range(pieces)], axis=1
    )
    meta = carried_ref[pieces * rows : (pieces + 1) * rows].astype(F32)
    gates = meta[:, 1:2] + meta[:, 2:3] + meta[:, 3:4]
    blocks = [ref[...] for ref in block_ins] + [carried_ref[(pieces + 1) * rows :]]
    fill(blocks, spread_ref)
    first = residual(x, gates, block_map(meta[:, 0:1], expert), spread_ref, width)
    first_ref[...] = first
    normed = normalize(first.astype(F32), gain_ref[...])
    write_blocks(normed, map_ref[...], spread_ref, block_refs)


def last_kernel(x_ref, b0, b1, b2, b3, map_ref, gates_ref, out_ref, spread_ref, done_ref, sems):
    chosen = map_ref[...]
    gates = gates_ref[:, 0:1]
    fill([ref[...] for ref in (b0, b1, b2, b3)], spread_ref)
    width = x_ref.shape[1]
    copies = []
    for i in range(PARTS):
        span = slice(i * width // PARTS, (i + 1) * width // PARTS)
        done_ref[:, span] = residual(x_ref[:, span], gates, chosen, spread_ref, width, span.start)
        copies.append(
            pltpu.make_async_copy(done_ref.at[:, span], out_ref.at[:, span], sems.at[i])
        )
        copies[-1].start()
    for copy in copies:
        copy.wait()


def expert_kernel(given, w_gate, w_up, w_down, *refs):
    ins, outs, spread_ref = refs[:given], refs[given:-1], refs[-1]
    width = w_gate.shape[0]
    rows = spread_ref.shape[1] * LANES // width - 1
    from_blocks([ref[...] for ref in ins], spread_ref)
    x = gathered(spread_ref, rows, width)
    gate_val = jnp.dot(x, w_gate[...], preferred_element_type=F32)
    up_val = jnp.dot(x, w_up[...], preferred_element_type=F32)
    hidden = (gate_val / (1.0 + jnp.exp(-gate_val)) * up_val).astype(BF16)
    for start in range(0, width, PIECE):
        piece = jnp.dot(hidden, w_down[:, start : start + PIECE], preferred_element_type=F32)
        spread(piece, spread_ref, width, start)
    to_blocks(spread_ref, outs)


def summed(refs):
    total = refs[0][...].astype(F32)
    for ref in refs[1:]:
        total = total + ref[...].astype(F32)
    return total.astype(BF16)


def sum_kernel(given, *refs):
    hand_out(summed(refs[:given]), refs[given:])


def carry_kernel(group, routes_ref, gates_ref, ahead_ref, *refs):
    ins, (out_ref, map_ref, column_ref) = refs[:-3], refs[-3:]
    rows = ahead_ref.shape[0]
    out_ref[:rows] = ahead_ref[...]
    out_ref[rows:] = summed(ins)
    slots = slots_of(upright(routes_ref[...].astype(F32)))
    map_ref[...] = block_map(slots, my_expert(group))
    column_ref[...] = jnp.broadcast_to(upright(gates_ref[...]), column_ref.shape)


def call(body, outs, ins, megabytes, scratch=(), flops=0, space=VMEM, out_space=VMEM):
    moved = sum(a.size * a.dtype.itemsize for a in (*ins, *outs))
    return pl.pallas_call(
        body,
        out_shape=outs,
        in_specs=[space] * len(ins),
        out_specs=[out_space] * len(outs),
        scratch_shapes=list(scratch),
        compiler_params=pltpu.CompilerParams(vmem_limit_bytes=megabytes << 20),
        cost_estimate=pl.CostEstimate(flops=flops, bytes_accessed=moved, transcendentals=0),
    )(*ins)


def on_device(tokens, gain, routes_1, gates_1, routes_2, gates_2, gate_proj, up_proj, down_proj):
    sections, devices = lax.axis_size("section"), lax.axis_size("expert")
    group = devices // EXPERTS
    rows, width = tokens.shape[1:]
    weights = (gate_proj[0, 0], up_proj[0, 0], down_proj[0, 0])
    tall, wide = block_shape(width)
    block = jax.ShapeDtypeStruct((tall, wide), BF16)
    packing = spread_scratch(pad_rows(EXPERTS * CAP), width)
    whole = jax.ShapeDtypeStruct((rows, width), BF16)
    ahead = (width // LANES + 1) * rows
    routes_1, gates_1, routes_2, gates_2 = (
        a.reshape(1, rows) for a in (routes_1, gates_1, routes_2, gates_2)
    )

    def to_expert(place):
        far = distance(place)
        return [(i, (i // group ^ far) * group + i % group) for i in range(devices)]

    def within(shift):
        return [(i, i // group * group + (i + shift) % group) for i in range(devices)]

    def onward(place):
        return [
            (s * devices + i, (s + 1) % sections * devices + j)
            for s in range(sections)
            for i, j in to_expert(place)
        ]

    def across(blocks):
        return [lax.ppermute(blocks[i], "expert", to_expert(i)) for i in range(EXPERTS - 1)]

    def shared(arrived):
        return arrived + [
            lax.ppermute(a, "expert", within(m)) for m in range(1, group) for a in arrived
        ]

    def experts(ins):
        count = sum(a.shape[0] for a in ins) // tall
        return call(
            functools.partial(expert_kernel, len(ins)),
            [jax.ShapeDtypeStruct((count // group * tall, wide), BF16)] * group,
            [*weights, *ins],
            24,
            [spread_scratch(pad_rows(count * CAP), width)],
            flops=6 * 256 * width * weights[0].shape[1],
        )

    def exchanged(sums):
        return [sums[0]] + [
            lax.ppermute(sums[m], "expert", within(-m)) for m in range(1, group)
        ]

    def added(terms):
        parts = terms[0].shape[0] // tall
        return call(
            functools.partial(sum_kernel, group), [block] * parts, terms, 8, flops=10**9
        )

    sources = [
        pltpu.with_memory_space_constraint(a, pltpu.HBM)
        for a in (tokens[0], gain, routes_1, gates_1)
    ]
    *blocks, travelling = call(
        functools.partial(pack_kernel, group),
        [block] * EXPERTS + [jax.ShapeDtypeStruct((ahead, LANES), BF16)],
        sources,
        8,
        [pltpu.VMEM(a.shape, a.dtype) for a in sources]
        + [packing, pltpu.SemaphoreType.DMA((len(sources),))],
        flops=10**10,
        space=HBM,
    )
    arrived = across(blocks[:-1])
    carry, second_map, second_gates = call(
        functools.partial(carry_kernel, group),
        [
            jax.ShapeDtypeStruct((ahead + tall, LANES), BF16),
            jax.ShapeDtypeStruct((rows, pad_rows(EXPERTS * CAP)), BF16),
            jax.ShapeDtypeStruct((rows, 128), F32),
        ],
        [routes_2, gates_2, travelling, *exchanged(experts(shared(blocks[-1:])))],
        8,
    )
    *ins, carry = lax.optimization_barrier((*shared(arrived), carry))
    *sums, carry = lax.optimization_barrier((*experts(ins), carry))
    terms = exchanged(sums)
    carried = lax.ppermute(carry, "section", [(i, (i + 1) % sections) for i in range(sections)])
    sums = added(terms)
    home = [lax.ppermute(sums[i], ("section", "expert"), onward(i)) for i in range(EXPERTS - 1)]
    first, *blocks = call(
        functools.partial(middle_kernel, group),
        [whole] + [block] * EXPERTS,
        [*home, carried, gain, second_map],
        8,
        [packing],
    )
    sums = added(exchanged(experts(shared(across(blocks[:-1]) + blocks[-1:]))))
    home = across(sums[:-1])
    (mixed,) = call(
        last_kernel,
        [whole],
        [first, *home, sums[-1], second_map, second_gates],
        8,
        [packing, pltpu.VMEM((rows, width), BF16), pltpu.SemaphoreType.DMA((PARTS,))],
        out_space=HBM,
    )
    return mixed[None]


def solution(mesh):
    rows = P("section", "expert", None)
    slabs = P("section", "expert", None, None)
    return jax.shard_map(
        on_device,
        mesh=mesh,
        in_specs=(rows, P("section", None), rows, rows, rows, rows, slabs, slabs, slabs),
        out_specs=rows,
        check_vma=False,
    )
```

```python
import functools

import jax
import jax.numpy as jnp
from jax import lax
from jax.experimental import pallas as pl
from jax.experimental.pallas import tpu as pltpu
from jax.sharding import PartitionSpec as P

EXPERTS = 4
CAP = 5
ROWS = 16
LANES = 256
PIECE = 256
PARTS = 4
EPS = 1e-06
F32 = jnp.float32
BF16 = jnp.bfloat16
VMEM = pl.BlockSpec(memory_space=pltpu.VMEM)
HBM = pl.BlockSpec(memory_space=pltpu.HBM)


def distance(place):
    return place ^ (2 + (place >> 1))


def fifth(value):
    return (value * 205) >> 10


def pad_rows(count):
    return -(-count // ROWS) * ROWS


def block_shape(width):
    return CAP * width // LANES, LANES


def spread_scratch(rows, width):
    return pltpu.VMEM((LANES // 128, (rows + 1) * width // LANES, 128), F32)


def spread(values, spread_ref, width, start=0):
    rows, columns = values.shape
    pieces = width // LANES
    for tile in range(columns // 128):
        piece, half = divmod(start // 128 + tile, LANES // 128)
        spread_ref[half, pl.ds(piece, rows, stride=pieces), :] = values[
            :, tile * 128 : (tile + 1) * 128
        ]


def gathered(spread_ref, rows, width, start=0, columns=None):
    pieces = width // LANES
    tiles = []
    for tile in range(start // 128, (start + (columns or width)) // 128):
        piece, half = divmod(tile, LANES // 128)
        tiles.append(spread_ref[half, pl.ds(piece, rows, stride=pieces), :].astype(BF16))
    return jnp.concatenate(tiles, axis=1)


def to_blocks(spread_ref, refs):
    start = 0
    for ref in refs:
        stop = start + ref.shape[0]
        for half in range(LANES // 128):
            ref[:, half * 128 : (half + 1) * 128] = spread_ref[half, start:stop, :].astype(BF16)
        start = stop


def from_blocks(arrays, spread_ref):
    start = 0
    for array in arrays:
        stop = start + array.shape[0]
        for half in range(LANES // 128):
            spread_ref[half, start:stop, :] = array[:, half * 128 : (half + 1) * 128].astype(F32)
        start = stop
    return start


def upright(row):
    rows = row.shape[1]
    same = lax.broadcasted_iota(jnp.int32, (rows, rows), 0) == lax.broadcasted_iota(
        jnp.int32, (rows, rows), 1
    )
    return jnp.sum(jnp.where(same, row, 0.0), axis=1, keepdims=True)


def slots_of(routes):
    rows = routes.shape[0]
    lanes = lax.broadcasted_iota(jnp.int32, (rows, 128), 1).astype(F32)
    one_hot = (routes == lanes).astype(F32)
    earlier = lax.broadcasted_iota(jnp.int32, (rows, rows), 0) > lax.broadcasted_iota(
        jnp.int32, (rows, rows), 1
    )
    before = jnp.dot(earlier.astype(BF16), one_hot.astype(BF16), preferred_element_type=F32)
    return routes * CAP + jnp.sum(before * one_hot, axis=1, keepdims=True)


def block_map(slots, expert):
    place = lax.broadcasted_iota(jnp.int32, (slots.shape[0], pad_rows(EXPERTS * CAP)), 1)
    block = fifth(place)
    target = (distance(block) ^ expert) * CAP + place - CAP * block
    target = jnp.where(block < EXPERTS, target, -1)
    return (slots == target.astype(F32)).astype(BF16)


def normalize(values, gain):
    inv_scale = lax.rsqrt(jnp.mean(values * values, axis=-1, keepdims=True) + EPS)
    return (values * inv_scale * gain).astype(BF16)


def write_blocks(normed, chosen, spread_ref, block_refs):
    packed = lax.dot_general(
        chosen, normed, (((0,), (0,)), ((), ())), preferred_element_type=F32
    )
    spread(packed, spread_ref, normed.shape[1])
    to_blocks(spread_ref, block_refs)


def hand_out(values, refs):
    start = 0
    for ref in refs:
        ref[...] = values[start : start + ref.shape[0]]
        start += ref.shape[0]


def my_expert(group):
    return lax.axis_index("expert") // group


def split_parts(values):
    parts = []
    for _ in range(3):
        parts.append(values.astype(BF16))
        values = values - parts[-1].astype(F32)
    return parts


def pack_kernel(group, *refs):
    sources, block_refs, ahead_ref = refs[:4], refs[4 : 4 + EXPERTS], refs[4 + EXPERTS]
    held, spread_ref, sems = refs[5 + EXPERTS : -2], refs[-2], refs[-1]
    copies = [
        pltpu.make_async_copy(source, place, sems.at[i])
        for i, (source, place) in enumerate(zip(sources, held))
    ]
    for copy in copies:
        copy.start()
    x_ref, gain_ref, routes_ref, gates_ref = held
    rows, width = x_ref.shape
    for copy in copies[2:]:
        copy.wait()
    slots = slots_of(upright(routes_ref[...].astype(F32)))
    lane = lax.broadcasted_iota(jnp.int32, (rows, LANES), 1)
    meta = jnp.zeros((rows, LANES), F32)
    for i, column in enumerate([slots, *split_parts(upright(gates_ref[...]))]):
        meta = jnp.where(lane == i, column.astype(F32), meta)
    chosen = block_map(slots, my_expert(group))
    for copy in copies[:2]:
        copy.wait()
    for piece in range(width // LANES):
        ahead_ref[piece * rows : (piece + 1) * rows] = x_ref[:, piece * LANES : (piece + 1) * LANES]
    ahead_ref[width // LANES * rows :] = meta.astype(BF16)
    normed = normalize(x_ref[...].astype(F32), gain_ref[...])
    write_blocks(normed, chosen, spread_ref, block_refs)


def fill(blocks, spread_ref):
    filled = from_blocks(blocks, spread_ref)
    spread_ref[:, filled:, :] = jnp.zeros(
        (spread_ref.shape[0], spread_ref.shape[1] - filled, 128), F32
    )


def residual(x, gates, chosen, spread_ref, width, start=0):
    found = jnp.dot(
        chosen,
        gathered(spread_ref, chosen.shape[1], width, start, x.shape[1]),
        preferred_element_type=F32,
    )
    update = (gates * found).astype(BF16)
    return (x.astype(F32) + update.astype(F32)).astype(BF16)


def middle_kernel(group, *refs):
    block_ins, carried_ref, gain_ref, map_ref = refs[: EXPERTS - 1], *refs[EXPERTS - 1 : EXPERTS + 2]
    first_ref, block_refs, spread_ref = refs[EXPERTS + 2], refs[EXPERTS + 3 : -1], refs[-1]
    expert = my_expert(group)
    rows, width = first_ref.shape
    pieces = width // LANES
    x = jnp.concatenate(
        [carried_ref[piece * rows : (piece + 1) * rows] for piece in range(pieces)], axis=1
    )
    meta = carried_ref[pieces * rows : (pieces + 1) * rows].astype(F32)
    gates = meta[:, 1:2] + meta[:, 2:3] + meta[:, 3:4]
    blocks = [ref[...] for ref in block_ins] + [carried_ref[(pieces + 1) * rows :]]
    fill(blocks, spread_ref)
    first = residual(x, gates, block_map(meta[:, 0:1], expert), spread_ref, width)
    first_ref[...] = first
    normed = normalize(first.astype(F32), gain_ref[...])
    write_blocks(normed, map_ref[...], spread_ref, block_refs)


def last_kernel(x_ref, b0, b1, b2, b3, map_ref, gates_ref, out_ref, spread_ref, done_ref, sems):
    chosen = map_ref[...]
    gates = gates_ref[:, 0:1]
    fill([ref[...] for ref in (b0, b1, b2, b3)], spread_ref)
    width = x_ref.shape[1]
    copies = []
    for i in range(PARTS):
        span = slice(i * width // PARTS, (i + 1) * width // PARTS)
        done_ref[:, span] = residual(x_ref[:, span], gates, chosen, spread_ref, width, span.start)
        copies.append(
            pltpu.make_async_copy(done_ref.at[:, span], out_ref.at[:, span], sems.at[i])
        )
        copies[-1].start()
    for copy in copies:
        copy.wait()


def expert_kernel(given, w_gate, w_up, w_down, *refs):
    ins, outs, spread_ref = refs[:given], refs[given:-1], refs[-1]
    width = w_gate.shape[0]
    rows = spread_ref.shape[1] * LANES // width - 1
    from_blocks([ref[...] for ref in ins], spread_ref)
    x = gathered(spread_ref, rows, width)
    hidden = []
    for start in range(0, w_gate.shape[1], PIECE):
        gate_val = jnp.dot(x, w_gate[:, start : start + PIECE], preferred_element_type=F32)
        up_val = jnp.dot(x, w_up[:, start : start + PIECE], preferred_element_type=F32)
        hidden.append((gate_val / (1.0 + jnp.exp(-gate_val)) * up_val).astype(BF16))
    hidden = jnp.concatenate(hidden, axis=1)
    for start in range(0, width, PIECE):
        piece = jnp.dot(hidden, w_down[:, start : start + PIECE], preferred_element_type=F32)
        spread(piece, spread_ref, width, start)
    to_blocks(spread_ref, outs)


def summed(refs):
    total = refs[0][...].astype(F32)
    for ref in refs[1:]:
        total = total + ref[...].astype(F32)
    return total.astype(BF16)


def sum_kernel(given, *refs):
    hand_out(summed(refs[:given]), refs[given:])


def carry_kernel(group, routes_ref, gates_ref, ahead_ref, *refs):
    ins, (out_ref, map_ref, column_ref) = refs[:-3], refs[-3:]
    rows = ahead_ref.shape[0]
    out_ref[:rows] = ahead_ref[...]
    out_ref[rows:] = summed(ins)
    slots = slots_of(upright(routes_ref[...].astype(F32)))
    map_ref[...] = block_map(slots, my_expert(group))
    column_ref[...] = jnp.broadcast_to(upright(gates_ref[...]), column_ref.shape)


def call(body, outs, ins, megabytes, scratch=(), flops=0, space=VMEM, out_space=VMEM):
    moved = sum(a.size * a.dtype.itemsize for a in (*ins, *outs))
    return pl.pallas_call(
        body,
        out_shape=outs,
        in_specs=[space] * len(ins),
        out_specs=[out_space] * len(outs),
        scratch_shapes=list(scratch),
        compiler_params=pltpu.CompilerParams(vmem_limit_bytes=megabytes << 20),
        cost_estimate=pl.CostEstimate(flops=flops, bytes_accessed=moved, transcendentals=0),
    )(*ins)


def on_device(tokens, gain, routes_1, gates_1, routes_2, gates_2, gate_proj, up_proj, down_proj):
    sections, devices = lax.axis_size("section"), lax.axis_size("expert")
    group = devices // EXPERTS
    rows, width = tokens.shape[1:]
    weights = (gate_proj[0, 0], up_proj[0, 0], down_proj[0, 0])
    tall, wide = block_shape(width)
    block = jax.ShapeDtypeStruct((tall, wide), BF16)
    packing = spread_scratch(pad_rows(EXPERTS * CAP), width)
    whole = jax.ShapeDtypeStruct((rows, width), BF16)
    ahead = (width // LANES + 1) * rows
    routes_1, gates_1, routes_2, gates_2 = (
        a.reshape(1, rows) for a in (routes_1, gates_1, routes_2, gates_2)
    )

    def to_expert(place):
        far = distance(place)
        return [(i, (i // group ^ far) * group + i % group) for i in range(devices)]

    def within(shift):
        return [(i, i // group * group + (i + shift) % group) for i in range(devices)]

    def onward(place):
        return [
            (s * devices + i, (s + 1) % sections * devices + j)
            for s in range(sections)
            for i, j in to_expert(place)
        ]

    def across(blocks):
        return [lax.ppermute(blocks[i], "expert", to_expert(i)) for i in range(EXPERTS - 1)]

    def shared(arrived):
        return arrived + [
            lax.ppermute(a, "expert", within(m)) for m in range(1, group) for a in arrived
        ]

    def experts(ins):
        count = sum(a.shape[0] for a in ins) // tall
        return call(
            functools.partial(expert_kernel, len(ins)),
            [jax.ShapeDtypeStruct((count // group * tall, wide), BF16)] * group,
            [*weights, *ins],
            24,
            [spread_scratch(pad_rows(count * CAP), width)],
            flops=6 * 256 * width * weights[0].shape[1],
        )

    def exchanged(sums):
        return [sums[0]] + [
            lax.ppermute(sums[m], "expert", within(-m)) for m in range(1, group)
        ]

    def added(terms):
        parts = terms[0].shape[0] // tall
        return call(
            functools.partial(sum_kernel, group), [block] * parts, terms, 8, flops=10**9
        )

    sources = [
        pltpu.with_memory_space_constraint(a, pltpu.HBM)
        for a in (tokens[0], gain, routes_1, gates_1)
    ]
    *blocks, travelling = call(
        functools.partial(pack_kernel, group),
        [block] * EXPERTS + [jax.ShapeDtypeStruct((ahead, LANES), BF16)],
        sources,
        8,
        [pltpu.VMEM(a.shape, a.dtype) for a in sources]
        + [packing, pltpu.SemaphoreType.DMA((len(sources),))],
        flops=10**10,
        space=HBM,
    )
    arrived = across(blocks[:-1])
    carry, second_map, second_gates = call(
        functools.partial(carry_kernel, group),
        [
            jax.ShapeDtypeStruct((ahead + tall, LANES), BF16),
            jax.ShapeDtypeStruct((rows, pad_rows(EXPERTS * CAP)), BF16),
            jax.ShapeDtypeStruct((rows, 128), F32),
        ],
        [routes_2, gates_2, travelling, *exchanged(experts(shared(blocks[-1:])))],
        8,
    )
    *ins, carry = lax.optimization_barrier((*shared(arrived), carry))
    *sums, carry = lax.optimization_barrier((*experts(ins), carry))
    terms = exchanged(sums)
    carried = lax.ppermute(carry, "section", [(i, (i + 1) % sections) for i in range(sections)])
    sums = added(terms)
    home = [lax.ppermute(sums[i], ("section", "expert"), onward(i)) for i in range(EXPERTS - 1)]
    first, *blocks = call(
        functools.partial(middle_kernel, group),
        [whole] + [block] * EXPERTS,
        [*home, carried, gain, second_map],
        8,
        [packing],
    )
    sums = added(exchanged(experts(shared(across(blocks[:-1]) + blocks[-1:]))))
    home = across(sums[:-1])
    (mixed,) = call(
        last_kernel,
        [whole],
        [first, *home, sums[-1], second_map, second_gates],
        8,
        [packing, pltpu.VMEM((rows, width), BF16), pltpu.SemaphoreType.DMA((PARTS,))],
        out_space=HBM,
    )
    return mixed[None]


def solution(mesh):
    rows = P("section", "expert", None)
    slabs = P("section", "expert", None, None)
    return jax.shard_map(
        on_device,
        mesh=mesh,
        in_specs=(rows, P("section", None), rows, rows, rows, rows, slabs, slabs, slabs),
        out_specs=rows,
        check_vma=False,
    )
```

```python
import functools

import jax
import jax.numpy as jnp
from jax import lax
from jax.experimental import pallas as pl
from jax.experimental.pallas import tpu as pltpu
from jax.sharding import PartitionSpec as P

EXPERTS = 4
CAP = 5
ROWS = 16
LANES = 256
PIECE = 256
PARTS = 4
EPS = 1e-06
F32 = jnp.float32
BF16 = jnp.bfloat16
VMEM = pl.BlockSpec(memory_space=pltpu.VMEM)
HBM = pl.BlockSpec(memory_space=pltpu.HBM)


def distance(place):
    return place ^ (2 + (place >> 1))


def fifth(value):
    return (value * 205) >> 10


def pad_rows(count):
    return -(-count // ROWS) * ROWS


def block_shape(width):
    return CAP * width // LANES, LANES


def spread_scratch(rows, width):
    return pltpu.VMEM((LANES // 128, (rows + 1) * width // LANES, 128), F32)


def spread(values, spread_ref, width, start=0):
    rows, columns = values.shape
    pieces = width // LANES
    for tile in range(columns // 128):
        piece, half = divmod(start // 128 + tile, LANES // 128)
        spread_ref[half, pl.ds(piece, rows, stride=pieces), :] = values[
            :, tile * 128 : (tile + 1) * 128
        ]


def gathered(spread_ref, rows, width, start=0, columns=None):
    pieces = width // LANES
    tiles = []
    for tile in range(start // 128, (start + (columns or width)) // 128):
        piece, half = divmod(tile, LANES // 128)
        tiles.append(spread_ref[half, pl.ds(piece, rows, stride=pieces), :].astype(BF16))
    return jnp.concatenate(tiles, axis=1)


def to_blocks(spread_ref, refs):
    start = 0
    for ref in refs:
        stop = start + ref.shape[0]
        for half in range(LANES // 128):
            ref[:, half * 128 : (half + 1) * 128] = spread_ref[half, start:stop, :].astype(BF16)
        start = stop


def from_blocks(arrays, spread_ref):
    start = 0
    for array in arrays:
        stop = start + array.shape[0]
        for half in range(LANES // 128):
            spread_ref[half, start:stop, :] = array[:, half * 128 : (half + 1) * 128].astype(F32)
        start = stop
    return start


def upright(row):
    rows = row.shape[1]
    same = lax.broadcasted_iota(jnp.int32, (rows, rows), 0) == lax.broadcasted_iota(
        jnp.int32, (rows, rows), 1
    )
    return jnp.sum(jnp.where(same, row, 0.0), axis=1, keepdims=True)


def slots_of(routes):
    rows = routes.shape[0]
    lanes = lax.broadcasted_iota(jnp.int32, (rows, 128), 1).astype(F32)
    one_hot = (routes == lanes).astype(F32)
    earlier = lax.broadcasted_iota(jnp.int32, (rows, rows), 0) > lax.broadcasted_iota(
        jnp.int32, (rows, rows), 1
    )
    before = jnp.dot(earlier.astype(BF16), one_hot.astype(BF16), preferred_element_type=F32)
    return routes * CAP + jnp.sum(before * one_hot, axis=1, keepdims=True)


def block_map(slots, expert):
    place = lax.broadcasted_iota(jnp.int32, (slots.shape[0], pad_rows(EXPERTS * CAP)), 1)
    block = fifth(place)
    target = (distance(block) ^ expert) * CAP + place - CAP * block
    target = jnp.where(block < EXPERTS, target, -1)
    return (slots == target.astype(F32)).astype(BF16)


def normalize(values, gain):
    inv_scale = lax.rsqrt(jnp.mean(values * values, axis=-1, keepdims=True) + EPS)
    return (values * inv_scale * gain).astype(BF16)


def write_blocks(normed, chosen, spread_ref, block_refs):
    packed = lax.dot_general(
        chosen, normed, (((0,), (0,)), ((), ())), preferred_element_type=F32
    )
    spread(packed, spread_ref, normed.shape[1])
    to_blocks(spread_ref, block_refs)


def hand_out(values, refs):
    start = 0
    for ref in refs:
        ref[...] = values[start : start + ref.shape[0]]
        start += ref.shape[0]


def my_expert(group):
    return lax.axis_index("expert") // group


def split_parts(values):
    parts = []
    for _ in range(3):
        parts.append(values.astype(BF16))
        values = values - parts[-1].astype(F32)
    return parts


def pack_kernel(group, *refs):
    sources, block_refs, ahead_ref = refs[:4], refs[4 : 4 + EXPERTS], refs[4 + EXPERTS]
    held, spread_ref, sems = refs[5 + EXPERTS : -2], refs[-2], refs[-1]
    copies = [
        pltpu.make_async_copy(source, place, sems.at[i])
        for i, (source, place) in enumerate(zip(sources, held))
    ]
    for copy in copies:
        copy.start()
    x_ref, gain_ref, routes_ref, gates_ref = held
    rows, width = x_ref.shape
    for copy in copies[2:]:
        copy.wait()
    slots = slots_of(upright(routes_ref[...].astype(F32)))
    lane = lax.broadcasted_iota(jnp.int32, (rows, LANES), 1)
    meta = jnp.zeros((rows, LANES), F32)
    for i, column in enumerate(split_parts(upright(gates_ref[...]))):
        meta = jnp.where(lane == 128 + i, column.astype(F32), meta)
    chosen = block_map(slots, my_expert(group))
    for copy in copies[:2]:
        copy.wait()
    for piece in range(width // LANES):
        ahead_ref[piece * rows : (piece + 1) * rows] = x_ref[:, piece * LANES : (piece + 1) * LANES]
    ahead_ref[width // LANES * rows :] = meta.astype(BF16)
    ahead_ref[width // LANES * rows :, : chosen.shape[1]] = chosen
    normed = normalize(x_ref[...].astype(F32), gain_ref[...])
    write_blocks(normed, chosen, spread_ref, block_refs)


def fill(blocks, spread_ref):
    filled = from_blocks(blocks, spread_ref)
    spread_ref[:, filled:, :] = jnp.zeros(
        (spread_ref.shape[0], spread_ref.shape[1] - filled, 128), F32
    )


def residual(x, gates, chosen, spread_ref, width, start=0):
    found = jnp.dot(
        chosen,
        gathered(spread_ref, chosen.shape[1], width, start, x.shape[1]),
        preferred_element_type=F32,
    )
    update = (gates * found).astype(BF16)
    return (x.astype(F32) + update.astype(F32)).astype(BF16)


def middle_kernel(*refs):
    block_ins, carried_ref, gain_ref, map_ref = refs[: EXPERTS - 1], *refs[EXPERTS - 1 : EXPERTS + 2]
    first_ref, block_refs, spread_ref = refs[EXPERTS + 2], refs[EXPERTS + 3 : -1], refs[-1]
    rows, width = first_ref.shape
    pieces = width // LANES
    x = jnp.concatenate(
        [carried_ref[piece * rows : (piece + 1) * rows] for piece in range(pieces)], axis=1
    )
    meta = carried_ref[pieces * rows : (pieces + 1) * rows].astype(F32)
    gates = meta[:, 128:129] + meta[:, 129:130] + meta[:, 130:131]
    chosen = meta[:, : pad_rows(EXPERTS * CAP)].astype(BF16)
    blocks = [ref[...] for ref in block_ins] + [carried_ref[(pieces + 1) * rows :]]
    fill(blocks, spread_ref)
    first = residual(x, gates, chosen, spread_ref, width)
    first_ref[...] = first
    normed = normalize(first.astype(F32), gain_ref[...])
    write_blocks(normed, map_ref[...], spread_ref, block_refs)


def last_kernel(x_ref, b0, b1, b2, b3, map_ref, gates_ref, out_ref, spread_ref, done_ref, sems):
    chosen = map_ref[...]
    gates = gates_ref[:, 0:1]
    fill([ref[...] for ref in (b0, b1, b2, b3)], spread_ref)
    width = x_ref.shape[1]
    copies = []
    for i in range(PARTS):
        span = slice(i * width // PARTS, (i + 1) * width // PARTS)
        done_ref[:, span] = residual(x_ref[:, span], gates, chosen, spread_ref, width, span.start)
        copies.append(
            pltpu.make_async_copy(done_ref.at[:, span], out_ref.at[:, span], sems.at[i])
        )
        copies[-1].start()
    for copy in copies:
        copy.wait()


def expert_kernel(given, w_gate, w_up, w_down, *refs):
    ins, outs, spread_ref = refs[:given], refs[given:-1], refs[-1]
    width = w_gate.shape[0]
    rows = spread_ref.shape[1] * LANES // width - 1
    from_blocks([ref[...] for ref in ins], spread_ref)
    x = gathered(spread_ref, rows, width)
    hidden = []
    for start in range(0, w_gate.shape[1], PIECE):
        gate_val = jnp.dot(x, w_gate[:, start : start + PIECE], preferred_element_type=F32)
        up_val = jnp.dot(x, w_up[:, start : start + PIECE], preferred_element_type=F32)
        hidden.append((gate_val / (1.0 + jnp.exp(-gate_val)) * up_val).astype(BF16))
    hidden = jnp.concatenate(hidden, axis=1)
    for start in range(0, width, PIECE):
        piece = jnp.dot(hidden, w_down[:, start : start + PIECE], preferred_element_type=F32)
        spread(piece, spread_ref, width, start)
    to_blocks(spread_ref, outs)


def summed(refs):
    total = refs[0][...].astype(F32)
    for ref in refs[1:]:
        total = total + ref[...].astype(F32)
    return total.astype(BF16)


def sum_kernel(given, *refs):
    hand_out(summed(refs[:given]), refs[given:])


def carry_kernel(group, routes_ref, gates_ref, ahead_ref, *refs):
    ins, (out_ref, map_ref, column_ref) = refs[:-3], refs[-3:]
    rows = ahead_ref.shape[0]
    out_ref[:rows] = ahead_ref[...]
    out_ref[rows:] = summed(ins)
    slots = slots_of(upright(routes_ref[...].astype(F32)))
    map_ref[...] = block_map(slots, my_expert(group))
    column_ref[...] = jnp.broadcast_to(upright(gates_ref[...]), column_ref.shape)


def call(body, outs, ins, megabytes, scratch=(), flops=0, space=VMEM, out_space=VMEM):
    moved = sum(a.size * a.dtype.itemsize for a in (*ins, *outs))
    return pl.pallas_call(
        body,
        out_shape=outs,
        in_specs=[space] * len(ins),
        out_specs=[out_space] * len(outs),
        scratch_shapes=list(scratch),
        compiler_params=pltpu.CompilerParams(vmem_limit_bytes=megabytes << 20),
        cost_estimate=pl.CostEstimate(flops=flops, bytes_accessed=moved, transcendentals=0),
    )(*ins)


def on_device(tokens, gain, routes_1, gates_1, routes_2, gates_2, gate_proj, up_proj, down_proj):
    sections, devices = lax.axis_size("section"), lax.axis_size("expert")
    group = devices // EXPERTS
    rows, width = tokens.shape[1:]
    weights = (gate_proj[0, 0], up_proj[0, 0], down_proj[0, 0])
    tall, wide = block_shape(width)
    block = jax.ShapeDtypeStruct((tall, wide), BF16)
    packing = spread_scratch(pad_rows(EXPERTS * CAP), width)
    whole = jax.ShapeDtypeStruct((rows, width), BF16)
    ahead = (width // LANES + 1) * rows
    routes_1, gates_1, routes_2, gates_2 = (
        a.reshape(1, rows) for a in (routes_1, gates_1, routes_2, gates_2)
    )

    def to_expert(place):
        far = distance(place)
        return [(i, (i // group ^ far) * group + i % group) for i in range(devices)]

    def within(shift):
        return [(i, i // group * group + (i + shift) % group) for i in range(devices)]

    def onward(place):
        return [
            (s * devices + i, (s + 1) % sections * devices + j)
            for s in range(sections)
            for i, j in to_expert(place)
        ]

    def across(blocks):
        return [lax.ppermute(blocks[i], "expert", to_expert(i)) for i in range(EXPERTS - 1)]

    def shared(arrived):
        return arrived + [
            lax.ppermute(a, "expert", within(m)) for m in range(1, group) for a in arrived
        ]

    def experts(ins):
        count = sum(a.shape[0] for a in ins) // tall
        return call(
            functools.partial(expert_kernel, len(ins)),
            [jax.ShapeDtypeStruct((count // group * tall, wide), BF16)] * group,
            [*weights, *ins],
            24,
            [spread_scratch(pad_rows(count * CAP), width)],
            flops=6 * 256 * width * weights[0].shape[1],
        )

    def exchanged(sums):
        return [sums[0]] + [
            lax.ppermute(sums[m], "expert", within(-m)) for m in range(1, group)
        ]

    def added(terms):
        parts = terms[0].shape[0] // tall
        return call(
            functools.partial(sum_kernel, group), [block] * parts, terms, 8, flops=10**9
        )

    sources = [
        pltpu.with_memory_space_constraint(a, pltpu.HBM)
        for a in (tokens[0], gain, routes_1, gates_1)
    ]
    *blocks, travelling = call(
        functools.partial(pack_kernel, group),
        [block] * EXPERTS + [jax.ShapeDtypeStruct((ahead, LANES), BF16)],
        sources,
        8,
        [pltpu.VMEM(a.shape, a.dtype) for a in sources]
        + [packing, pltpu.SemaphoreType.DMA((len(sources),))],
        flops=10**10,
        space=HBM,
    )
    arrived = across(blocks[:-1])
    carry, second_map, second_gates = call(
        functools.partial(carry_kernel, group),
        [
            jax.ShapeDtypeStruct((ahead + tall, LANES), BF16),
            jax.ShapeDtypeStruct((rows, pad_rows(EXPERTS * CAP)), BF16),
            jax.ShapeDtypeStruct((rows, 128), F32),
        ],
        [routes_2, gates_2, travelling, *exchanged(experts(shared(blocks[-1:])))],
        8,
    )
    *ins, carry = lax.optimization_barrier((*shared(arrived), carry))
    *sums, carry = lax.optimization_barrier((*experts(ins), carry))
    terms = exchanged(sums)
    carried = lax.ppermute(carry, "section", [(i, (i + 1) % sections) for i in range(sections)])
    sums = added(terms)
    home = [lax.ppermute(sums[i], ("section", "expert"), onward(i)) for i in range(EXPERTS - 1)]
    first, *blocks = call(
        middle_kernel,
        [whole] + [block] * EXPERTS,
        [*home, carried, gain, second_map],
        8,
        [packing],
    )
    sums = added(exchanged(experts(shared(across(blocks[:-1]) + blocks[-1:]))))
    home = across(sums[:-1])
    (mixed,) = call(
        last_kernel,
        [whole],
        [first, *home, sums[-1], second_map, second_gates],
        8,
        [packing, pltpu.VMEM((rows, width), BF16), pltpu.SemaphoreType.DMA((PARTS,))],
        out_space=HBM,
    )
    return mixed[None]


def solution(mesh):
    rows = P("section", "expert", None)
    slabs = P("section", "expert", None, None)
    return jax.shard_map(
        on_device,
        mesh=mesh,
        in_specs=(rows, P("section", None), rows, rows, rows, rows, slabs, slabs, slabs),
        out_specs=rows,
        check_vma=False,
    )
```
